256 devices in a mesh: gz: 8 (over z_lo, x), gy: 8 (over z_hi, core), gx: 4 (over y).
Axes of the slice: x: 4, y: 4, z: 8 (z_hi: 4, z_lo: 2; z = z_hi * 2 + z_lo), core: 2. Of those that a mesh axis runs over, the one named last changes fastest.
Arguments:
- volume: bfloat16 [16, 64, 128, 512], P(None, 'gz', 'gy', 'gx'), may hold values from -6 to 6
- surface_conv: bfloat16 [16, 16, 3, 3, 3], replicated, may hold values from -0.4375 to 0.4375
- surface_bias: float32 [16], replicated, may hold values from -3 to 3
- second_conv: bfloat16 [32, 16, 3, 3, 3], replicated, may hold values from -0.4375 to 0.4375
- second_bias: float32 [32], replicated, may hold values from -3 to 3
- middle_conv: bfloat16 [64, 32, 3, 3, 3], replicated, may hold values from -0.3125 to 0.3125
- middle_bias: float32 [64], replicated, may hold values from -3 to 3
- bottom_conv: bfloat16 [128, 64, 3, 3, 3], replicated, may hold values from -0.21875 to 0.21875
- bottom_bias: float32 [128], replicated, may hold values from -3 to 3
- middle_lift: bfloat16 [64, 128], replicated, may hold values from -0.75 to 0.75
- middle_return: bfloat16 [64, 128, 3, 3, 3], replicated, may hold values from -0.15625 to 0.15625
- middle_offset: float32 [64], replicated, may hold values from -3 to 3
- second_lift: bfloat16 [32, 64], replicated, may hold values from -1 to 1
- second_return: bfloat16 [32, 64, 3, 3, 3], replicated, may hold values from -0.21875 to 0.21875
- second_offset: float32 [32], replicated, may hold values from -3 to 3
- surface_lift: bfloat16 [16, 32], replicated, may hold values from -1.5 to 1.5
- surface_return: bfloat16 [16, 32, 3, 3, 3], replicated, may hold values from -0.3125 to 0.3125
- surface_offset: float32 [16], replicated, may hold values from -3 to 3
Outputs:
- decoded: bfloat16 [16, 64, 128, 512], P(None, 'gz', 'gy', 'gx')
The draws below stay inside these ranges and needn't reach their ends.
All inputs are finite; a program needn't handle non-finite values.
Results may differ from the reference program's by a relative error of at most 0.024.
Values may be sent and summed in bfloat16 or wider, within the bound.
A program may use at most 128 MiB of HBM per device.

```python
import jax
import jax.numpy as jnp
from jax import lax

C0 = 16
C1 = 32
C2 = 64
C3 = 128
DEPTH = 64
HEIGHT = 128
WIDTH = 512


def levels(own_key, shape, pieces, smallest, top_value):
    loudness, own = 1.0, jax.random.fold_in(own_key, 6)
    for dim, parts in pieces:
        heights = jnp.exp(jax.random.uniform(jax.random.fold_in(own, dim), (parts,), jnp.float32, smallest / len(pieces), top_value / len(pieces)))
        loudness = loudness * jnp.repeat(heights, shape[dim] // parts).reshape([-1 if axis == dim else 1 for axis in range(len(shape))])
    return loudness


def gaussian(stream_key, dims, deviation, most, split=(), dtype=jnp.bfloat16):
    loudness = levels(stream_key, dims, split, -0.22, 0.18) if split else 1.0
    values = jax.random.normal(stream_key, dims, jnp.float32) * deviation * loudness
    return jnp.minimum(jnp.maximum(values, -most), most).astype(dtype)


def setup_inputs(seed: int = 0) -> dict:
    splits = jax.random.split(jax.random.key(seed), 19)
    return {
        "volume": gaussian(splits[0], (C0, DEPTH, HEIGHT, WIDTH), 1.0, 6.0, ((1, 8), (2, 8), (3, 4))),
        "surface_conv": gaussian(splits[1], (C0, C0, 3, 3, 3), (27 * C0 // 2) ** -0.5, 0.4375),
        "surface_bias": gaussian(splits[2], (C0,), 0.5, 3.0, (), jnp.float32),
        "second_conv": gaussian(splits[3], (C1, C0, 3, 3, 3), (27 * C0 // 2) ** -0.5, 0.4375),
        "second_bias": gaussian(splits[4], (C1,), 0.5, 3.0, (), jnp.float32),
        "middle_conv": gaussian(splits[5], (C2, C1, 3, 3, 3), (27 * C1 // 2) ** -0.5, 0.3125),
        "middle_bias": gaussian(splits[6], (C2,), 0.5, 3.0, (), jnp.float32),
        "bottom_conv": gaussian(splits[7], (C3, C2, 3, 3, 3), (27 * C2 // 2) ** -0.5, 0.21875),
        "bottom_bias": gaussian(splits[8], (C3,), 0.5, 3.0, (), jnp.float32),
        "middle_lift": gaussian(splits[9], (C2, C3), (C3 // 2) ** -0.5, 0.75),
        "middle_return": gaussian(splits[10], (C2, 2 * C2, 3, 3, 3), (27 * C2) ** -0.5, 0.15625),
        "middle_offset": gaussian(splits[11], (C2,), 0.5, 3.0, (), jnp.float32),
        "second_lift": gaussian(splits[12], (C1, C2), (C2 // 2) ** -0.5, 1.0),
        "second_return": gaussian(splits[13], (C1, 2 * C1, 3, 3, 3), (27 * C1) ** -0.5, 0.21875),
        "second_offset": gaussian(splits[14], (C1,), 0.5, 3.0, (), jnp.float32),
        "surface_lift": gaussian(splits[15], (C0, C1), (C1 // 2) ** -0.5, 1.5),
        "surface_return": gaussian(splits[16], (C0, 2 * C0, 3, 3, 3), (27 * C0) ** -0.5, 0.3125),
        "surface_offset": gaussian(splits[17], (C0,), 0.5, 3.0, (), jnp.float32),
    }


def convolve(values, kernel, offset):
    out = lax.conv_general_dilated(values.astype(jnp.float32)[None], kernel.astype(jnp.float32), (1, 1, 1), "SAME", dimension_numbers=("NCDHW", "OIDHW", "NCDHW"), precision=lax.Precision.HIGHEST)[0]
    out = out + offset[:, None, None, None]
    return jnp.maximum(out, 0.1 * out).astype(jnp.bfloat16)


def pooled(values):
    chans, depth, height, width = values.shape
    return values.reshape(chans, depth // 2, 2, height // 2, 2, width // 2, 2).max(axis=(2, 4, 6))


def upsampled(values):
    return jnp.repeat(jnp.repeat(jnp.repeat(values, 2, axis=1), 2, axis=2), 2, axis=3)


def lifted(matrix, values):
    return jnp.einsum("oi,idhw->odhw", matrix.astype(jnp.float32), values.astype(jnp.float32), precision=lax.Precision.HIGHEST).astype(jnp.bfloat16)


def reference(volume, surface_conv, surface_bias, second_conv, second_bias, middle_conv, middle_bias, bottom_conv, bottom_bias, middle_lift, middle_return, middle_offset, second_lift, second_return, second_offset, surface_lift, surface_return, surface_offset):
    skip_zero = convolve(volume, surface_conv, surface_bias)
    skip_one = convolve(pooled(skip_zero), second_conv, second_bias)
    skip_two = convolve(pooled(skip_one), middle_conv, middle_bias)
    bottom = convolve(pooled(skip_two), bottom_conv, bottom_bias)
    lift_two = lifted(middle_lift, bottom)
    upper_two = convolve(jnp.concatenate([skip_two, upsampled(lift_two)], axis=0), middle_return, middle_offset)
    lift_one = lifted(second_lift, upper_two)
    upper_one = convolve(jnp.concatenate([skip_one, upsampled(lift_one)], axis=0), second_return, second_offset)
    lift_zero = lifted(surface_lift, upper_one)
    return convolve(jnp.concatenate([skip_zero, upsampled(lift_zero)], axis=0), surface_return, surface_offset)
```

```python
import itertools

import jax
import jax.numpy as jnp
from jax import lax
from jax.experimental import pallas as pl
from jax.experimental.pallas import tpu as pltpu
from jax.sharding import PartitionSpec as P

BF16 = jnp.bfloat16
F32 = jnp.float32
STEPS = (-1, 0, 1)
PLANE = [(dz, dy) for dz in STEPS for dy in STEPS]
RING = [step for step in PLANE if step != (0, 0)]
FAR = [(dz, dy) for dz in (-2, -1, 0, 1, 2) for dy in STEPS]


def span(step, size, halo):
    if step == 0:
        return halo, halo, size
    if step > 0:
        return size, 0, halo
    return halo, halo + size, halo


def region(step, size, halo):
    if step == 0:
        return halo, size, 0
    if step < 0:
        return 0, halo, size - halo
    return halo + size, halo, 0


def leaky(total):
    return jnp.maximum(total, 0.1 * total)


def kernel(
    x_ref,
    k0, b0, k1, b1, k2, b2, k3, b3,
    lift2, ku2, c2, lift1, ku1, c1, lift0, kd0, c0,
    out_ref,
    xf, vol, edge0, mine0, stack0,
    zero, edgez, minez,
    pool0, edge1, mine1,
    join1, pool1, join2, pool2, edge2, mine2, join0,
    wa0, wd0, w1, w2, w3, wu2, wu1, wl0,
    pick, grow,
    bias0, bias1, bias2, bias3, off2, off1, off0,
    send_sem, recv_sem,
):
    z, y, x = lax.axis_index("gz"), lax.axis_index("gy"), lax.axis_index("gx")
    nz, ny, nx = lax.axis_size("gz"), lax.axis_size("gy"), lax.axis_size("gx")

    def device(dz, dy, dx):
        return (lax.rem(z + dz + nz, nz), lax.rem(y + dy + ny, ny), lax.rem(x + dx + nx, nx))

    others = [(dz, dy, dx) for dz, dy in FAR for dx in STEPS if (dz, dy, dx) != (0, 0, 0)]
    barrier = pltpu.get_barrier_semaphore()
    for step in others:
        pl.semaphore_signal(
            barrier, inc=1, device_id=device(*step), device_id_type=pl.DeviceIdType.MESH
        )

    count = itertools.count()

    def send(src, dst, step):
        k = next(count)
        copy = pltpu.make_async_remote_copy(
            src_ref=src,
            dst_ref=dst,
            send_sem=send_sem.at[k],
            recv_sem=recv_sem.at[k],
            device_id=device(*step),
            device_id_type=pl.DeviceIdType.MESH,
        )
        copy.start()
        return copy

    def send_rows(buffer, sizes, halo):
        copies = []
        for dz, dy in RING:
            s0, t0, n0 = span(dz, sizes[0], halo)
            s1, t1, n1 = span(dy, sizes[1], halo)
            copies.append(
                send(
                    buffer.at[pl.ds(s0, n0), pl.ds(s1, n1)],
                    buffer.at[pl.ds(t0, n0), pl.ds(t1, n1)],
                    (dz, dy, 0),
                )
            )
        return copies

    def send_edges(mine, edge, steps, reach):
        copies = []
        for dz, dy in steps:
            for dx in (-1, 1):
                side = 0 if dx > 0 else 1
                copies.append(
                    send(mine.at[1 - side], edge.at[side, reach - dz, 1 - dy], (dz, dy, dx))
                )
        return copies

    def wait_recv(copies):
        for copy in copies:
            copy.wait_recv()

    def wait_send(copies):
        for copy in copies:
            copy.wait_send()

    lane = lax.broadcasted_iota(jnp.int32, (1, 128), 1)
    inside_left = (x > 0).astype(jnp.int32)
    inside_right = (x < nx - 1).astype(jnp.int32)

    def within(dz, dy):
        pz, py = z + dz, y + dy
        ok = (pz >= 0) & (pz < nz) & (py >= 0) & (py < ny)
        return ok.astype(jnp.int32)

    for c in range(16):
        xf[pl.ds(c * 128, 128), :] = x_ref[c].reshape(128, 128).astype(F32)

    def to_row(r, _):
        vol[1 + lax.div(r, 16), 1 + lax.rem(r, 16)] = xf[pl.ds(r, 16, stride=128), :].astype(BF16)
        return 0

    lax.fori_loop(0, 128, to_row, 0, unroll=8)
    row_id = lax.broadcasted_iota(jnp.int32, (32, 2048), 0)
    col_id = lax.broadcasted_iota(jnp.int32, (32, 2048), 1)
    wanted = lax.rem(row_id, 16) * 128 + jnp.where(row_id < 16, 0, 127)
    chooser = (col_id == wanted).astype(F32).astype(BF16)
    flat = jnp.concatenate([x_ref[c].reshape(128, 128) for c in range(16)], axis=1)
    ends = lax.dot_general(
        chooser, flat, (((1,), (1,)), ((), ())), preferred_element_type=F32
    ).astype(BF16)
    mine0[0] = ends[:16]
    mine0[1] = ends[16:]

    pl.semaphore_wait(barrier, len(others))
    sent = []
    rows_in = send_rows(vol, (8, 16), 1)
    edges_in = send_edges(mine0, edge0, PLANE, 1)
    sent += rows_in + edges_in

    def column(ref, size):
        a = lax.broadcasted_iota(jnp.int32, (size, size), 0)
        b = lax.broadcasted_iota(jnp.int32, (size, size), 1)
        spread = jnp.broadcast_to(ref[...], (size, size))
        return jnp.sum(jnp.where(a == b, spread, 0.0), axis=1, keepdims=True)

    for ref, target, size, times in (
        (b0, bias0, 16, 4),
        (b1, bias1, 32, 2),
        (b2, bias2, 64, 1),
        (b3, bias3, 128, 1),
        (c2, off2, 64, 1),
        (c1, off1, 32, 2),
        (c0, off0, 16, 4),
    ):
        wide = jnp.broadcast_to(column(ref, size), (size, 128))
        for j in range(times):
            target[pl.ds(j * size, size), :] = wide

    for ref in (wa0, wd0, w1, wu1, wl0):
        ref[...] = jnp.zeros(ref.shape, BF16)
    for a, e, f in itertools.product(range(3), repeat=3):
        tap = (a * 3 + e) * 3 + f
        first, last = k0[tap], kd0[tap]
        for j in range(4):
            at = (a * 6 + e + j) * 48 + f * 16
            wa0[j * 16 : j * 16 + 16, at : at + 16] = first
            at = (a * 6 + e + j) * 96 + f * 16
            wd0[j * 16 : j * 16 + 16, at : at + 16] = last[:, :16]
            wd0[j * 16 : j * 16 + 16, at + 48 : at + 64] = last[:, 16:]
        for j in range(2):
            at = (a * 4 + e + j) * 16
            row = (f * 2 + j) * 32
            w1[row : row + 32, at : at + 16] = k1[tap]
            at = (a * 4 + e + j) * 64
            wu1[row : row + 32, at : at + 64] = ku1[tap]
        at = a * 3 + e
        w2[f * 64 : f * 64 + 64, at * 32 : at * 32 + 32] = k2[tap]
        w3[f * 128 : f * 128 + 128, at * 64 : at * 64 + 64] = k3[tap]
        wu2[f * 64 : f * 64 + 64, at * 128 : at * 128 + 128] = ku2[tap]
    for j in range(2):
        wl0[j * 16 : j * 16 + 16, j * 32 : j * 32 + 32] = lift0[...]

    a = lax.broadcasted_iota(jnp.int32, (128, 256), 0)
    b = lax.broadcasted_iota(jnp.int32, (128, 256), 1)
    cell = lax.rem(b, 128) - 32
    hit = (cell >= 0) & (cell < 64) & (a == 2 * cell + lax.div(b, 128))
    pick[...] = hit.astype(F32).astype(BF16)
    a = lax.broadcasted_iota(jnp.int32, (128, 384), 0)
    b = lax.broadcasted_iota(jnp.int32, (128, 384), 1)
    hit = a == lax.div(lax.rem(b, 128) + lax.div(b, 128) + 1, 2) + 31
    grow[...] = hit.astype(F32).astype(BF16)

    def shifted(src, edge, target, base):
        for dz, dy in PLANE:
            p0, n0, s0 = region(dz, 8, 1)
            p1, n1, s1 = region(dy, 16, 1)
            ok = within(dz, dy)
            ok_left = (ok * inside_left).astype(F32)
            ok_right = (ok * inside_right).astype(F32)
            ok = ok.astype(F32)
            left_edge = edge[0, dz + 1, dy + 1].astype(F32) * ok_left
            right_edge = edge[1, dz + 1, dy + 1].astype(F32) * ok_right

            def body(i, _):
                i0, i1 = lax.div(i, n1), lax.rem(i, n1)
                r = (s0 + i0) * 16 + s1 + i1
                row = src[p0 + i0, p1 + i1].astype(F32)
                if (dz, dy) != (0, 0):
                    row = row * ok
                left = pltpu.roll(left_edge, lax.rem(128 - r, 128), 1)
                right = pltpu.roll(right_edge, 127 - r, 1)
                d, h = base + p0 + i0, base + p1 + i1
                target[d, h, 0:16, :] = jnp.where(lane == 0, left, pltpu.roll(row, 1, 1)).astype(BF16)
                target[d, h, 16:32, :] = row.astype(BF16)
                target[d, h, 32:48, :] = jnp.where(
                    lane == 127, right, pltpu.roll(row, 127, 1)
                ).astype(BF16)
                return 0

            lax.fori_loop(0, n0 * n1, body, 0, unroll=min(4, n0 * n1))

    wait_recv(rows_in + edges_in)
    shifted(vol, edge0, stack0, 0)

    def encode(i, _):
        d, h = lax.div(i, 4) * 2, lax.rem(i, 4) * 4
        cells = [stack0[pl.ds(d + j, 3), pl.ds(h, 6)].reshape(864, 128) for j in range(2)]
        total = jnp.dot(wa0[...], jnp.concatenate(cells, axis=1), preferred_element_type=F32)
        halves = [
            leaky(total[:, j * 128 : j * 128 + 128] + bias0[...]).astype(BF16) for j in range(2)
        ]
        for j in range(2):
            zero[1 + d + j, pl.ds(1 + h, 4)] = halves[j].reshape(4, 16, 128)
        top = jnp.maximum(halves[0], halves[1]).reshape(2, 2, 16, 128)
        top = jnp.maximum(top[:, 0], top[:, 1]).reshape(32, 128)
        both = jnp.dot(top, pick[...], preferred_element_type=F32)
        best = jnp.maximum(both[:, :128], both[:, 128:]).astype(BF16)
        pool0[3 + lax.div(d, 2), pl.ds(3 + lax.div(h, 2), 2)] = best.reshape(2, 16, 128)
        return 0

    lax.fori_loop(0, 16, encode, 0, unroll=2)

    def pack1(r, carry):
        first, last = carry
        row = pool0[3 + lax.div(r, 8), 3 + lax.rem(r, 8)].astype(F32)
        mine = lax.div(lane, 4) == r
        first = jnp.where(mine, pltpu.roll(row, lax.rem(4 * r + 96, 128), 1), first)
        last = jnp.where(mine, pltpu.roll(row, lax.rem(4 * r + 35, 128), 1), last)
        return first, last

    blank = jnp.zeros((16, 128), F32)
    first, last = lax.fori_loop(0, 32, pack1, (blank, blank), unroll=4)
    mine1[0] = first.astype(BF16)
    mine1[1] = last.astype(BF16)
    rows1 = send_rows(pool0, (4, 8), 3)
    edges1 = send_edges(mine1, edge1, PLANE, 1)
    sent += edges1

    def packz(r, carry):
        first, last = carry
        row = zero[1 + lax.div(r, 16), 1 + lax.rem(r, 16)].astype(F32)
        first = jnp.where(lane == r, pltpu.roll(row, r, 1), first)
        last = jnp.where(lane == r, pltpu.roll(row, lax.rem(r + 1, 128), 1), last)
        return first, last

    first, last = lax.fori_loop(0, 128, packz, (blank, blank), unroll=4)
    minez[0] = first.astype(BF16)
    minez[1] = last.astype(BF16)
    rowsz = send_rows(zero, (8, 16), 1)
    edgesz = send_edges(minez, edgez, PLANE, 1)
    sent += rowsz + edgesz

    wait_recv(rows1 + edges1)
    wait_send(rows1)
    for dz, dy in PLANE:
        p0, n0, s0 = region(dz, 4, 3)
        p1, n1, s1 = region(dy, 8, 3)
        ok = within(dz, dy)
        left_edge = edge1[0, dz + 1, dy + 1].astype(F32) * (ok * inside_left).astype(F32)
        right_edge = edge1[1, dz + 1, dy + 1].astype(F32) * (ok * inside_right).astype(F32)
        keep = ok.astype(F32)

        def join_rows(i, _):
            i0, i1 = lax.div(i, n1), lax.rem(i, n1)
            r = (s0 + i0) * 8 + s1 + i1
            row = pool0[p0 + i0, p1 + i1].astype(F32) * keep
            left = pltpu.roll(left_edge, lax.rem(157 - 4 * r, 128), 1)
            right = pltpu.roll(right_edge, lax.rem(224 - 4 * r, 128), 1)
            row = jnp.where((lane >= 29) & (lane < 32), left, row)
            row = jnp.where((lane >= 96) & (lane < 99), right, row)
            pool0[p0 + i0, p1 + i1] = row.astype(BF16)
            return 0

        lax.fori_loop(0, n0 * n1, join_rows, 0, unroll=3 if n0 * n1 == 9 else 4)

    lanes_ok = ((lane >= 32) | (x > 0)) & ((lane < 96) | (x < nx - 1))
    lanes_ok = lanes_ok.astype(jnp.int32)

    def keeps(d, h, depth, height):
        gd, gh = z * depth + d, y * height + h
        ok = (gd >= 0) & (gd < nz * depth) & (gh >= 0) & (gh < ny * height)
        return (lanes_ok * ok.astype(jnp.int32)) > 0

    def combine(total, rows, shift, part):
        cut = slice(part * 128, part * 128 + 128)
        return (
            pltpu.roll(total[:rows, cut], shift, 1)
            + total[rows : 2 * rows, cut]
            + pltpu.roll(total[2 * rows :, cut], 128 - shift, 1)
        )

    def pairs(row, width):
        even = lax.rem(lax.div(lane, width), 2) == 0
        other = jnp.where(even, pltpu.roll(row, 128 - width, 1), pltpu.roll(row, width, 1))
        return jnp.maximum(row, other)

    def second(i, _):
        d, h = lax.div(i, 6) * 2, lax.rem(i, 6) * 2
        cells = [pool0[pl.ds(d + j, 3), pl.ds(h, 4)].reshape(192, 128) for j in range(2)]
        total = jnp.dot(w1[...], jnp.concatenate(cells, axis=1), preferred_element_type=F32)
        best = None
        for j in range(2):
            value = leaky(combine(total, 64, 1, j) + bias1[...])
            for g in range(2):
                row = jnp.where(keeps(d + j - 2, h + g - 2, 4, 8), value[g * 32 : g * 32 + 32], 0.0)
                join1[d + j, h + g, 0:32, :] = row.astype(BF16)
                best = row if best is None else jnp.maximum(best, row)
        pool1[lax.div(d, 2), lax.div(h, 2)] = pairs(best, 1).astype(BF16)
        return 0

    lax.fori_loop(0, 24, second, 0, unroll=2)

    own = (lane >= 32) & (lane < 96)

    def third(h, _):
        cells = [pool1[pl.ds(j, 3), pl.ds(h, 3)].reshape(288, 128) for j in range(2)]
        total = jnp.dot(w2[...], jnp.concatenate(cells, axis=1), preferred_element_type=F32)
        for j in range(2):
            value = leaky(combine(total, 64, 2, j) + bias2[...])
            join2[2 + j, 2 + h, 0:64, :] = jnp.where(own, value, 0.0).astype(BF16)
        return 0

    lax.fori_loop(0, 4, third, 0, unroll=2)
    first = jnp.zeros((64, 128), F32)
    last = jnp.zeros((64, 128), F32)
    for h in range(2):
        best = None
        for j, g in itertools.product(range(2), repeat=2):
            row = join2[2 + j, 2 + 2 * h + g, 0:64, :].astype(F32)
            best = row if best is None else jnp.maximum(best, row)
            r = j * 4 + 2 * h + g
            here = lax.div(lane, 4) == r
            first = jnp.where(here, pltpu.roll(row, (4 * r + 96) % 128, 1), first)
            last = jnp.where(here, pltpu.roll(row, (4 * r + 36) % 128, 1), last)
        best = pairs(best, 2)
        pool2[2, 2 + h] = best.astype(BF16)
        here = lax.div(lane, 8) == 4 + h
        first = jnp.where(here, pltpu.roll(best, 8 * h, 1), first)
        last = jnp.where(here, pltpu.roll(best, 8 * h + 72, 1), last)
    mine2[0] = first.astype(BF16)
    mine2[1] = last.astype(BF16)
    edges2 = send_edges(mine2, edge2, FAR, 2)
    pools2 = [
        send(
            pool2.at[pl.ds(2, 1), pl.ds(2, 2)],
            pool2.at[pl.ds(2 - dz, 1), pl.ds(2 - 2 * dy, 2)],
            (dz, dy, 0),
        )
        for dz, dy in FAR
        if (dz, dy) != (0, 0)
    ]
    rows2 = []
    for dz, dy in RING:
        s0, t0, n0 = span(dz, 2, 2)
        s1, t1, n1 = span(dy, 4, 2)
        rows2.append(
            send(
                join2.at[pl.ds(s0, n0), pl.ds(s1, n1), pl.ds(0, 64)],
                join2.at[pl.ds(t0, n0), pl.ds(t1, n1), pl.ds(0, 64)],
                (dz, dy, 0),
            )
        )
    sent += edges2

    wait_recv(rowsz + edgesz)
    shifted(zero, edgez, join0, 1)

    wait_recv(edges2 + pools2)
    wait_send(pools2)
    for dz, dy in FAR:
        ok = within(dz, dy)
        left_edge = edge2[0, dz + 2, dy + 1].astype(F32) * (ok * inside_left).astype(F32)
        right_edge = edge2[1, dz + 2, dy + 1].astype(F32) * (ok * inside_right).astype(F32)
        keep = ok.astype(F32)
        for r in range(2):
            row = pool2[2 + dz, 2 + 2 * dy + r].astype(F32) * keep
            left = pltpu.roll(left_edge, (24 - 32 - 8 * r) % 128, 1)
            right = pltpu.roll(right_edge, (96 - 32 - 8 * r) % 128, 1)
            row = jnp.where((lane >= 24) & (lane < 32), left, row)
            row = jnp.where((lane >= 96) & (lane < 104), right, row)
            pool2[2 + dz, 2 + 2 * dy + r] = row.astype(BF16)

    def coarsest(i, _):
        d, h = lax.div(i, 2), lax.rem(i, 2) * 2
        cells = [pool2[pl.ds(d, 3), pl.ds(h + j, 3)].reshape(576, 128) for j in range(2)]
        total = jnp.dot(w3[...], jnp.concatenate(cells, axis=1), preferred_element_type=F32)
        low = []
        for j in range(2):
            value = leaky(combine(total, 128, 4, j) + bias3[...])
            low.append(jnp.where(keeps(d - 1, h + j - 1, 1, 2), value, 0.0).astype(BF16))
        up = jnp.dot(lift2[...], jnp.concatenate(low, axis=1), preferred_element_type=F32).astype(BF16)
        for j in range(2):
            for p, q in itertools.product(range(2), repeat=2):
                join2[2 * d + p, 2 * (h + j) + q, 64:128, :] = up[:, j * 128 : j * 128 + 128]
        return 0

    lax.fori_loop(0, 6, coarsest, 0)

    wait_recv(rows2)
    wait_send(rows2)
    for dz, dy in PLANE:
        p0, n0, s0 = region(dz, 2, 2)
        p1, n1, s1 = region(dy, 4, 2)
        ok = within(dz, dy)
        left_edge = edge2[0, dz + 2, dy + 1].astype(F32) * (ok * inside_left).astype(F32)
        right_edge = edge2[1, dz + 2, dy + 1].astype(F32) * (ok * inside_right).astype(F32)
        keep = ok.astype(F32)
        for i0, i1 in itertools.product(range(n0), range(n1)):
            r = (s0 + i0) * 4 + s1 + i1
            row = join2[p0 + i0, p1 + i1, 0:64, :].astype(F32) * keep
            left = pltpu.roll(left_edge, (28 - 4 * r) % 128, 1)
            right = pltpu.roll(right_edge, (96 - 4 * r) % 128, 1)
            row = jnp.where((lane >= 28) & (lane < 32), left, row)
            row = jnp.where((lane >= 96) & (lane < 100), right, row)
            join2[p0 + i0, p1 + i1, 0:64, :] = row.astype(BF16)

    def upper_two(i, _):
        d, h = lax.div(i, 6) * 2, lax.rem(i, 6)
        cells = [join2[pl.ds(d + j, 3), pl.ds(h, 3)].reshape(1152, 128) for j in range(2)]
        total = jnp.dot(wu2[...], jnp.concatenate(cells, axis=1), preferred_element_type=F32)
        low = []
        for j in range(2):
            value = leaky(combine(total, 64, 2, j) + off2[...])
            low.append(jnp.where(keeps(d + j - 1, h - 1, 2, 4), value, 0.0).astype(BF16))
        up = jnp.dot(lift1[...], jnp.concatenate(low, axis=1), preferred_element_type=F32).astype(BF16)
        for j in range(2):
            for p, q in itertools.product(range(2), repeat=2):
                join1[2 * (d + j) + p, 2 * h + q, 32:64, :] = up[:, j * 128 : j * 128 + 128]
        return 0

    lax.fori_loop(0, 12, upper_two, 0)

    def upper_one(i, _):
        d, h = lax.div(i, 5) * 2, lax.rem(i, 5) * 2
        cells = [join1[pl.ds(d + j, 3), pl.ds(h, 4)].reshape(768, 128) for j in range(2)]
        total = jnp.dot(wu1[...], jnp.concatenate(cells, axis=1), preferred_element_type=F32)
        low = []
        for j in range(2):
            value = leaky(combine(total, 64, 1, j) + off1[...])
            kept = [
                jnp.where(keeps(d + j - 1, h + g - 1, 4, 8), value[g * 32 : g * 32 + 32], 0.0)
                for g in range(2)
            ]
            low.append(jnp.concatenate(kept, axis=0).astype(BF16))
        up = jnp.dot(wl0[...], jnp.concatenate(low, axis=1), preferred_element_type=F32).astype(BF16)
        up = jnp.concatenate([up[:, :128], up[:, 128:]], axis=0)
        wide = jnp.dot(up, grow[...], preferred_element_type=F32).astype(BF16)
        for j, g in itertools.product(range(2), repeat=2):
            at = (j * 2 + g) * 16
            three = [wide[at : at + 16, f * 128 : f * 128 + 128] for f in range(3)]
            three = jnp.concatenate(three, axis=0)
            for p, q in itertools.product(range(2), repeat=2):
                join0[2 * (d + j) + p, 2 * (h + g) + q, 48:96, :] = three
        return 0

    lax.fori_loop(0, 15, upper_one, 0)

    def decode(i, _):
        d, h = lax.div(i, 4) * 2, lax.rem(i, 4) * 4
        cells = [join0[pl.ds(d + 1 + j, 3), pl.ds(h + 1, 6)].reshape(1728, 128) for j in range(2)]
        total = jnp.dot(wd0[...], jnp.concatenate(cells, axis=1), preferred_element_type=F32)
        for j in range(2):
            value = leaky(total[:, j * 128 : j * 128 + 128] + off0[...])
            for g in range(4):
                xf[pl.ds((d + j) * 16 + h + g, 16, stride=128), :] = value[g * 16 : g * 16 + 16]
        return 0

    lax.fori_loop(0, 16, decode, 0)
    for c in range(16):
        out_ref[c] = xf[pl.ds(c * 128, 128), :].astype(BF16).reshape(8, 16, 128)

    wait_send(sent)


def taps(weights):
    out, inner = weights.shape[:2]
    return jnp.transpose(weights, (2, 3, 4, 0, 1)).reshape(27, out, inner)


def per_device(
    volume,
    surface_conv,
    surface_bias,
    second_conv,
    second_bias,
    middle_conv,
    middle_bias,
    bottom_conv,
    bottom_bias,
    middle_lift,
    middle_return,
    middle_offset,
    second_lift,
    second_return,
    second_offset,
    surface_lift,
    surface_return,
    surface_offset,
):
    def tile(*shape):
        return pltpu.VMEM(shape, BF16)

    def wide(rows):
        return pltpu.VMEM((rows, 128), F32)

    scratch = [
        wide(2048), tile(10, 18, 16, 128), tile(2, 3, 3, 16, 128), tile(2, 16, 128), tile(10, 18, 48, 128),
        tile(10, 18, 16, 128), tile(2, 3, 3, 16, 128), tile(2, 16, 128),
        tile(10, 14, 16, 128), tile(2, 3, 3, 16, 128), tile(2, 16, 128),
        tile(8, 12, 64, 128), tile(4, 6, 32, 128), tile(6, 8, 128, 128),
        tile(5, 6, 64, 128), tile(2, 5, 3, 64, 128), tile(2, 64, 128), tile(12, 20, 96, 128),
        tile(64, 864), tile(64, 1728), tile(192, 192), tile(192, 288), tile(384, 576),
        tile(192, 1152), tile(192, 768), tile(32, 64),
        tile(128, 256), tile(128, 384),
        wide(64), wide(64), wide(64), wide(128), wide(64), wide(64), wide(64),
        pltpu.SemaphoreType.DMA((130,)), pltpu.SemaphoreType.DMA((130,)),
    ]

    def line(values):
        return values.reshape(1, values.shape[0])

    operands = (
        volume,
        taps(surface_conv), line(surface_bias),
        taps(second_conv), line(second_bias),
        taps(middle_conv), line(middle_bias),
        taps(bottom_conv), line(bottom_bias),
        middle_lift, taps(middle_return), line(middle_offset),
        second_lift, taps(second_return), line(second_offset),
        surface_lift, taps(surface_return), line(surface_offset),
    )
    return pl.pallas_call(
        kernel,
        out_shape=jax.ShapeDtypeStruct(volume.shape, BF16),
        in_specs=[pl.BlockSpec(memory_space=pltpu.VMEM)] * len(operands),
        out_specs=pl.BlockSpec(memory_space=pltpu.VMEM),
        scratch_shapes=scratch,
        compiler_params=pltpu.CompilerParams(
            collective_id=0, has_side_effects=True, vmem_limit_bytes=48 * 2**20
        ),
    )(*operands)


def solution(mesh):
    placed = (P(None, "gz", "gy", "gx"),) + (P(),) * 17
    return jax.shard_map(
        per_device, mesh=mesh, in_specs=placed, out_specs=P(None, "gz", "gy", "gx"), check_vma=False
    )
```

```python
import itertools

import jax
import jax.numpy as jnp
from jax import lax
from jax.experimental import pallas as pl
from jax.experimental.pallas import tpu as pltpu
from jax.sharding import PartitionSpec as P

BF16 = jnp.bfloat16
F32 = jnp.float32
STEPS = (-1, 0, 1)
PLANE = [(dz, dy) for dz in STEPS for dy in STEPS]
RING = [step for step in PLANE if step != (0, 0)]
FAR = [(dz, dy) for dz in (-2, -1, 0, 1, 2) for dy in STEPS]


def span(step, size, halo):
    if step == 0:
        return halo, halo, size
    if step > 0:
        return size, 0, halo
    return halo, halo + size, halo


def region(step, size, halo):
    if step == 0:
        return halo, size, 0
    if step < 0:
        return 0, halo, size - halo
    return halo + size, halo, 0


def leaky(total):
    return jnp.maximum(total, 0.1 * total)


def kernel(*refs):
    sources, refs = refs[:18], refs[18:]
    out_ref, refs = refs[0], refs[1:]
    locals_, refs = refs[:18], refs[18:]
    body(sources, locals_, out_ref, *refs)


def body(
    sources,
    locals_,
    out_ref,
    xf, vol, edge0, mine0, stack0,
    zero, edgez, minez,
    pool0, pair0, edge1, mine1,
    join1, pool1, join2, pool2, wide2, edge2, mine2, folded2, folded3, join0,
    wa0, wd0, w1, w2, w3, wu2, wu1, wl0,
    pick, grow, fold2, unfold2, fold3, unfold3, fold_edge, unfold_edge,
    bias0, bias1, bias2, bias3, off2, off1, off0,
    send_sem, recv_sem, load_sem,
):
    (
        x_ref,
        k0, b0, k1, b1, k2, b2, k3, b3,
        lift2, ku2, c2, lift1, ku1, c1, lift0, kd0, c0,
    ) = locals_
    z, y, x = lax.axis_index("gz"), lax.axis_index("gy"), lax.axis_index("gx")
    nz, ny, nx = lax.axis_size("gz"), lax.axis_size("gy"), lax.axis_size("gx")

    def device(dz, dy, dx):
        return (lax.rem(z + dz + nz, nz), lax.rem(y + dy + ny, ny), lax.rem(x + dx + nx, nx))

    others = [(dz, dy, dx) for dz, dy in FAR for dx in STEPS if (dz, dy, dx) != (0, 0, 0)]
    barrier = pltpu.get_barrier_semaphore()
    for step in others:
        pl.semaphore_signal(
            barrier, inc=1, device_id=device(*step), device_id_type=pl.DeviceIdType.MESH
        )

    loads = [
        pltpu.make_async_copy(source, local, load_sem.at[k])
        for k, (source, local) in enumerate(zip(sources, locals_))
    ]
    for load in loads:
        load.start()

    count = itertools.count()

    def send(src, dst, step):
        k = next(count)
        copy = pltpu.make_async_remote_copy(
            src_ref=src,
            dst_ref=dst,
            send_sem=send_sem.at[k],
            recv_sem=recv_sem.at[k],
            device_id=device(*step),
            device_id_type=pl.DeviceIdType.MESH,
        )
        copy.start()
        return copy

    def send_rows(buffer, sizes, halos):
        copies = []
        for dz, dy in RING:
            s0, t0, n0 = span(dz, sizes[0], halos[0])
            s1, t1, n1 = span(dy, sizes[1], halos[1])
            copies.append(
                send(
                    buffer.at[pl.ds(s0, n0), pl.ds(s1, n1)],
                    buffer.at[pl.ds(t0, n0), pl.ds(t1, n1)],
                    (dz, dy, 0),
                )
            )
        return copies

    def send_edges(mine, edge, steps, reach):
        copies = []
        for dz, dy in steps:
            for dx in (-1, 1):
                side = 0 if dx > 0 else 1
                copies.append(
                    send(mine.at[1 - side], edge.at[side, reach - dz, 1 - dy], (dz, dy, dx))
                )
        return copies

    def wait_recv(copies):
        for copy in copies:
            copy.wait_recv()

    def wait_send(copies):
        for copy in copies:
            copy.wait_send()

    lane = lax.broadcasted_iota(jnp.int32, (1, 128), 1)
    inside_left = (x > 0).astype(jnp.int32)
    inside_right = (x < nx - 1).astype(jnp.int32)

    def within(dz, dy):
        pz, py = z + dz, y + dy
        ok = (pz >= 0) & (pz < nz) & (py >= 0) & (py < ny)
        return ok.astype(jnp.int32)

    loads[0].wait()
    for c in range(16):
        xf[pl.ds(c * 128, 128), :] = x_ref[c].reshape(128, 128).astype(F32)

    def to_row(r, _):
        vol[1 + lax.div(r, 16), 1 + lax.rem(r, 16)] = xf[pl.ds(r, 16, stride=128), :].astype(BF16)
        return 0

    lax.fori_loop(0, 128, to_row, 0, unroll=8)
    row_id = lax.broadcasted_iota(jnp.int32, (32, 2048), 0)
    col_id = lax.broadcasted_iota(jnp.int32, (32, 2048), 1)
    wanted = lax.rem(row_id, 16) * 128 + jnp.where(row_id < 16, 0, 127)
    chooser = (col_id == wanted).astype(F32).astype(BF16)
    flat = jnp.concatenate([x_ref[c].reshape(128, 128) for c in range(16)], axis=1)
    ends = lax.dot_general(
        chooser, flat, (((1,), (1,)), ((), ())), preferred_element_type=F32
    ).astype(BF16)
    mine0[0] = ends[:16]
    mine0[1] = ends[16:]

    pl.semaphore_wait(barrier, len(others))
    sent = []
    rows_in = send_rows(vol, (8, 16), (1, 1))
    edges_in = send_edges(mine0, edge0, PLANE, 1)
    sent += rows_in + edges_in

    for load in loads[1:]:
        load.wait()

    def column(ref, size):
        a = lax.broadcasted_iota(jnp.int32, (size, size), 0)
        b = lax.broadcasted_iota(jnp.int32, (size, size), 1)
        spread = jnp.broadcast_to(ref[...], (size, size))
        return jnp.sum(jnp.where(a == b, spread, 0.0), axis=1, keepdims=True)

    for ref, target, size, times in (
        (b0, bias0, 16, 4),
        (b1, bias1, 32, 2),
        (b2, bias2, 64, 1),
        (b3, bias3, 128, 1),
        (c2, off2, 64, 1),
        (c1, off1, 32, 2),
        (c0, off0, 16, 4),
    ):
        wide = jnp.broadcast_to(column(ref, size), (size, 128))
        for j in range(times):
            target[pl.ds(j * size, size), :] = wide

    for ref in (wa0, wd0, wu1, wl0):
        ref[...] = jnp.zeros(ref.shape, BF16)
    for a, e, f in itertools.product(range(3), repeat=3):
        tap = (a * 3 + e) * 3 + f
        first, last = k0[tap], kd0[tap]
        for j in range(4):
            at = (a * 6 + e + j) * 48 + f * 16
            wa0[j * 16 : j * 16 + 16, at : at + 16] = first
            at = (a * 6 + e + j) * 96 + f * 16
            wd0[j * 16 : j * 16 + 16, at : at + 16] = last[:, :16]
            wd0[j * 16 : j * 16 + 16, at + 48 : at + 64] = last[:, 16:]
        for j in range(2):
            row = (f * 2 + j) * 32
            at = (a * 4 + e + j) * 64
            wu1[row : row + 32, at : at + 64] = ku1[tap]
        at = a * 3 + e
        wu2[f * 64 : f * 64 + 64, at * 128 : at * 128 + 128] = ku2[tap]

    def turned(pieces, size):
        a = lax.broadcasted_iota(jnp.int32, (size, size), 0)
        b = lax.broadcasted_iota(jnp.int32, (size, size), 1)
        return lax.dot_general(
            (a == b).astype(F32).astype(BF16),
            jnp.concatenate(pieces, axis=0),
            (((1,), (1,)), ((), ())),
            preferred_element_type=F32,
        ).astype(BF16)

    gap = jnp.zeros((16, 32), BF16)
    for f in range(3):
        for j in range(2):
            pieces = [
                k1[(a * 3 + g - j) * 3 + f] if 0 <= g - j < 3 else gap
                for a, g in itertools.product(range(3), range(4))
            ]
            row = (f * 2 + j) * 32
            w1[row : row + 32, :] = turned(pieces, 32)
        w2[f * 64 : f * 64 + 64, :] = turned([k2[at * 3 + f] for at in range(9)], 64)
        w3[f * 128 : f * 128 + 128, :] = turned([k3[at * 3 + f] for at in range(9)], 128)
    for j in range(2):
        wl0[j * 16 : j * 16 + 16, j * 32 : j * 32 + 32] = lift0[...]

    def selector(target, rule):
        a = lax.broadcasted_iota(jnp.int32, target.shape, 0)
        b = lax.broadcasted_iota(jnp.int32, target.shape, 1)
        target[...] = rule(a, b).astype(F32).astype(BF16)

    def pick_rule(a, b):
        cell = (b & 127) - 32
        return (cell >= 0) & (cell < 64) & (a == 2 * cell + (b >> 7))

    def rule2(tall, flat, spread):
        q, at = tall >> 7, (tall & 127) - 32
        w = flat & 31
        return (q == (flat >> 5)) & (at >= 2 * w) & (at < 2 * w + spread)

    def rule3(tall, flat, spread):
        r, q, at = tall >> 9, (tall >> 7) & 3, (tall & 127) - 32
        w = flat & 15
        return (q == (flat >> 5)) & (r == ((flat >> 4) & 1)) & (at >= 4 * w) & (at < 4 * w + spread)

    def rule_edge(tall, flat, spread):
        q, at, m = tall >> 7, tall & 127, flat & 31
        size = jnp.where(m < 16, 2, 4)
        start = jnp.where(m < 16, 2 * m, 4 * m - 32)
        return (q == (flat >> 5)) & (m < 20) & (at >= start) & (at < start + (size if spread else 1))

    selector(pick, pick_rule)
    selector(grow, lambda a, b: a == (((b & 127) + (b >> 7) + 1) >> 1) + 31)
    selector(fold2, lambda a, b: rule2(a, b, 1))
    selector(unfold2, lambda a, b: rule2(b, a, 2))
    selector(fold3, lambda a, b: rule3(a, b, 1))
    selector(unfold3, lambda a, b: rule3(b, a, 4))
    selector(fold_edge, lambda a, b: rule_edge(a, b, False))
    selector(unfold_edge, lambda a, b: rule_edge(b, a, True))

    def shifted(src, edge, target, base):
        for dz, dy in PLANE:
            p0, n0, s0 = region(dz, 8, 1)
            p1, n1, s1 = region(dy, 16, 1)
            ok = within(dz, dy)
            ok_left = (ok * inside_left).astype(F32)
            ok_right = (ok * inside_right).astype(F32)
            ok = ok.astype(F32)
            left_edge = edge[0, dz + 1, dy + 1].astype(F32) * ok_left
            right_edge = edge[1, dz + 1, dy + 1].astype(F32) * ok_right

            def body(i, _):
                i0, i1 = lax.div(i, n1), lax.rem(i, n1)
                r = (s0 + i0) * 16 + s1 + i1
                row = src[p0 + i0, p1 + i1].astype(F32)
                if (dz, dy) != (0, 0):
                    row = row * ok
                left = pltpu.roll(left_edge, lax.rem(128 - r, 128), 1)
                right = pltpu.roll(right_edge, 127 - r, 1)
                d, h = base + p0 + i0, base + p1 + i1
                target[d, h, 0:16, :] = jnp.where(lane == 0, left, pltpu.roll(row, 1, 1)).astype(BF16)
                target[d, h, 16:32, :] = row.astype(BF16)
                target[d, h, 32:48, :] = jnp.where(
                    lane == 127, right, pltpu.roll(row, 127, 1)
                ).astype(BF16)
                return 0

            lax.fori_loop(0, n0 * n1, body, 0, unroll=min(4, n0 * n1))

    wait_recv(rows_in + edges_in)
    shifted(vol, edge0, stack0, 0)

    def encode(i, _):
        d, h = lax.div(i, 4) * 2, lax.rem(i, 4) * 4
        cells = [stack0[pl.ds(d + j, 3), pl.ds(h, 6)].reshape(864, 128) for j in range(2)]
        total = jnp.dot(wa0[...], jnp.concatenate(cells, axis=1), preferred_element_type=F32)
        halves = [
            leaky(total[:, j * 128 : j * 128 + 128] + bias0[...]).astype(BF16) for j in range(2)
        ]
        for j in range(2):
            zero[1 + d + j, pl.ds(1 + h, 4)] = halves[j].reshape(4, 16, 128)
        top = jnp.maximum(halves[0], halves[1]).reshape(2, 2, 16, 128)
        top = jnp.maximum(top[:, 0], top[:, 1]).reshape(32, 128)
        both = jnp.dot(top, pick[...], preferred_element_type=F32)
        best = jnp.maximum(both[:, :128], both[:, 128:])
        pool0[3 + lax.div(d, 2), pl.ds(3 + lax.div(h, 2), 2)] = best.astype(BF16).reshape(2, 16, 128)
        pair0[3 + lax.div(d, 2), 2 + lax.div(h, 4)] = (
            best[:16] + pltpu.roll(best[16:], 64, 1)
        ).astype(BF16)
        return 0

    lax.fori_loop(0, 16, encode, 0, unroll=2)

    def pack1(r, carry):
        first, last = carry
        row = pool0[3 + lax.div(r, 8), 3 + lax.rem(r, 8)].astype(F32)
        mine = lax.div(lane, 4) == r
        first = jnp.where(mine, pltpu.roll(row, lax.rem(4 * r + 96, 128), 1), first)
        last = jnp.where(mine, pltpu.roll(row, lax.rem(4 * r + 35, 128), 1), last)
        return first, last

    blank = jnp.zeros((16, 128), F32)
    first, last = lax.fori_loop(0, 32, pack1, (blank, blank), unroll=4)
    mine1[0] = first.astype(BF16)
    mine1[1] = last.astype(BF16)
    rows1 = send_rows(pair0, (4, 4), (3, 2))
    edges1 = send_edges(mine1, edge1, PLANE, 1)
    sent += rows1 + edges1

    wait_recv(rows1 + edges1)

    def packz(r, carry):
        first, last = carry
        row = zero[1 + lax.div(r, 16), 1 + lax.rem(r, 16)].astype(F32)
        first = jnp.where(lane == r, pltpu.roll(row, r, 1), first)
        last = jnp.where(lane == r, pltpu.roll(row, lax.rem(r + 1, 128), 1), last)
        return first, last

    first, last = lax.fori_loop(0, 128, packz, (blank, blank), unroll=4)
    minez[0] = first.astype(BF16)
    minez[1] = last.astype(BF16)
    rowsz = send_rows(zero, (8, 16), (1, 1))
    edgesz = send_edges(minez, edgez, PLANE, 1)
    sent += rowsz + edgesz

    own = (lane >= 32) & (lane < 96)
    for dz, dy in PLANE:
        p0, n0, s0 = region(dz, 4, 3)
        p1, n1, s1 = region(dy, 8, 3)
        ok = within(dz, dy)
        left_edge = edge1[0, dz + 1, dy + 1].astype(F32) * (ok * inside_left).astype(F32)
        right_edge = edge1[1, dz + 1, dy + 1].astype(F32) * (ok * inside_right).astype(F32)
        keep = ok.astype(F32)

        def join_rows(i, _):
            i0, i1 = lax.div(i, n1), lax.rem(i, n1)
            r = (s0 + i0) * 8 + s1 + i1
            if (dz, dy) == (0, 0):
                row = pool0[p0 + i0, p1 + i1].astype(F32)
            else:
                at = p1 + i1 + 1
                row = pair0[p0 + i0, lax.div(at, 2)].astype(F32) * keep
                row = jnp.where(own, pltpu.roll(row, 64 * lax.rem(at, 2), 1), 0.0)
            left = pltpu.roll(left_edge, lax.rem(157 - 4 * r, 128), 1)
            right = pltpu.roll(right_edge, lax.rem(224 - 4 * r, 128), 1)
            row = jnp.where((lane >= 29) & (lane < 32), left, row)
            row = jnp.where((lane >= 96) & (lane < 99), right, row)
            pool0[p0 + i0, p1 + i1] = row.astype(BF16)
            return 0

        lax.fori_loop(0, n0 * n1, join_rows, 0, unroll=3 if n0 * n1 == 9 else 4)

    lanes_ok = ((lane >= 32) | (x > 0)) & ((lane < 96) | (x < nx - 1))
    lanes_ok = lanes_ok.astype(jnp.int32)

    def keeps(d, h, depth, height):
        gd, gh = z * depth + d, y * height + h
        ok = (gd >= 0) & (gd < nz * depth) & (gh >= 0) & (gh < ny * height)
        return (lanes_ok * ok.astype(jnp.int32)) > 0

    def combine(total, rows, shift, part):
        cut = slice(part * 128, part * 128 + 128)
        return (
            pltpu.roll(total[:rows, cut], shift, 1)
            + total[rows : 2 * rows, cut]
            + pltpu.roll(total[2 * rows :, cut], 128 - shift, 1)
        )

    def pairs(row, width):
        even = lax.rem(lax.div(lane, width), 2) == 0
        other = jnp.where(even, pltpu.roll(row, 128 - width, 1), pltpu.roll(row, width, 1))
        return jnp.maximum(row, other)

    def second(i, _):
        d, h = lax.div(i, 6) * 2, lax.rem(i, 6) * 2
        cells = [pool0[pl.ds(d + j, 3), pl.ds(h, 4)].reshape(192, 128) for j in range(2)]
        total = jnp.dot(w1[...], jnp.concatenate(cells, axis=1), preferred_element_type=F32)
        best = None
        for j in range(2):
            value = leaky(combine(total, 64, 1, j) + bias1[...])
            for g in range(2):
                row = jnp.where(keeps(d + j - 2, h + g - 2, 4, 8), value[g * 32 : g * 32 + 32], 0.0)
                join1[d + j, h + g, 0:32, :] = row.astype(BF16)
                best = row if best is None else jnp.maximum(best, row)
        pool1[lax.div(d, 2), lax.div(h, 2)] = pairs(best, 1).astype(BF16)
        return 0

    lax.fori_loop(0, 24, second, 0, unroll=2)


    def third(h, _):
        cells = [pool1[pl.ds(j, 3), pl.ds(h, 3)].reshape(288, 128) for j in range(2)]
        total = jnp.dot(w2[...], jnp.concatenate(cells, axis=1), preferred_element_type=F32)
        for j in range(2):
            value = leaky(combine(total, 64, 2, j) + bias2[...])
            join2[2 + j, 2 + h, 0:64, :] = jnp.where(own, value, 0.0).astype(BF16)
        return 0

    lax.fori_loop(0, 4, third, 0, unroll=2)
    first = jnp.zeros((64, 128), F32)
    last = jnp.zeros((64, 128), F32)
    for h in range(2):
        best = None
        for j, g in itertools.product(range(2), repeat=2):
            row = join2[2 + j, 2 + 2 * h + g, 0:64, :].astype(F32)
            best = row if best is None else jnp.maximum(best, row)
            r = j * 4 + 2 * h + g
            here = lax.div(lane, 4) == r
            first = jnp.where(here, pltpu.roll(row, (4 * r + 96) % 128, 1), first)
            last = jnp.where(here, pltpu.roll(row, (4 * r + 36) % 128, 1), last)
        best = pairs(best, 2)
        pool2[2, 2 + h] = best.astype(BF16)
        here = lax.div(lane, 8) == 4 + h
        first = jnp.where(here, pltpu.roll(best, 8 * h, 1), first)
        last = jnp.where(here, pltpu.roll(best, 8 * h + 72, 1), last)
    def fold(rows, groups, matrix):
        size = rows[0].shape[0] // groups
        pieces = [row[q * size : q * size + size] for q in range(groups) for row in rows]
        return jnp.dot(
            jnp.concatenate(pieces, axis=1), matrix[...], preferred_element_type=F32
        ).astype(BF16)

    mine2[0] = fold([first.astype(BF16)], 4, fold_edge)
    mine2[1] = fold([last.astype(BF16)], 4, fold_edge)
    pieces = [pool2[2, 2 + r][q * 16 : q * 16 + 16] for r in range(2) for q in range(4)]
    folded3[2, 1] = jnp.dot(
        jnp.concatenate(pieces, axis=1), fold3[...], preferred_element_type=F32
    ).astype(BF16)
    edges2 = send_edges(mine2, edge2, FAR, 2)
    pools2 = [
        send(folded3.at[2, 1], folded3.at[2 - dz, 1 - dy], (dz, dy, 0))
        for dz, dy in FAR
        if (dz, dy) != (0, 0)
    ]
    for j, g in itertools.product(range(2), repeat=2):
        rows = [join2[2 + j, 2 + 2 * g + p, 0:64, :] for p in range(2)]
        folded2[2 + j, 1 + g] = fold(rows, 2, fold2)
    rows2 = send_rows(folded2, (2, 2), (2, 1))
    sent += pools2 + rows2
    sent += edges2

    wait_recv(rowsz + edgesz)
    shifted(zero, edgez, join0, 1)

    wait_recv(edges2 + pools2)
    for side in range(2):
        for dz in range(5):
            parts = jnp.dot(
                edge2[side, dz].reshape(48, 128), unfold_edge[...], preferred_element_type=F32
            ).astype(BF16)
            for q in range(4):
                wide2[side, dz, :, q * 16 : q * 16 + 16, :] = parts[
                    :, q * 128 : q * 128 + 128
                ].reshape(3, 16, 128)
    for dz in range(-2, 3):
        if dz != 0:
            tiles, steps = folded3[2 + dz].reshape(48, 128), STEPS
        else:
            tiles, steps = jnp.concatenate([folded3[2, 0], folded3[2, 2]], axis=0), (-1, 1)
        parts = jnp.dot(tiles, unfold3[...], preferred_element_type=F32).astype(BF16)
        for k, dy in enumerate(steps):
            for r, q in itertools.product(range(2), range(4)):
                at = (r * 4 + q) * 128
                pool2[2 + dz, 2 + 2 * dy + r, q * 16 : q * 16 + 16, :] = parts[
                    k * 16 : k * 16 + 16, at : at + 128
                ]
    for dz, dy in FAR:
        ok = within(dz, dy)
        left_edge = wide2[0, dz + 2, dy + 1].astype(F32) * (ok * inside_left).astype(F32)
        right_edge = wide2[1, dz + 2, dy + 1].astype(F32) * (ok * inside_right).astype(F32)
        keep = ok.astype(F32)
        for r in range(2):
            row = pool2[2 + dz, 2 + 2 * dy + r].astype(F32) * keep
            left = pltpu.roll(left_edge, (24 - 32 - 8 * r) % 128, 1)
            right = pltpu.roll(right_edge, (96 - 32 - 8 * r) % 128, 1)
            row = jnp.where((lane >= 24) & (lane < 32), left, row)
            row = jnp.where((lane >= 96) & (lane < 104), right, row)
            pool2[2 + dz, 2 + 2 * dy + r] = row.astype(BF16)

    def coarsest(i, _):
        d, h = lax.div(i, 2), lax.rem(i, 2) * 2
        cells = [pool2[pl.ds(d, 3), pl.ds(h + j, 3)].reshape(576, 128) for j in range(2)]
        total = jnp.dot(w3[...], jnp.concatenate(cells, axis=1), preferred_element_type=F32)
        low = []
        for j in range(2):
            value = leaky(combine(total, 128, 4, j) + bias3[...])
            low.append(jnp.where(keeps(d - 1, h + j - 1, 1, 2), value, 0.0).astype(BF16))
        up = jnp.dot(lift2[...], jnp.concatenate(low, axis=1), preferred_element_type=F32).astype(BF16)
        for j in range(2):
            for p, q in itertools.product(range(2), repeat=2):
                join2[2 * d + p, 2 * (h + j) + q, 64:128, :] = up[:, j * 128 : j * 128 + 128]
        return 0

    lax.fori_loop(0, 6, coarsest, 0, unroll=3)

    wait_recv(rows2)
    for d in range(6):
        near = d in (2, 3)
        tiles = [folded2[d, g] for g in ((0, 3) if near else range(4))]
        parts = jnp.dot(
            jnp.concatenate(tiles, axis=0), unfold2[...], preferred_element_type=F32
        ).astype(BF16)
        for k, g in enumerate((0, 3) if near else range(4)):
            for q, p in itertools.product(range(2), repeat=2):
                at = (q * 2 + p) * 128
                join2[d, 2 * g + p, q * 32 : q * 32 + 32, :] = parts[
                    k * 32 : k * 32 + 32, at : at + 128
                ]
    for dz, dy in PLANE:
        p0, n0, s0 = region(dz, 2, 2)
        p1, n1, s1 = region(dy, 4, 2)
        ok = within(dz, dy)
        left_edge = wide2[0, dz + 2, dy + 1].astype(F32) * (ok * inside_left).astype(F32)
        right_edge = wide2[1, dz + 2, dy + 1].astype(F32) * (ok * inside_right).astype(F32)
        keep = ok.astype(F32)
        for i0, i1 in itertools.product(range(n0), range(n1)):
            r = (s0 + i0) * 4 + s1 + i1
            row = join2[p0 + i0, p1 + i1, 0:64, :].astype(F32) * keep
            left = pltpu.roll(left_edge, (28 - 4 * r) % 128, 1)
            right = pltpu.roll(right_edge, (96 - 4 * r) % 128, 1)
            row = jnp.where((lane >= 28) & (lane < 32), left, row)
            row = jnp.where((lane >= 96) & (lane < 100), right, row)
            join2[p0 + i0, p1 + i1, 0:64, :] = row.astype(BF16)

    def upper_two(i, _):
        d, h = lax.div(i, 6) * 2, lax.rem(i, 6)
        cells = [join2[pl.ds(d + j, 3), pl.ds(h, 3)].reshape(1152, 128) for j in range(2)]
        total = jnp.dot(wu2[...], jnp.concatenate(cells, axis=1), preferred_element_type=F32)
        low = []
        for j in range(2):
            value = leaky(combine(total, 64, 2, j) + off2[...])
            low.append(jnp.where(keeps(d + j - 1, h - 1, 2, 4), value, 0.0).astype(BF16))
        up = jnp.dot(lift1[...], jnp.concatenate(low, axis=1), preferred_element_type=F32).astype(BF16)
        for j in range(2):
            for p, q in itertools.product(range(2), repeat=2):
                join1[2 * (d + j) + p, 2 * h + q, 32:64, :] = up[:, j * 128 : j * 128 + 128]
        return 0

    lax.fori_loop(0, 12, upper_two, 0, unroll=3)

    def upper_one(i, _):
        d, h = lax.div(i, 5) * 2, lax.rem(i, 5) * 2
        cells = [join1[pl.ds(d + j, 3), pl.ds(h, 4)].reshape(768, 128) for j in range(2)]
        total = jnp.dot(wu1[...], jnp.concatenate(cells, axis=1), preferred_element_type=F32)
        low = []
        for j in range(2):
            value = leaky(combine(total, 64, 1, j) + off1[...])
            kept = [
                jnp.where(keeps(d + j - 1, h + g - 1, 4, 8), value[g * 32 : g * 32 + 32], 0.0)
                for g in range(2)
            ]
            low.append(jnp.concatenate(kept, axis=0).astype(BF16))
        up = jnp.dot(wl0[...], jnp.concatenate(low, axis=1), preferred_element_type=F32).astype(BF16)
        up = jnp.concatenate([up[:, :128], up[:, 128:]], axis=0)
        wide = jnp.dot(up, grow[...], preferred_element_type=F32).astype(BF16)
        for j, g in itertools.product(range(2), repeat=2):
            at = (j * 2 + g) * 16
            three = [wide[at : at + 16, f * 128 : f * 128 + 128] for f in range(3)]
            three = jnp.concatenate(three, axis=0)
            for p, q in itertools.product(range(2), repeat=2):
                join0[2 * (d + j) + p, 2 * (h + g) + q, 48:96, :] = three
        return 0

    lax.fori_loop(0, 15, upper_one, 0, unroll=3)

    def decode(i, _):
        d, h = lax.div(i, 4) * 2, lax.rem(i, 4) * 4
        cells = [join0[pl.ds(d + 1 + j, 3), pl.ds(h + 1, 6)].reshape(1728, 128) for j in range(2)]
        total = jnp.dot(wd0[...], jnp.concatenate(cells, axis=1), preferred_element_type=F32)
        for j in range(2):
            value = leaky(total[:, j * 128 : j * 128 + 128] + off0[...])
            for g in range(4):
                xf[pl.ds((d + j) * 16 + h + g, 16, stride=128), :] = value[g * 16 : g * 16 + 16]
        return 0

    lax.fori_loop(0, 16, decode, 0, unroll=2)
    for c in range(16):
        out_ref[c] = xf[pl.ds(c * 128, 128), :].astype(BF16).reshape(8, 16, 128)

    wait_send(sent)


def taps(weights):
    out, inner = weights.shape[:2]
    return jnp.transpose(weights, (2, 3, 4, 0, 1)).reshape(27, out, inner)


def turned_taps(weights):
    out, inner = weights.shape[:2]
    return jnp.transpose(weights, (2, 3, 4, 1, 0)).reshape(27, inner, out)


def per_device(
    volume,
    surface_conv,
    surface_bias,
    second_conv,
    second_bias,
    middle_conv,
    middle_bias,
    bottom_conv,
    bottom_bias,
    middle_lift,
    middle_return,
    middle_offset,
    second_lift,
    second_return,
    second_offset,
    surface_lift,
    surface_return,
    surface_offset,
):
    def tile(*shape):
        return pltpu.VMEM(shape, BF16)

    def wide(rows):
        return pltpu.VMEM((rows, 128), F32)

    scratch = [
        wide(2048), tile(10, 18, 16, 128), tile(2, 3, 3, 16, 128), tile(2, 16, 128), tile(10, 18, 48, 128),
        tile(10, 18, 16, 128), tile(2, 3, 3, 16, 128), tile(2, 16, 128),
        tile(10, 14, 16, 128), tile(10, 8, 16, 128), tile(2, 3, 3, 16, 128), tile(2, 16, 128),
        tile(8, 12, 64, 128), tile(4, 6, 32, 128), tile(6, 8, 128, 128),
        tile(5, 6, 64, 128), tile(2, 5, 3, 64, 128), tile(2, 5, 3, 16, 128), tile(2, 16, 128),
        tile(6, 4, 32, 128), tile(5, 3, 16, 128), tile(12, 20, 96, 128),
        tile(64, 864), tile(64, 1728), tile(192, 192), tile(192, 288), tile(384, 576),
        tile(192, 1152), tile(192, 768), tile(32, 64),
        tile(128, 256), tile(128, 384),
        tile(512, 128), tile(128, 512), tile(1024, 128), tile(128, 1024), tile(512, 128), tile(128, 512),
        wide(64), wide(64), wide(64), wide(128), wide(64), wide(64), wide(64),
        pltpu.SemaphoreType.DMA((130,)), pltpu.SemaphoreType.DMA((130,)), pltpu.SemaphoreType.DMA((18,)),
    ]

    def line(values):
        return values.reshape(1, values.shape[0])

    operands = (
        volume,
        taps(surface_conv), line(surface_bias),
        turned_taps(second_conv), line(second_bias),
        turned_taps(middle_conv), line(middle_bias),
        turned_taps(bottom_conv), line(bottom_bias),
        middle_lift, taps(middle_return), line(middle_offset),
        second_lift, taps(second_return), line(second_offset),
        surface_lift, taps(surface_return), line(surface_offset),
    )
    return pl.pallas_call(
        kernel,
        out_shape=jax.ShapeDtypeStruct(volume.shape, BF16),
        in_specs=[pl.BlockSpec(memory_space=pltpu.HBM)] * len(operands),
        out_specs=pl.BlockSpec(memory_space=pltpu.VMEM),
        scratch_shapes=[pltpu.VMEM(value.shape, value.dtype) for value in operands] + scratch,
        compiler_params=pltpu.CompilerParams(
            collective_id=0, has_side_effects=True, vmem_limit_bytes=60 * 2**20
        ),
    )(*operands)


def solution(mesh):
    placed = (P(None, "gz", "gy", "gx"),) + (P(),) * 17
    return jax.shard_map(
        per_device, mesh=mesh, in_specs=placed, out_specs=P(None, "gz", "gy", "gx"), check_vma=False
    )
```

```python
import itertools

import jax
import jax.numpy as jnp
from jax import lax
from jax.experimental import pallas as pl
from jax.experimental.pallas import tpu as pltpu
from jax.sharding import PartitionSpec as P

BF16 = jnp.bfloat16
F32 = jnp.float32
STEPS = (-1, 0, 1)
PLANE = [(dz, dy) for dz in STEPS for dy in STEPS]
RING = [step for step in PLANE if step != (0, 0)]
FAR = [(dz, dy) for dz in (-2, -1, 0, 1, 2) for dy in STEPS]


def span(step, size, halo):
    if step == 0:
        return halo, halo, size
    if step > 0:
        return size, 0, halo
    return halo, halo + size, halo


def region(step, size, halo):
    if step == 0:
        return halo, size, 0
    if step < 0:
        return 0, halo, size - halo
    return halo + size, halo, 0


def leaky(total):
    return jnp.maximum(total, 0.1 * total)


def kernel(*refs):
    sources, refs = refs[:18], refs[18:]
    out_ref, refs = refs[0], refs[1:]
    locals_, refs = refs[:18], refs[18:]
    body(sources, locals_, out_ref, *refs)


def body(
    sources,
    locals_,
    out_ref,
    xf, vol, edge0, mine0, stack0,
    zero, edgez, minez,
    top0, pool0, pair0, edge1, mine1,
    skip1, low2, lifted1, pool1, skip2, low3, up2, pool2, wide2, edge2, mine2, folded2, folded3, low1, lifted0, part0, part1,
    wa0, wds, wdl, w1, w2, w3, wu2, wus, wul, wl0,
    pick, grow, fold2, unfold2, fold3, unfold3, fold_edge, unfold_edge,
    bias0, bias1, bias2, bias3, off2, off1, off0,
    send_sem, recv_sem, load_sem,
):
    (
        x_ref,
        k0, b0, k1, b1, k2, b2, k3, b3,
        lift2, ku2, c2, lift1, ku1, c1, lift0, kd0, c0,
    ) = locals_
    z, y, x = lax.axis_index("gz"), lax.axis_index("gy"), lax.axis_index("gx")
    nz, ny, nx = lax.axis_size("gz"), lax.axis_size("gy"), lax.axis_size("gx")

    def device(dz, dy, dx):
        return (lax.rem(z + dz + nz, nz), lax.rem(y + dy + ny, ny), lax.rem(x + dx + nx, nx))

    beyond = [step for step in FAR if step not in PLANE]
    others = [(*step, dx) for step in PLANE + beyond for dx in STEPS if (*step, dx) != (0, 0, 0)]
    barrier = pltpu.get_barrier_semaphore()
    for step in others:
        pl.semaphore_signal(
            barrier, inc=1, device_id=device(*step), device_id_type=pl.DeviceIdType.MESH
        )

    loads = [
        pltpu.make_async_copy(source, local, load_sem.at[k])
        for k, (source, local) in enumerate(zip(sources, locals_))
    ]
    for load in loads:
        load.start()

    count = itertools.count()

    def send(src, dst, step):
        k = next(count)
        copy = pltpu.make_async_remote_copy(
            src_ref=src,
            dst_ref=dst,
            send_sem=send_sem.at[k],
            recv_sem=recv_sem.at[k],
            device_id=device(*step),
            device_id_type=pl.DeviceIdType.MESH,
        )
        copy.start()
        return copy

    def send_rows(buffer, sizes, halos):
        copies = []
        for dz, dy in RING:
            s0, t0, n0 = span(dz, sizes[0], halos[0])
            s1, t1, n1 = span(dy, sizes[1], halos[1])
            copies.append(
                send(
                    buffer.at[pl.ds(s0, n0), pl.ds(s1, n1)],
                    buffer.at[pl.ds(t0, n0), pl.ds(t1, n1)],
                    (dz, dy, 0),
                )
            )
        return copies

    def send_edges(mine, edge, steps, reach):
        copies = []
        for dz, dy in steps:
            for dx in (-1, 1):
                side = 0 if dx > 0 else 1
                copies.append(
                    send(mine.at[1 - side], edge.at[side, reach - dz, 1 - dy], (dz, dy, dx))
                )
        return copies

    def wait_recv(copies):
        for copy in copies:
            copy.wait_recv()

    def wait_send(copies):
        for copy in copies:
            copy.wait_send()

    lane = lax.broadcasted_iota(jnp.int32, (1, 128), 1)
    inside_left = (x > 0).astype(jnp.int32)
    inside_right = (x < nx - 1).astype(jnp.int32)

    def within(dz, dy):
        pz, py = z + dz, y + dy
        ok = (pz >= 0) & (pz < nz) & (py >= 0) & (py < ny)
        return ok.astype(jnp.int32)

    loads[0].wait()
    for c in range(16):
        xf[pl.ds(c * 128, 128), :] = x_ref[c].reshape(128, 128).astype(F32)

    def to_row(r, _):
        vol[1 + lax.div(r, 16), 1 + lax.rem(r, 16)] = xf[pl.ds(r, 16, stride=128), :].astype(BF16)
        return 0

    lax.fori_loop(0, 128, to_row, 0, unroll=8)
    row_id = lax.broadcasted_iota(jnp.int32, (32, 2048), 0)
    col_id = lax.broadcasted_iota(jnp.int32, (32, 2048), 1)
    wanted = lax.rem(row_id, 16) * 128 + jnp.where(row_id < 16, 0, 127)
    chooser = (col_id == wanted).astype(F32).astype(BF16)
    flat = jnp.concatenate([x_ref[c].reshape(128, 128) for c in range(16)], axis=1)
    ends = lax.dot_general(
        chooser, flat, (((1,), (1,)), ((), ())), preferred_element_type=F32
    ).astype(BF16)
    mine0[0] = ends[:16]
    mine0[1] = ends[16:]

    pl.semaphore_wait(barrier, len(others))
    sent = []
    rows_in = send_rows(vol, (8, 16), (1, 1))
    edges_in = send_edges(mine0, edge0, PLANE, 1)
    sent += rows_in + edges_in

    for load in loads[1:]:
        load.wait()

    def column(ref, size):
        a = lax.broadcasted_iota(jnp.int32, (size, size), 0)
        b = lax.broadcasted_iota(jnp.int32, (size, size), 1)
        spread = jnp.broadcast_to(ref[...], (size, size))
        return jnp.sum(jnp.where(a == b, spread, 0.0), axis=1, keepdims=True)

    for ref, target, size, times in (
        (b0, bias0, 16, 4),
        (b1, bias1, 32, 2),
        (b2, bias2, 64, 1),
        (b3, bias3, 128, 1),
        (c2, off2, 64, 1),
        (c1, off1, 32, 2),
        (c0, off0, 16, 4),
    ):
        wide = jnp.broadcast_to(column(ref, size), (size, 128))
        for j in range(times):
            target[pl.ds(j * size, size), :] = wide

    wa0[...] = jnp.zeros(wa0.shape, BF16)
    for a, e, f in itertools.product(range(3), repeat=3):
        first = k0[(a * 3 + e) * 3 + f]
        for j in range(4):
            at = (a * 6 + e + j) * 48 + f * 16
            wa0[j * 16 : j * 16 + 16, at : at + 16] = first

    def selector(target, rule):
        a = lax.broadcasted_iota(jnp.int32, target.shape, 0)
        b = lax.broadcasted_iota(jnp.int32, target.shape, 1)
        target[...] = rule(a, b).astype(F32).astype(BF16)

    def pick_rule(a, b):
        cell = (b & 127) - 32
        return (cell >= 0) & (cell < 64) & (a == 2 * cell + (b >> 7))

    def rule2(tall, flat, spread):
        q, at = tall >> 7, (tall & 127) - 32
        w = flat & 31
        return (q == (flat >> 5)) & (at >= 2 * w) & (at < 2 * w + spread)

    def rule3(tall, flat, spread):
        r, q, at = tall >> 9, (tall >> 7) & 3, (tall & 127) - 32
        w = flat & 15
        return (q == (flat >> 5)) & (r == ((flat >> 4) & 1)) & (at >= 4 * w) & (at < 4 * w + spread)

    def rule_edge(tall, flat, spread):
        q, at, m = tall >> 7, tall & 127, flat & 31
        size = jnp.where(m < 16, 2, 4)
        start = jnp.where(m < 16, 2 * m, 4 * m - 32)
        return (q == (flat >> 5)) & (m < 20) & (at >= start) & (at < start + (size if spread else 1))

    selector(pick, pick_rule)
    def shifted(src, edge, target):
        for dz, dy in PLANE:
            p0, n0, s0 = region(dz, 8, 1)
            p1, n1, s1 = region(dy, 16, 1)
            ok = within(dz, dy)
            ok_left = (ok * inside_left).astype(F32)
            ok_right = (ok * inside_right).astype(F32)
            ok = ok.astype(F32)
            left_edge = edge[0, dz + 1, dy + 1].astype(F32) * ok_left
            right_edge = edge[1, dz + 1, dy + 1].astype(F32) * ok_right

            def body(i, _):
                i0, i1 = lax.div(i, n1), lax.rem(i, n1)
                r = (s0 + i0) * 16 + s1 + i1
                row = src[p0 + i0, p1 + i1].astype(F32)
                if (dz, dy) != (0, 0):
                    row = row * ok
                left = pltpu.roll(left_edge, lax.rem(128 - r, 128), 1)
                right = pltpu.roll(right_edge, 127 - r, 1)
                d, h = p0 + i0, p1 + i1
                target[d, h, 0:16, :] = jnp.where(lane == 0, left, pltpu.roll(row, 1, 1)).astype(BF16)
                target[d, h, 16:32, :] = row.astype(BF16)
                target[d, h, 32:48, :] = jnp.where(
                    lane == 127, right, pltpu.roll(row, 127, 1)
                ).astype(BF16)
                return 0

            lax.fori_loop(0, n0 * n1, body, 0, unroll=min(8, n0 * n1))

    wait_recv(rows_in + edges_in)
    shifted(vol, edge0, stack0)

    def encode(i, _):
        d, h = lax.div(i, 4) * 2, lax.rem(i, 4) * 4
        cells = [stack0[pl.ds(d + j, 3), pl.ds(h, 6)].reshape(864, 128) for j in range(2)]
        total = jnp.dot(wa0[...], jnp.concatenate(cells, axis=1), preferred_element_type=F32)
        halves = [
            leaky(total[:, j * 128 : j * 128 + 128] + bias0[...]).astype(BF16) for j in range(2)
        ]
        for j in range(2):
            zero[1 + d + j, pl.ds(1 + h, 4)] = halves[j].reshape(4, 16, 128)
        top = jnp.maximum(halves[0], halves[1]).reshape(2, 2, 16, 128)
        top = jnp.maximum(top[:, 0], top[:, 1])
        top0[lax.div(d, 2), pl.ds(lax.div(h, 2), 2)] = top
        return 0

    lax.fori_loop(0, 16, encode, 0, unroll=4)
    for d in range(4):
        both = jnp.dot(top0[d].reshape(128, 128), pick[...], preferred_element_type=F32)
        best = jnp.maximum(both[:, :128], both[:, 128:])
        pool0[3 + d, 3:11] = best.astype(BF16).reshape(8, 16, 128)
        best = best.reshape(4, 2, 16, 128)
        odd = pltpu.roll(best[:, 1].reshape(64, 128), 64, 1)
        pair0[3 + d, 2:6] = (best[:, 0].reshape(64, 128) + odd).astype(BF16).reshape(4, 16, 128)

    def pack1(r, carry):
        first, last = carry
        row = pool0[3 + lax.div(r, 8), 3 + lax.rem(r, 8)].astype(F32)
        mine = lax.div(lane, 4) == r
        first = jnp.where(mine, pltpu.roll(row, lax.rem(4 * r + 96, 128), 1), first)
        last = jnp.where(mine, pltpu.roll(row, lax.rem(4 * r + 35, 128), 1), last)
        return first, last

    blank = jnp.zeros((16, 128), F32)
    first, last = lax.fori_loop(0, 32, pack1, (blank, blank), unroll=8)
    mine1[0] = first.astype(BF16)
    mine1[1] = last.astype(BF16)
    rows1 = send_rows(pair0, (4, 4), (3, 2))
    edges1 = send_edges(mine1, edge1, PLANE, 1)
    sent += rows1 + edges1

    for ref in (wds, wdl, wus, wul, wl0):
        ref[...] = jnp.zeros(ref.shape, BF16)
    for a, e, f in itertools.product(range(3), repeat=3):
        tap = (a * 3 + e) * 3 + f
        last = kd0[tap]
        for j in range(4):
            at = (a * 6 + e + j) * 48 + f * 16
            wds[j * 16 : j * 16 + 16, at : at + 16] = last[:, :16]
            wdl[j * 16 : j * 16 + 16, at : at + 16] = last[:, 16:]
        for j in range(2):
            row = (f * 2 + j) * 32
            at = (a * 4 + e + j) * 32
            wus[row : row + 32, at : at + 32] = ku1[tap][:, :32]
            wul[row : row + 32, at : at + 32] = ku1[tap][:, 32:]
        at = a * 3 + e
        wu2[f * 64 : f * 64 + 64, at * 128 : at * 128 + 128] = ku2[tap]

    def turned(pieces, size):
        a = lax.broadcasted_iota(jnp.int32, (size, size), 0)
        b = lax.broadcasted_iota(jnp.int32, (size, size), 1)
        return lax.dot_general(
            (a == b).astype(F32).astype(BF16),
            jnp.concatenate(pieces, axis=0),
            (((1,), (1,)), ((), ())),
            preferred_element_type=F32,
        ).astype(BF16)

    gap = jnp.zeros((16, 32), BF16)
    for f in range(3):
        for j in range(2):
            pieces = [
                k1[(a * 3 + g - j) * 3 + f] if 0 <= g - j < 3 else gap
                for a, g in itertools.product(range(3), range(4))
            ]
            row = (f * 2 + j) * 32
            w1[row : row + 32, :] = turned(pieces, 32)
        w2[f * 64 : f * 64 + 64, :] = turned([k2[at * 3 + f] for at in range(9)], 64)
        w3[f * 128 : f * 128 + 128, :] = turned([k3[at * 3 + f] for at in range(9)], 128)
    for j in range(2):
        wl0[j * 16 : j * 16 + 16, j * 32 : j * 32 + 32] = lift0[...]

    selector(grow, lambda a, b: a == (((b & 127) + (b >> 7) + 1) >> 1) + 31)
    selector(fold2, lambda a, b: rule2(a, b, 1))
    selector(unfold2, lambda a, b: rule2(b, a, 2))
    selector(fold3, lambda a, b: rule3(a, b, 1))
    selector(unfold3, lambda a, b: rule3(b, a, 4))
    selector(fold_edge, lambda a, b: rule_edge(a, b, False))
    selector(unfold_edge, lambda a, b: rule_edge(b, a, True))

    wait_recv(rows1 + edges1)

    def packz(r, carry):
        first, last = carry
        row = zero[1 + lax.div(r, 16), 1 + lax.rem(r, 16)].astype(F32)
        first = jnp.where(lane == r, pltpu.roll(row, r, 1), first)
        last = jnp.where(lane == r, pltpu.roll(row, lax.rem(r + 1, 128), 1), last)
        return first, last

    first, last = lax.fori_loop(0, 128, packz, (blank, blank), unroll=8)
    minez[0] = first.astype(BF16)
    minez[1] = last.astype(BF16)
    rowsz = send_rows(zero, (8, 16), (1, 1))
    edgesz = send_edges(minez, edgez, PLANE, 1)
    sent += rowsz + edgesz

    own = (lane >= 32) & (lane < 96)
    for dz, dy in PLANE:
        p0, n0, s0 = region(dz, 4, 3)
        p1, n1, s1 = region(dy, 8, 3)
        ok = within(dz, dy)
        left_edge = edge1[0, dz + 1, dy + 1].astype(F32) * (ok * inside_left).astype(F32)
        right_edge = edge1[1, dz + 1, dy + 1].astype(F32) * (ok * inside_right).astype(F32)
        keep = ok.astype(F32)

        def join_rows(i, _):
            i0, i1 = lax.div(i, n1), lax.rem(i, n1)
            r = (s0 + i0) * 8 + s1 + i1
            if (dz, dy) == (0, 0):
                row = pool0[p0 + i0, p1 + i1].astype(F32)
            else:
                at = p1 + i1 + 1
                row = pair0[p0 + i0, lax.div(at, 2)].astype(F32) * keep
                row = jnp.where(own, pltpu.roll(row, 64 * lax.rem(at, 2), 1), 0.0)
            left = pltpu.roll(left_edge, lax.rem(157 - 4 * r, 128), 1)
            right = pltpu.roll(right_edge, lax.rem(224 - 4 * r, 128), 1)
            row = jnp.where((lane >= 29) & (lane < 32), left, row)
            row = jnp.where((lane >= 96) & (lane < 99), right, row)
            pool0[p0 + i0, p1 + i1] = row.astype(BF16)
            return 0

        lax.fori_loop(0, n0 * n1, join_rows, 0, unroll=9 if n0 * n1 == 9 else 6 if n0 * n1 < 32 else 8)

    lanes_ok = ((lane >= 32) | (x > 0)) & ((lane < 96) | (x < nx - 1))
    lanes_ok = lanes_ok.astype(jnp.int32)

    def keeps(d, h, depth, height):
        gd, gh = z * depth + d, y * height + h
        ok = (gd >= 0) & (gd < nz * depth) & (gh >= 0) & (gh < ny * height)
        return (lanes_ok * ok.astype(jnp.int32)) > 0

    def combine(total, rows, shift, part):
        cut = slice(part * 128, part * 128 + 128)
        return (
            pltpu.roll(total[:rows, cut], shift, 1)
            + total[rows : 2 * rows, cut]
            + pltpu.roll(total[2 * rows :, cut], 128 - shift, 1)
        )

    def pairs(row, width):
        even = lax.rem(lax.div(lane, width), 2) == 0
        other = jnp.where(even, pltpu.roll(row, 128 - width, 1), pltpu.roll(row, width, 1))
        return jnp.maximum(row, other)

    def second(i, _):
        d, h = lax.div(i, 6) * 2, lax.rem(i, 6) * 2
        cells = [pool0[pl.ds(d + j, 3), pl.ds(h, 4)].reshape(192, 128) for j in range(2)]
        total = jnp.dot(w1[...], jnp.concatenate(cells, axis=1), preferred_element_type=F32)
        best = None
        for j in range(2):
            value = leaky(combine(total, 64, 1, j) + bias1[...])
            for g in range(2):
                row = jnp.where(keeps(d + j - 2, h + g - 2, 4, 8), value[g * 32 : g * 32 + 32], 0.0)
                skip1[d + j, h + g] = row.astype(BF16)
                best = row if best is None else jnp.maximum(best, row)
        pool1[lax.div(d, 2), lax.div(h, 2)] = pairs(best, 1).astype(BF16)
        return 0

    lax.fori_loop(0, 24, second, 0, unroll=4)


    def third(h, _):
        cells = [pool1[pl.ds(j, 3), pl.ds(h, 3)].reshape(288, 128) for j in range(2)]
        total = jnp.dot(w2[...], jnp.concatenate(cells, axis=1), preferred_element_type=F32)
        for j in range(2):
            value = leaky(combine(total, 64, 2, j) + bias2[...])
            skip2[2 + j, 2 + h] = jnp.where(own, value, 0.0).astype(BF16)
        return 0

    lax.fori_loop(0, 4, third, 0, unroll=2)
    first = jnp.zeros((64, 128), F32)
    last = jnp.zeros((64, 128), F32)
    for h in range(2):
        best = None
        for j, g in itertools.product(range(2), repeat=2):
            row = skip2[2 + j, 2 + 2 * h + g].astype(F32)
            best = row if best is None else jnp.maximum(best, row)
            r = j * 4 + 2 * h + g
            here = lax.div(lane, 4) == r
            first = jnp.where(here, pltpu.roll(row, (4 * r + 96) % 128, 1), first)
            last = jnp.where(here, pltpu.roll(row, (4 * r + 36) % 128, 1), last)
        best = pairs(best, 2)
        pool2[2, 2 + h] = best.astype(BF16)
        here = lax.div(lane, 8) == 4 + h
        first = jnp.where(here, pltpu.roll(best, 8 * h, 1), first)
        last = jnp.where(here, pltpu.roll(best, 8 * h + 72, 1), last)
    def fold(rows, groups, matrix):
        size = rows[0].shape[0] // groups
        pieces = [row[q * size : q * size + size] for q in range(groups) for row in rows]
        return jnp.dot(
            jnp.concatenate(pieces, axis=1), matrix[...], preferred_element_type=F32
        ).astype(BF16)

    mine2[0] = fold([first.astype(BF16)], 4, fold_edge)
    mine2[1] = fold([last.astype(BF16)], 4, fold_edge)
    pieces = [pool2[2, 2 + r][q * 16 : q * 16 + 16] for r in range(2) for q in range(4)]
    folded3[2, 1] = jnp.dot(
        jnp.concatenate(pieces, axis=1), fold3[...], preferred_element_type=F32
    ).astype(BF16)
    edges2 = send_edges(mine2, edge2, FAR, 2)
    pools2 = [
        send(folded3.at[2, 1], folded3.at[2 - dz, 1 - dy], (dz, dy, 0))
        for dz, dy in FAR
        if (dz, dy) != (0, 0)
    ]
    for j, g in itertools.product(range(2), repeat=2):
        rows = [skip2[2 + j, 2 + 2 * g + p] for p in range(2)]
        folded2[2 + j, 1 + g] = fold(rows, 2, fold2)
    rows2 = send_rows(folded2, (2, 2), (2, 1))
    sent += pools2 + rows2
    sent += edges2

    def upper_one_skip(i, _):
        d, h = lax.div(i, 5) * 2, lax.rem(i, 5) * 2
        cells = [skip1[pl.ds(d + j, 3), pl.ds(h, 4)].reshape(384, 128) for j in range(2)]
        total = jnp.dot(wus[...], jnp.concatenate(cells, axis=1), preferred_element_type=F32)
        for j in range(2):
            part1[i, j] = combine(total, 64, 1, j) + off1[...]
        return 0

    lax.fori_loop(0, 15, upper_one_skip, 0, unroll=3)

    wait_recv(rowsz + edgesz)
    shifted(zero, edgez, stack0)

    def decode_skip(i, _):
        d, h = lax.div(i, 4) * 2, lax.rem(i, 4) * 4
        cells = [stack0[pl.ds(d + j, 3), pl.ds(h, 6)].reshape(864, 128) for j in range(2)]
        total = jnp.dot(wds[...], jnp.concatenate(cells, axis=1), preferred_element_type=F32)
        for j in range(2):
            value = total[:, j * 128 : j * 128 + 128] + off0[...]
            part0[d + j, pl.ds(h, 4)] = value.reshape(4, 16, 128)
        return 0

    lax.fori_loop(0, 16, decode_skip, 0, unroll=4)

    wait_recv(edges2 + pools2)
    for side in range(2):
        for dz in range(5):
            parts = jnp.dot(
                edge2[side, dz].reshape(48, 128), unfold_edge[...], preferred_element_type=F32
            ).astype(BF16)
            for q in range(4):
                wide2[side, dz, :, q * 16 : q * 16 + 16, :] = parts[
                    :, q * 128 : q * 128 + 128
                ].reshape(3, 16, 128)
    for dz in range(-2, 3):
        if dz != 0:
            tiles, steps = folded3[2 + dz].reshape(48, 128), STEPS
        else:
            tiles, steps = jnp.concatenate([folded3[2, 0], folded3[2, 2]], axis=0), (-1, 1)
        parts = jnp.dot(tiles, unfold3[...], preferred_element_type=F32).astype(BF16)
        for k, dy in enumerate(steps):
            for r, q in itertools.product(range(2), range(4)):
                at = (r * 4 + q) * 128
                pool2[2 + dz, 2 + 2 * dy + r, q * 16 : q * 16 + 16, :] = parts[
                    k * 16 : k * 16 + 16, at : at + 128
                ]
    for dz, dy in FAR:
        ok = within(dz, dy)
        left_edge = wide2[0, dz + 2, dy + 1].astype(F32) * (ok * inside_left).astype(F32)
        right_edge = wide2[1, dz + 2, dy + 1].astype(F32) * (ok * inside_right).astype(F32)
        keep = ok.astype(F32)
        for r in range(2):
            row = pool2[2 + dz, 2 + 2 * dy + r].astype(F32) * keep
            left = pltpu.roll(left_edge, (24 - 32 - 8 * r) % 128, 1)
            right = pltpu.roll(right_edge, (96 - 32 - 8 * r) % 128, 1)
            row = jnp.where((lane >= 24) & (lane < 32), left, row)
            row = jnp.where((lane >= 96) & (lane < 104), right, row)
            pool2[2 + dz, 2 + 2 * dy + r] = row.astype(BF16)

    def coarsest(i, _):
        d, h = lax.div(i, 2), lax.rem(i, 2) * 2
        cells = [pool2[pl.ds(d, 3), pl.ds(h + j, 3)].reshape(576, 128) for j in range(2)]
        total = jnp.dot(w3[...], jnp.concatenate(cells, axis=1), preferred_element_type=F32)
        for j in range(2):
            value = leaky(combine(total, 128, 4, j) + bias3[...])
            row = jnp.where(keeps(d - 1, h + j - 1, 1, 2), value, 0.0)
            low3[d, h + j] = row.astype(BF16)
        return 0

    def lifts(matrix, rows):
        wide = jnp.dot(
            matrix[...], jnp.concatenate(rows, axis=1), preferred_element_type=F32
        ).astype(BF16)
        return [wide[:, k * 128 : k * 128 + 128] for k in range(len(rows))]

    lax.fori_loop(0, 6, coarsest, 0, unroll=6)
    for d in range(3):
        for h, row in enumerate(lifts(lift2, [low3[d, h] for h in range(4)])):
            up2[d, h] = row

    wait_recv(rows2)
    for d in range(6):
        near = d in (2, 3)
        tiles = [folded2[d, g] for g in ((0, 3) if near else range(4))]
        parts = jnp.dot(
            jnp.concatenate(tiles, axis=0), unfold2[...], preferred_element_type=F32
        ).astype(BF16)
        for k, g in enumerate((0, 3) if near else range(4)):
            for q, p in itertools.product(range(2), repeat=2):
                at = (q * 2 + p) * 128
                skip2[d, 2 * g + p, q * 32 : q * 32 + 32, :] = parts[
                    k * 32 : k * 32 + 32, at : at + 128
                ]
    for dz, dy in PLANE:
        p0, n0, s0 = region(dz, 2, 2)
        p1, n1, s1 = region(dy, 4, 2)
        ok = within(dz, dy)
        left_edge = wide2[0, dz + 2, dy + 1].astype(F32) * (ok * inside_left).astype(F32)
        right_edge = wide2[1, dz + 2, dy + 1].astype(F32) * (ok * inside_right).astype(F32)
        keep = ok.astype(F32)
        for i0, i1 in itertools.product(range(n0), range(n1)):
            r = (s0 + i0) * 4 + s1 + i1
            row = skip2[p0 + i0, p1 + i1].astype(F32) * keep
            left = pltpu.roll(left_edge, (28 - 4 * r) % 128, 1)
            right = pltpu.roll(right_edge, (96 - 4 * r) % 128, 1)
            row = jnp.where((lane >= 28) & (lane < 32), left, row)
            row = jnp.where((lane >= 96) & (lane < 100), right, row)
            skip2[p0 + i0, p1 + i1] = row.astype(BF16)

    def upper_two(i, _):
        d, h = lax.div(i, 6) * 2, lax.rem(i, 6)
        cells = []
        for j in range(2):
            pieces = []
            for a, e in itertools.product(range(3), repeat=2):
                pieces.append(skip2[d + j + a, h + e])
                pieces.append(up2[lax.div(i, 6) + (j + a) // 2, lax.div(h + e, 2)])
            cells.append(jnp.concatenate(pieces, axis=0))
        total = jnp.dot(wu2[...], jnp.concatenate(cells, axis=1), preferred_element_type=F32)
        for j in range(2):
            value = leaky(combine(total, 64, 2, j) + off2[...])
            low2[d + j, h] = jnp.where(keeps(d + j - 1, h - 1, 2, 4), value, 0.0).astype(BF16)
        return 0

    lax.fori_loop(0, 12, upper_two, 0, unroll=3)
    for d in range(4):
        for h, row in enumerate(lifts(lift1, [low2[d, h] for h in range(6)])):
            lifted1[d, h] = row

    def upper_one(i, _):
        d, h = lax.div(i, 5) * 2, lax.rem(i, 5) * 2
        cells = []
        for j in range(2):
            pieces = [
                lifted1[lax.div(i, 5) + (j + a) // 2, lax.rem(i, 5) + g // 2]
                for a, g in itertools.product(range(3), range(4))
            ]
            cells.append(jnp.concatenate(pieces, axis=0))
        total = jnp.dot(wul[...], jnp.concatenate(cells, axis=1), preferred_element_type=F32)
        for j in range(2):
            value = leaky(combine(total, 64, 1, j) + part1[i, j])
            kept = [
                jnp.where(keeps(d + j - 1, h + g - 1, 4, 8), value[g * 32 : g * 32 + 32], 0.0)
                for g in range(2)
            ]
            low1[i, j] = jnp.concatenate(kept, axis=0).astype(BF16)
        return 0

    lax.fori_loop(0, 15, upper_one, 0, unroll=5)
    for d in range(3):
        order = list(itertools.product(range(2), range(5)))
        rows = lifts(wl0, [low1[d * 5 + h, j] for j, h in order])
        wide = jnp.dot(
            jnp.concatenate(rows, axis=0), grow[...], preferred_element_type=F32
        ).astype(BF16)
        for k, (j, h) in enumerate(order):
            for g, f in itertools.product(range(2), range(3)):
                at = k * 32 + g * 16
                lifted0[2 * d + j, 2 * h + g, f * 16 : f * 16 + 16, :] = wide[
                    at : at + 16, f * 128 : f * 128 + 128
                ]

    def decode(i, _):
        d, h = lax.div(i, 4) * 2, lax.rem(i, 4) * 4
        cells = []
        for j in range(2):
            pieces = [
                lifted0[lax.div(d, 2) + (1 + j + a) // 2, lax.div(h, 2) + (1 + g) // 2]
                for a, g in itertools.product(range(3), range(6))
            ]
            cells.append(jnp.concatenate(pieces, axis=0))
        total = jnp.dot(wdl[...], jnp.concatenate(cells, axis=1), preferred_element_type=F32)
        for j in range(2):
            held = part0[d + j, pl.ds(h, 4)].reshape(64, 128)
            value = leaky(total[:, j * 128 : j * 128 + 128] + held)
            for g in range(4):
                xf[pl.ds((d + j) * 16 + h + g, 16, stride=128), :] = value[g * 16 : g * 16 + 16]
        return 0

    lax.fori_loop(0, 16, decode, 0, unroll=4)
    for c in range(16):
        out_ref[c] = xf[pl.ds(c * 128, 128), :].astype(BF16).reshape(8, 16, 128)

    wait_send(sent)


def taps(weights):
    out, inner = weights.shape[:2]
    return jnp.transpose(weights, (2, 3, 4, 0, 1)).reshape(27, out, inner)


def turned_taps(weights):
    out, inner = weights.shape[:2]
    return jnp.transpose(weights, (2, 3, 4, 1, 0)).reshape(27, inner, out)


def per_device(
    volume,
    surface_conv,
    surface_bias,
    second_conv,
    second_bias,
    middle_conv,
    middle_bias,
    bottom_conv,
    bottom_bias,
    middle_lift,
    middle_return,
    middle_offset,
    second_lift,
    second_return,
    second_offset,
    surface_lift,
    surface_return,
    surface_offset,
):
    def tile(*shape):
        return pltpu.VMEM(shape, BF16)

    def wide(rows):
        return pltpu.VMEM((rows, 128), F32)

    scratch = [
        wide(2048), tile(10, 18, 16, 128), tile(2, 3, 3, 16, 128), tile(2, 16, 128), tile(10, 18, 48, 128),
        tile(10, 18, 16, 128), tile(2, 3, 3, 16, 128), tile(2, 16, 128),
        tile(4, 8, 16, 128), tile(10, 14, 16, 128), tile(10, 8, 16, 128), tile(2, 3, 3, 16, 128), tile(2, 16, 128),
        tile(8, 12, 32, 128), tile(4, 6, 64, 128), tile(4, 6, 32, 128), tile(4, 6, 32, 128),
        tile(6, 8, 64, 128), tile(3, 4, 128, 128), tile(3, 4, 64, 128),
        tile(5, 6, 64, 128), tile(2, 5, 3, 64, 128), tile(2, 5, 3, 16, 128), tile(2, 16, 128),
        tile(6, 4, 32, 128), tile(5, 3, 16, 128), tile(15, 2, 64, 128), tile(6, 10, 48, 128),
        pltpu.VMEM((8, 16, 16, 128), F32), pltpu.VMEM((15, 2, 64, 128), F32),
        tile(64, 864), tile(64, 864), tile(64, 864), tile(192, 192), tile(192, 288), tile(384, 576),
        tile(192, 1152), tile(192, 384), tile(192, 384), tile(32, 64),
        tile(128, 256), tile(128, 384),
        tile(512, 128), tile(128, 512), tile(1024, 128), tile(128, 1024), tile(512, 128), tile(128, 512),
        wide(64), wide(64), wide(64), wide(128), wide(64), wide(64), wide(64),
        pltpu.SemaphoreType.DMA((130,)), pltpu.SemaphoreType.DMA((130,)), pltpu.SemaphoreType.DMA((18,)),
    ]

    def line(values):
        return values.reshape(1, values.shape[0])

    operands = (
        volume,
        taps(surface_conv), line(surface_bias),
        turned_taps(second_conv), line(second_bias),
        turned_taps(middle_conv), line(middle_bias),
        turned_taps(bottom_conv), line(bottom_bias),
        middle_lift, taps(middle_return), line(middle_offset),
        second_lift, taps(second_return), line(second_offset),
        surface_lift, taps(surface_return), line(surface_offset),
    )
    return pl.pallas_call(
        kernel,
        out_shape=jax.ShapeDtypeStruct(volume.shape, BF16),
        in_specs=[pl.BlockSpec(memory_space=pltpu.HBM)] * len(operands),
        out_specs=pl.BlockSpec(memory_space=pltpu.VMEM),
        scratch_shapes=[pltpu.VMEM(value.shape, value.dtype) for value in operands] + scratch,
        compiler_params=pltpu.CompilerParams(
            collective_id=0, has_side_effects=True, vmem_limit_bytes=60 * 2**20
        ),
    )(*operands)


def solution(mesh):
    placed = (P(None, "gz", "gy", "gx"),) + (P(),) * 17
    return jax.shard_map(
        per_device, mesh=mesh, in_specs=placed, out_specs=P(None, "gz", "gy", "gx"), check_vma=False
    )
```

```python
import itertools

import jax
import jax.numpy as jnp
from jax import lax
from jax.experimental import pallas as pl
from jax.experimental.pallas import tpu as pltpu
from jax.sharding import PartitionSpec as P

BF16 = jnp.bfloat16
F32 = jnp.float32
STEPS = (-1, 0, 1)
PLANE = [(dz, dy) for dz in STEPS for dy in STEPS]
RING = [step for step in PLANE if step != (0, 0)]
FAR = [(dz, dy) for dz in (-2, -1, 0, 1, 2) for dy in STEPS]


def span(step, size, halo):
    if step == 0:
        return halo, halo, size
    if step > 0:
        return size, 0, halo
    return halo, halo + size, halo


def region(step, size, halo):
    if step == 0:
        return halo, size, 0
    if step < 0:
        return 0, halo, size - halo
    return halo + size, halo, 0


def leaky(total):
    return jnp.maximum(total, 0.1 * total)


def kernel(*refs):
    sources, refs = refs[:18], refs[18:]
    out_ref, refs = refs[0], refs[1:]
    locals_, refs = refs[:18], refs[18:]
    body(sources, locals_, out_ref, *refs)


def body(
    sources,
    locals_,
    out_ref,
    xf, vol, edge0, mine0, stack0,
    zero, edgez, minez,
    top0, pool0, pair0, edge1, mine1,
    skip1, low2, lifted1, pool1, skip2, low3, up2, pool2, wide2, edge2, mine2, folded2, folded3, low1, lifted0, part0, part1,
    wa0, wds, wdl, w1, w2, w3, wu2, wus, wul, wl0,
    pick, grow, fold2, unfold2, fold3, unfold3, fold_edge, unfold_edge,
    bias0, bias1, bias2, bias3, off2, off1, off0,
    send_sem, recv_sem, load_sem,
):
    (
        x_ref,
        k0, b0, k1, b1, k2, b2, k3, b3,
        lift2, ku2, c2, lift1, ku1, c1, lift0, kd0, c0,
    ) = locals_
    z, y, x = lax.axis_index("gz"), lax.axis_index("gy"), lax.axis_index("gx")
    nz, ny, nx = lax.axis_size("gz"), lax.axis_size("gy"), lax.axis_size("gx")

    def device(dz, dy, dx):
        return (lax.rem(z + dz + nz, nz), lax.rem(y + dy + ny, ny), lax.rem(x + dx + nx, nx))

    others = [(*step, dx) for step in PLANE for dx in STEPS if (*step, dx) != (0, 0, 0)]
    loads = [
        pltpu.make_async_copy(source, local, load_sem.at[k])
        for k, (source, local) in enumerate(zip(sources, locals_))
    ]
    loads[0].start()
    barrier = pltpu.get_barrier_semaphore()
    for step in others:
        pl.semaphore_signal(
            barrier, inc=1, device_id=device(*step), device_id_type=pl.DeviceIdType.MESH
        )
    for load in loads[1:]:
        load.start()

    count = itertools.count()

    def send(src, dst, step):
        k = next(count)
        copy = pltpu.make_async_remote_copy(
            src_ref=src,
            dst_ref=dst,
            send_sem=send_sem.at[k],
            recv_sem=recv_sem.at[k],
            device_id=device(*step),
            device_id_type=pl.DeviceIdType.MESH,
        )
        copy.start()
        return copy

    def send_rows(buffer, sizes, halos):
        copies = []
        for dz, dy in RING:
            s0, t0, n0 = span(dz, sizes[0], halos[0])
            s1, t1, n1 = span(dy, sizes[1], halos[1])
            copies.append(
                send(
                    buffer.at[pl.ds(s0, n0), pl.ds(s1, n1)],
                    buffer.at[pl.ds(t0, n0), pl.ds(t1, n1)],
                    (dz, dy, 0),
                )
            )
        return copies

    def send_edges(mine, edge, steps, reach):
        copies = []
        for dz, dy in steps:
            for dx in (-1, 1):
                side = 0 if dx > 0 else 1
                copies.append(
                    send(mine.at[1 - side], edge.at[side, reach - dz, 1 - dy], (dz, dy, dx))
                )
        return copies

    def wait_recv(copies):
        for copy in copies:
            copy.wait_recv()

    def wait_send(copies):
        for copy in copies:
            copy.wait_send()

    lane = lax.broadcasted_iota(jnp.int32, (1, 128), 1)
    inside_left = (x > 0).astype(jnp.int32)
    inside_right = (x < nx - 1).astype(jnp.int32)

    def only(keep, values):
        if keep.dtype != jnp.bool_:
            keep = (lane * 0 + keep) > 0
        return jnp.where(keep, values, jnp.zeros((), values.dtype))

    def within(dz, dy):
        pz, py = z + dz, y + dy
        ok = (pz >= 0) & (pz < nz) & (py >= 0) & (py < ny)
        return ok.astype(jnp.int32)

    loads[0].wait()
    for c in range(16):
        xf[pl.ds(c * 128, 128), :] = x_ref[c].reshape(128, 128).astype(F32)

    def to_row(r, _):
        vol[1 + lax.div(r, 16), 1 + lax.rem(r, 16)] = xf[pl.ds(r, 16, stride=128), :].astype(BF16)
        return 0

    lax.fori_loop(0, 128, to_row, 0, unroll=8)
    row_id = lax.broadcasted_iota(jnp.int32, (32, 2048), 0)
    col_id = lax.broadcasted_iota(jnp.int32, (32, 2048), 1)
    wanted = lax.rem(row_id, 16) * 128 + jnp.where(row_id < 16, 0, 127)
    chooser = (col_id == wanted).astype(F32).astype(BF16)
    flat = jnp.concatenate([x_ref[c].reshape(128, 128) for c in range(16)], axis=1)
    ends = lax.dot_general(
        chooser, flat, (((1,), (1,)), ((), ())), preferred_element_type=F32
    ).astype(BF16)
    mine0[0] = ends[:16]
    mine0[1] = ends[16:]

    pl.semaphore_wait(barrier, len(others))
    sent = []
    near_in = send_edges(mine0, edge0, [(0, 0)], 1)
    rows_in = send_rows(vol, (8, 16), (1, 1))
    edges_in = send_edges(mine0, edge0, RING, 1)
    sent += near_in + rows_in + edges_in

    for load in loads[1:]:
        load.wait()

    def column(ref, size):
        a = lax.broadcasted_iota(jnp.int32, (size, size), 0)
        b = lax.broadcasted_iota(jnp.int32, (size, size), 1)
        spread = jnp.broadcast_to(ref[...], (size, size))
        return jnp.sum(jnp.where(a == b, spread, 0.0), axis=1, keepdims=True)

    for ref, target, size, times in (
        (b0, bias0, 16, 4),
        (b1, bias1, 32, 2),
        (b2, bias2, 64, 1),
        (b3, bias3, 128, 1),
        (c2, off2, 64, 1),
        (c1, off1, 32, 2),
        (c0, off0, 16, 4),
    ):
        wide = jnp.broadcast_to(column(ref, size), (size, 128))
        for j in range(times):
            target[pl.ds(j * size, size), :] = wide

    wa0[...] = jnp.zeros(wa0.shape, BF16)
    for a, e, f in itertools.product(range(3), repeat=3):
        first = k0[(a * 3 + e) * 3 + f]
        for j in range(4):
            at = (a * 6 + e + j) * 48 + f * 16
            wa0[j * 16 : j * 16 + 16, at : at + 16] = first

    def selector(target, rule):
        a = lax.broadcasted_iota(jnp.int32, target.shape, 0)
        b = lax.broadcasted_iota(jnp.int32, target.shape, 1)
        target[...] = rule(a, b).astype(F32).astype(BF16)

    def pick_rule(a, b):
        cell = (b & 127) - 32
        return (cell >= 0) & (cell < 64) & (a == 2 * cell + (b >> 7))

    def rule2(tall, flat, spread):
        q, at = tall >> 7, (tall & 127) - 32
        w = flat & 31
        return (q == (flat >> 5)) & (at >= 2 * w) & (at < 2 * w + spread)

    def rule3(tall, flat, spread):
        r, q, at = tall >> 9, (tall >> 7) & 3, (tall & 127) - 32
        w = flat & 15
        return (q == (flat >> 5)) & (r == ((flat >> 4) & 1)) & (at >= 4 * w) & (at < 4 * w + spread)

    def rule_edge(tall, flat, spread):
        q, at, m = tall >> 7, tall & 127, flat & 31
        size = jnp.where(m < 16, 2, 4)
        start = jnp.where(m < 16, 2 * m, 4 * m - 32)
        return (q == (flat >> 5)) & (m < 20) & (at >= start) & (at < start + (size if spread else 1))

    selector(pick, pick_rule)
    def shifted(src, edge, target, steps):
        for dz, dy in steps:
            p0, n0, s0 = region(dz, 8, 1)
            p1, n1, s1 = region(dy, 16, 1)
            ok = within(dz, dy)
            left_edge = only(ok * inside_left, edge[0, dz + 1, dy + 1])
            right_edge = only(ok * inside_right, edge[1, dz + 1, dy + 1])

            def body(i, _):
                i0, i1 = lax.div(i, n1), lax.rem(i, n1)
                r = (s0 + i0) * 16 + s1 + i1
                row = only(ok, src[p0 + i0, p1 + i1])
                left = pltpu.roll(left_edge, lax.rem(128 - r, 128), 1)
                right = pltpu.roll(right_edge, 127 - r, 1)
                d, h = p0 + i0, p1 + i1
                target[d, h, 0:16, :] = jnp.where(lane == 0, left, pltpu.roll(row, 1, 1))
                target[d, h, 16:32, :] = row
                target[d, h, 32:48, :] = jnp.where(
                    lane == 127, right, pltpu.roll(row, 127, 1)
                )
                return 0

            lax.fori_loop(0, n0 * n1, body, 0, unroll=min(8, n0 * n1))

    def shift_own(src, target):
        def spread(i, _):
            d, h = 1 + lax.div(i, 16), 1 + lax.rem(i, 16)
            row = src[d, h]
            target[d, h, 0:16, :] = pltpu.roll(row, 1, 1)
            target[d, h, 16:32, :] = row
            target[d, h, 32:48, :] = pltpu.roll(row, 127, 1)
            return 0

        lax.fori_loop(0, 128, spread, 0, unroll=8)

    def close_own(edge, target):
        left_edge = only(inside_left, edge[0, 1, 1])
        right_edge = only(inside_right, edge[1, 1, 1])

        def close(r, _):
            d, h = 1 + lax.div(r, 16), 1 + lax.rem(r, 16)
            left = pltpu.roll(left_edge, lax.rem(128 - r, 128), 1)
            right = pltpu.roll(right_edge, 127 - r, 1)
            target[d, h, 0:16, :] = jnp.where(lane == 0, left, target[d, h, 0:16, :])
            target[d, h, 32:48, :] = jnp.where(lane == 127, right, target[d, h, 32:48, :])
            return 0

        lax.fori_loop(0, 128, close, 0, unroll=8)

    shift_own(vol, stack0)
    wait_recv(near_in)
    close_own(edge0, stack0)
    wait_recv(rows_in + edges_in)
    shifted(vol, edge0, stack0, RING)

    def encode(i, _):
        d, h = lax.div(i, 4) * 2, lax.rem(i, 4) * 4
        cells = [stack0[pl.ds(d + j, 3), pl.ds(h, 6)].reshape(864, 128) for j in range(2)]
        total = jnp.dot(wa0[...], jnp.concatenate(cells, axis=1), preferred_element_type=F32)
        halves = [
            leaky(total[:, j * 128 : j * 128 + 128] + bias0[...]).astype(BF16) for j in range(2)
        ]
        for j in range(2):
            zero[1 + d + j, pl.ds(1 + h, 4)] = halves[j].reshape(4, 16, 128)
        top = jnp.maximum(halves[0], halves[1]).reshape(2, 2, 16, 128)
        top = jnp.maximum(top[:, 0], top[:, 1])
        top0[lax.div(d, 2), pl.ds(lax.div(h, 2), 2)] = top
        return 0

    lax.fori_loop(0, 16, encode, 0, unroll=4)
    for d in range(4):
        both = jnp.dot(top0[d].reshape(128, 128), pick[...], preferred_element_type=F32)
        best = jnp.maximum(both[:, :128], both[:, 128:])
        pool0[3 + d, 3:11] = best.astype(BF16).reshape(8, 16, 128)
        best = best.reshape(4, 2, 16, 128)
        odd = pltpu.roll(best[:, 1].reshape(64, 128), 64, 1)
        pair0[3 + d, 2:6] = (best[:, 0].reshape(64, 128) + odd).astype(BF16).reshape(4, 16, 128)

    def pack1(r, carry):
        first, last = carry
        row = pool0[3 + lax.div(r, 8), 3 + lax.rem(r, 8)]
        mine = lax.div(lane, 4) == r
        first = jnp.where(mine, pltpu.roll(row, lax.rem(4 * r + 96, 128), 1), first)
        last = jnp.where(mine, pltpu.roll(row, lax.rem(4 * r + 35, 128), 1), last)
        return first, last

    blank = jnp.zeros((16, 128), BF16)
    first, last = lax.fori_loop(0, 32, pack1, (blank, blank), unroll=8)
    mine1[0] = first
    mine1[1] = last
    near1 = send_edges(mine1, edge1, [(0, 0)], 1)
    rows1 = send_rows(pair0, (4, 4), (3, 2))
    edges1 = send_edges(mine1, edge1, RING, 1)
    sent += near1 + rows1 + edges1

    own = (lane >= 32) & (lane < 96)

    for ref in (wds, wdl, wus, wul, wl0):
        ref[...] = jnp.zeros(ref.shape, BF16)
    for a, e, f in itertools.product(range(3), repeat=3):
        tap = (a * 3 + e) * 3 + f
        last = kd0[tap]
        for j in range(4):
            at = (a * 6 + e + j) * 48 + f * 16
            wds[j * 16 : j * 16 + 16, at : at + 16] = last[:, :16]
            wdl[j * 16 : j * 16 + 16, at : at + 16] = last[:, 16:]
        for j in range(2):
            row = (f * 2 + j) * 32
            at = (a * 4 + e + j) * 32
            wus[row : row + 32, at : at + 32] = ku1[tap][:, :32]
            wul[row : row + 32, at : at + 32] = ku1[tap][:, 32:]
        at = a * 3 + e
        wu2[f * 64 : f * 64 + 64, at * 128 : at * 128 + 128] = ku2[tap]

    def turned(pieces, size):
        a = lax.broadcasted_iota(jnp.int32, (size, size), 0)
        b = lax.broadcasted_iota(jnp.int32, (size, size), 1)
        return lax.dot_general(
            (a == b).astype(F32).astype(BF16),
            jnp.concatenate(pieces, axis=0),
            (((1,), (1,)), ((), ())),
            preferred_element_type=F32,
        ).astype(BF16)

    gap = jnp.zeros((16, 32), BF16)
    for f in range(3):
        for j in range(2):
            pieces = [
                k1[(a * 3 + g - j) * 3 + f] if 0 <= g - j < 3 else gap
                for a, g in itertools.product(range(3), range(4))
            ]
            row = (f * 2 + j) * 32
            w1[row : row + 32, :] = turned(pieces, 32)
        w2[f * 64 : f * 64 + 64, :] = turned([k2[at * 3 + f] for at in range(9)], 64)
        w3[f * 128 : f * 128 + 128, :] = turned([k3[at * 3 + f] for at in range(9)], 128)
    for j in range(2):
        wl0[j * 16 : j * 16 + 16, j * 32 : j * 32 + 32] = lift0[...]

    selector(grow, lambda a, b: a == (((b & 127) + (b >> 7) + 1) >> 1) + 31)
    selector(fold2, lambda a, b: rule2(a, b, 1))
    selector(unfold2, lambda a, b: rule2(b, a, 2))
    selector(fold3, lambda a, b: rule3(a, b, 1))
    selector(unfold3, lambda a, b: rule3(b, a, 4))
    selector(fold_edge, lambda a, b: rule_edge(a, b, False))
    selector(unfold_edge, lambda a, b: rule_edge(b, a, True))

    def packz(r, carry):
        first, last = carry
        row = zero[1 + lax.div(r, 16), 1 + lax.rem(r, 16)]
        first = jnp.where(lane == r, pltpu.roll(row, r, 1), first)
        last = jnp.where(lane == r, pltpu.roll(row, lax.rem(r + 1, 128), 1), last)
        return first, last

    first, last = lax.fori_loop(0, 128, packz, (blank, blank), unroll=8)
    minez[0] = first
    minez[1] = last
    def join_regions(steps):
        for dz, dy in steps:
            p0, n0, s0 = region(dz, 4, 3)
            p1, n1, s1 = region(dy, 8, 3)
            ok = within(dz, dy)
            left_edge = only(ok * inside_left, edge1[0, dz + 1, dy + 1])
            right_edge = only(ok * inside_right, edge1[1, dz + 1, dy + 1])
            keep = (own.astype(jnp.int32) * ok) > 0

            def join_rows(i, _):
                i0, i1 = lax.div(i, n1), lax.rem(i, n1)
                r = (s0 + i0) * 8 + s1 + i1
                if (dz, dy) == (0, 0):
                    row = pool0[p0 + i0, p1 + i1]
                else:
                    at = p1 + i1 + 1
                    row = pair0[p0 + i0, lax.div(at, 2)]
                    row = only(keep, pltpu.roll(row, 64 * lax.rem(at, 2), 1))
                left = pltpu.roll(left_edge, lax.rem(157 - 4 * r, 128), 1)
                right = pltpu.roll(right_edge, lax.rem(224 - 4 * r, 128), 1)
                row = jnp.where((lane >= 29) & (lane < 32), left, row)
                row = jnp.where((lane >= 96) & (lane < 99), right, row)
                pool0[p0 + i0, p1 + i1] = row
                return 0

            lax.fori_loop(0, n0 * n1, join_rows, 0, unroll=9 if n0 * n1 == 9 else 6 if n0 * n1 < 32 else 8)

    shift_own(zero, stack0)
    wait_recv(near1)
    join_regions([(0, 0)])
    wait_recv(rows1 + edges1)

    rowsz = send_rows(zero, (8, 16), (1, 1))
    edgesz = send_edges(minez, edgez, PLANE, 1)
    sent += rowsz + edgesz
    join_regions(RING)

    lanes_ok = ((lane >= 32) | (x > 0)) & ((lane < 96) | (x < nx - 1))
    lanes_ok = lanes_ok.astype(jnp.int32)

    def keeps(d, h, depth, height):
        gd, gh = z * depth + d, y * height + h
        ok = (gd >= 0) & (gd < nz * depth) & (gh >= 0) & (gh < ny * height)
        return (lanes_ok * ok.astype(jnp.int32)) > 0

    def combine(total, rows, shift, part):
        cut = slice(part * 128, part * 128 + 128)
        return (
            pltpu.roll(total[:rows, cut], shift, 1)
            + total[rows : 2 * rows, cut]
            + pltpu.roll(total[2 * rows :, cut], 128 - shift, 1)
        )

    def pairs(row, width):
        even = lax.rem(lax.div(lane, width), 2) == 0
        other = jnp.where(even, pltpu.roll(row, 128 - width, 1), pltpu.roll(row, width, 1))
        return jnp.maximum(row, other)

    def second(i, _):
        d, h = lax.div(i, 6) * 2, lax.rem(i, 6) * 2
        cells = [pool0[pl.ds(d + j, 3), pl.ds(h, 4)].reshape(192, 128) for j in range(2)]
        total = jnp.dot(w1[...], jnp.concatenate(cells, axis=1), preferred_element_type=F32)
        best = None
        for j in range(2):
            value = leaky(combine(total, 64, 1, j) + bias1[...])
            for g in range(2):
                row = jnp.where(keeps(d + j - 2, h + g - 2, 4, 8), value[g * 32 : g * 32 + 32], 0.0)
                skip1[d + j, h + g] = row.astype(BF16)
                best = row if best is None else jnp.maximum(best, row)
        pool1[lax.div(d, 2), lax.div(h, 2)] = pairs(best, 1).astype(BF16)
        return 0

    lax.fori_loop(0, 24, second, 0, unroll=8)


    def third(h, _):
        cells = [pool1[pl.ds(j, 3), pl.ds(h, 3)].reshape(288, 128) for j in range(2)]
        total = jnp.dot(w2[...], jnp.concatenate(cells, axis=1), preferred_element_type=F32)
        for j in range(2):
            value = leaky(combine(total, 64, 2, j) + bias2[...])
            skip2[2 + j, 2 + h] = jnp.where(own, value, 0.0).astype(BF16)
        return 0

    lax.fori_loop(0, 4, third, 0, unroll=4)
    first = jnp.zeros((64, 128), BF16)
    last = jnp.zeros((64, 128), BF16)
    for h in range(2):
        best = None
        for j, g in itertools.product(range(2), repeat=2):
            row = skip2[2 + j, 2 + 2 * h + g]
            best = row if best is None else jnp.maximum(best, row)
            r = j * 4 + 2 * h + g
            here = lax.div(lane, 4) == r
            first = jnp.where(here, pltpu.roll(row, (4 * r + 96) % 128, 1), first)
            last = jnp.where(here, pltpu.roll(row, (4 * r + 36) % 128, 1), last)
        best = pairs(best, 2)
        pool2[2, 2 + h] = best
        here = lax.div(lane, 8) == 4 + h
        first = jnp.where(here, pltpu.roll(best, 8 * h, 1), first)
        last = jnp.where(here, pltpu.roll(best, 8 * h + 72, 1), last)
    def fold(rows, groups, matrix):
        size = rows[0].shape[0] // groups
        pieces = [row[q * size : q * size + size] for q in range(groups) for row in rows]
        return jnp.dot(
            jnp.concatenate(pieces, axis=1), matrix[...], preferred_element_type=F32
        ).astype(BF16)

    mine2[0] = fold([first], 4, fold_edge)
    mine2[1] = fold([last], 4, fold_edge)
    pieces = [pool2[2, 2 + r][q * 16 : q * 16 + 16] for r in range(2) for q in range(4)]
    folded3[2, 1] = jnp.dot(
        jnp.concatenate(pieces, axis=1), fold3[...], preferred_element_type=F32
    ).astype(BF16)
    edges2 = send_edges(mine2, edge2, FAR, 2)
    pools2 = [
        send(folded3.at[2, 1], folded3.at[2 - dz, 1 - dy], (dz, dy, 0))
        for dz, dy in FAR
        if (dz, dy) != (0, 0)
    ]
    for j, g in itertools.product(range(2), repeat=2):
        rows = [skip2[2 + j, 2 + 2 * g + p] for p in range(2)]
        folded2[2 + j, 1 + g] = fold(rows, 2, fold2)
    rows2 = send_rows(folded2, (2, 2), (2, 1))
    sent += pools2 + rows2
    sent += edges2

    def upper_one_skip(i, _):
        d, h = lax.div(i, 5) * 2, lax.rem(i, 5) * 2
        cells = [skip1[pl.ds(d + j, 3), pl.ds(h, 4)].reshape(384, 128) for j in range(2)]
        total = jnp.dot(wus[...], jnp.concatenate(cells, axis=1), preferred_element_type=F32)
        for j in range(2):
            part1[i, j] = combine(total, 64, 1, j) + off1[...]
        return 0

    lax.fori_loop(0, 15, upper_one_skip, 0, unroll=3)

    wait_recv(rowsz + edgesz)
    close_own(edgez, stack0)
    shifted(zero, edgez, stack0, RING)

    def decode_skip(i, _):
        d, h = lax.div(i, 4) * 2, lax.rem(i, 4) * 4
        cells = [stack0[pl.ds(d + j, 3), pl.ds(h, 6)].reshape(864, 128) for j in range(2)]
        total = jnp.dot(wds[...], jnp.concatenate(cells, axis=1), preferred_element_type=F32)
        for j in range(2):
            value = total[:, j * 128 : j * 128 + 128] + off0[...]
            part0[d + j, pl.ds(h, 4)] = value.reshape(4, 16, 128)
        return 0

    lax.fori_loop(0, 16, decode_skip, 0, unroll=4)

    wait_recv(edges2 + pools2)
    for side in range(2):
        for dz in range(5):
            parts = jnp.dot(
                edge2[side, dz].reshape(48, 128), unfold_edge[...], preferred_element_type=F32
            ).astype(BF16)
            for q in range(4):
                wide2[side, dz, :, q * 16 : q * 16 + 16, :] = parts[
                    :, q * 128 : q * 128 + 128
                ].reshape(3, 16, 128)
    for dz in range(-2, 3):
        if dz != 0:
            tiles, steps = folded3[2 + dz].reshape(48, 128), STEPS
        else:
            tiles, steps = jnp.concatenate([folded3[2, 0], folded3[2, 2]], axis=0), (-1, 1)
        parts = jnp.dot(tiles, unfold3[...], preferred_element_type=F32).astype(BF16)
        for k, dy in enumerate(steps):
            for r, q in itertools.product(range(2), range(4)):
                at = (r * 4 + q) * 128
                pool2[2 + dz, 2 + 2 * dy + r, q * 16 : q * 16 + 16, :] = parts[
                    k * 16 : k * 16 + 16, at : at + 128
                ]
    for dz, dy in FAR:
        ok = within(dz, dy)
        left_edge = only(ok * inside_left, wide2[0, dz + 2, dy + 1])
        right_edge = only(ok * inside_right, wide2[1, dz + 2, dy + 1])
        for r in range(2):
            row = only(ok, pool2[2 + dz, 2 + 2 * dy + r])
            left = pltpu.roll(left_edge, (24 - 32 - 8 * r) % 128, 1)
            right = pltpu.roll(right_edge, (96 - 32 - 8 * r) % 128, 1)
            row = jnp.where((lane >= 24) & (lane < 32), left, row)
            row = jnp.where((lane >= 96) & (lane < 104), right, row)
            pool2[2 + dz, 2 + 2 * dy + r] = row

    def coarsest(i, _):
        d, h = lax.div(i, 2), lax.rem(i, 2) * 2
        cells = [pool2[pl.ds(d, 3), pl.ds(h + j, 3)].reshape(576, 128) for j in range(2)]
        total = jnp.dot(w3[...], jnp.concatenate(cells, axis=1), preferred_element_type=F32)
        for j in range(2):
            value = leaky(combine(total, 128, 4, j) + bias3[...])
            row = jnp.where(keeps(d - 1, h + j - 1, 1, 2), value, 0.0)
            low3[d, h + j] = row.astype(BF16)
        return 0

    def lifts(matrix, rows):
        wide = jnp.dot(
            matrix[...], jnp.concatenate(rows, axis=1), preferred_element_type=F32
        ).astype(BF16)
        return [wide[:, k * 128 : k * 128 + 128] for k in range(len(rows))]

    lax.fori_loop(0, 6, coarsest, 0, unroll=6)
    for d in range(3):
        for h, row in enumerate(lifts(lift2, [low3[d, h] for h in range(4)])):
            up2[d, h] = row

    wait_recv(rows2)
    for d in range(6):
        near = d in (2, 3)
        tiles = [folded2[d, g] for g in ((0, 3) if near else range(4))]
        parts = jnp.dot(
            jnp.concatenate(tiles, axis=0), unfold2[...], preferred_element_type=F32
        ).astype(BF16)
        for k, g in enumerate((0, 3) if near else range(4)):
            for q, p in itertools.product(range(2), repeat=2):
                at = (q * 2 + p) * 128
                skip2[d, 2 * g + p, q * 32 : q * 32 + 32, :] = parts[
                    k * 32 : k * 32 + 32, at : at + 128
                ]
    for dz, dy in PLANE:
        p0, n0, s0 = region(dz, 2, 2)
        p1, n1, s1 = region(dy, 4, 2)
        ok = within(dz, dy)
        left_edge = only(ok * inside_left, wide2[0, dz + 2, dy + 1])
        right_edge = only(ok * inside_right, wide2[1, dz + 2, dy + 1])
        for i0, i1 in itertools.product(range(n0), range(n1)):
            r = (s0 + i0) * 4 + s1 + i1
            row = only(ok, skip2[p0 + i0, p1 + i1])
            left = pltpu.roll(left_edge, (28 - 4 * r) % 128, 1)
            right = pltpu.roll(right_edge, (96 - 4 * r) % 128, 1)
            row = jnp.where((lane >= 28) & (lane < 32), left, row)
            row = jnp.where((lane >= 96) & (lane < 100), right, row)
            skip2[p0 + i0, p1 + i1] = row

    def upper_two(i, _):
        d, h = lax.div(i, 6) * 2, lax.rem(i, 6)
        cells = []
        for j in range(2):
            pieces = []
            for a, e in itertools.product(range(3), repeat=2):
                pieces.append(skip2[d + j + a, h + e])
                pieces.append(up2[lax.div(i, 6) + (j + a) // 2, lax.div(h + e, 2)])
            cells.append(jnp.concatenate(pieces, axis=0))
        total = jnp.dot(wu2[...], jnp.concatenate(cells, axis=1), preferred_element_type=F32)
        for j in range(2):
            value = leaky(combine(total, 64, 2, j) + off2[...])
            low2[d + j, h] = jnp.where(keeps(d + j - 1, h - 1, 2, 4), value, 0.0).astype(BF16)
        return 0

    lax.fori_loop(0, 12, upper_two, 0, unroll=3)
    for d in range(4):
        for h, row in enumerate(lifts(lift1, [low2[d, h] for h in range(6)])):
            lifted1[d, h] = row

    def upper_one(i, _):
        d, h = lax.div(i, 5) * 2, lax.rem(i, 5) * 2
        cells = []
        for j in range(2):
            pieces = [
                lifted1[lax.div(i, 5) + (j + a) // 2, lax.rem(i, 5) + g // 2]
                for a, g in itertools.product(range(3), range(4))
            ]
            cells.append(jnp.concatenate(pieces, axis=0))
        total = jnp.dot(wul[...], jnp.concatenate(cells, axis=1), preferred_element_type=F32)
        for j in range(2):
            value = leaky(combine(total, 64, 1, j) + part1[i, j])
            kept = [
                jnp.where(keeps(d + j - 1, h + g - 1, 4, 8), value[g * 32 : g * 32 + 32], 0.0)
                for g in range(2)
            ]
            low1[i, j] = jnp.concatenate(kept, axis=0).astype(BF16)
        return 0

    lax.fori_loop(0, 15, upper_one, 0, unroll=5)
    for d in range(3):
        order = list(itertools.product(range(2), range(5)))
        rows = lifts(wl0, [low1[d * 5 + h, j] for j, h in order])
        wide = jnp.dot(
            jnp.concatenate(rows, axis=0), grow[...], preferred_element_type=F32
        ).astype(BF16)
        for k, (j, h) in enumerate(order):
            for g, f in itertools.product(range(2), range(3)):
                at = k * 32 + g * 16
                lifted0[2 * d + j, 2 * h + g, f * 16 : f * 16 + 16, :] = wide[
                    at : at + 16, f * 128 : f * 128 + 128
                ]

    def decode(p, _):
        d = 2 * p
        for h in range(0, 16, 4):
            cells = []
            for j in range(2):
                pieces = [
                    lifted0[p + (1 + j + a) // 2, h // 2 + (1 + g) // 2]
                    for a, g in itertools.product(range(3), range(6))
                ]
                cells.append(jnp.concatenate(pieces, axis=0))
            total = jnp.dot(wdl[...], jnp.concatenate(cells, axis=1), preferred_element_type=F32)
            for j in range(2):
                held = part0[d + j, pl.ds(h, 4)].reshape(64, 128)
                value = leaky(total[:, j * 128 : j * 128 + 128] + held)
                for g in range(4):
                    at = (d + j) * 16 + h + g
                    xf[pl.ds(at, 16, stride=128), :] = value[g * 16 : g * 16 + 16]
        for c in range(16):
            rows = xf[pl.ds(pl.multiple_of(c * 128 + p * 32, 32), 32), :].astype(BF16)
            out_ref[c, pl.ds(d, 2)] = rows.reshape(2, 16, 128)
        return 0

    lax.fori_loop(0, 4, decode, 0)

    wait_send(sent)


def taps(weights):
    out, inner = weights.shape[:2]
    return jnp.transpose(weights, (2, 3, 4, 0, 1)).reshape(27, out, inner)


def turned_taps(weights):
    out, inner = weights.shape[:2]
    return jnp.transpose(weights, (2, 3, 4, 1, 0)).reshape(27, inner, out)


def per_device(
    volume,
    surface_conv,
    surface_bias,
    second_conv,
    second_bias,
    middle_conv,
    middle_bias,
    bottom_conv,
    bottom_bias,
    middle_lift,
    middle_return,
    middle_offset,
    second_lift,
    second_return,
    second_offset,
    surface_lift,
    surface_return,
    surface_offset,
):
    def tile(*shape):
        return pltpu.VMEM(shape, BF16)

    def wide(rows):
        return pltpu.VMEM((rows, 128), F32)

    scratch = [
        wide(2048), tile(10, 18, 16, 128), tile(2, 3, 3, 16, 128), tile(2, 16, 128), tile(10, 18, 48, 128),
        tile(10, 18, 16, 128), tile(2, 3, 3, 16, 128), tile(2, 16, 128),
        tile(4, 8, 16, 128), tile(10, 14, 16, 128), tile(10, 8, 16, 128), tile(2, 3, 3, 16, 128), tile(2, 16, 128),
        tile(8, 12, 32, 128), tile(4, 6, 64, 128), tile(4, 6, 32, 128), tile(4, 6, 32, 128),
        tile(6, 8, 64, 128), tile(3, 4, 128, 128), tile(3, 4, 64, 128),
        tile(5, 6, 64, 128), tile(2, 5, 3, 64, 128), tile(2, 5, 3, 16, 128), tile(2, 16, 128),
        tile(6, 4, 32, 128), tile(5, 3, 16, 128), tile(15, 2, 64, 128), tile(6, 10, 48, 128),
        pltpu.VMEM((8, 16, 16, 128), F32), pltpu.VMEM((15, 2, 64, 128), F32),
        tile(64, 864), tile(64, 864), tile(64, 864), tile(192, 192), tile(192, 288), tile(384, 576),
        tile(192, 1152), tile(192, 384), tile(192, 384), tile(32, 64),
        tile(128, 256), tile(128, 384),
        tile(512, 128), tile(128, 512), tile(1024, 128), tile(128, 1024), tile(512, 128), tile(128, 512),
        wide(64), wide(64), wide(64), wide(128), wide(64), wide(64), wide(64),
        pltpu.SemaphoreType.DMA((130,)), pltpu.SemaphoreType.DMA((130,)), pltpu.SemaphoreType.DMA((18,)),
    ]

    def line(values):
        return values.reshape(1, values.shape[0])

    operands = (
        volume,
        taps(surface_conv), line(surface_bias),
        turned_taps(second_conv), line(second_bias),
        turned_taps(middle_conv), line(middle_bias),
        turned_taps(bottom_conv), line(bottom_bias),
        middle_lift, taps(middle_return), line(middle_offset),
        second_lift, taps(second_return), line(second_offset),
        surface_lift, taps(surface_return), line(surface_offset),
    )
    return pl.pallas_call(
        kernel,
        out_shape=pltpu.VMEM(volume.shape, BF16),
        in_specs=[pl.BlockSpec(memory_space=pltpu.HBM)] * len(operands),
        out_specs=pl.BlockSpec(memory_space=pltpu.VMEM),
        scratch_shapes=[pltpu.VMEM(value.shape, value.dtype) for value in operands] + scratch,
        compiler_params=pltpu.CompilerParams(
            collective_id=0, has_side_effects=True, vmem_limit_bytes=60 * 2**20
        ),
    )(*operands)


def solution(mesh):
    placed = (P(None, "gz", "gy", "gx"),) + (P(),) * 17
    return jax.shard_map(
        per_device, mesh=mesh, in_specs=placed, out_specs=P(None, "gz", "gy", "gx"), check_vma=False
    )
```

```python
import itertools

import jax
import jax.numpy as jnp
from jax import lax
from jax.experimental import pallas as pl
from jax.experimental.pallas import tpu as pltpu
from jax.sharding import PartitionSpec as P

BF16 = jnp.bfloat16
F32 = jnp.float32
STEPS = (-1, 0, 1)
PLANE = [(dz, dy) for dz in STEPS for dy in STEPS]
RING = [step for step in PLANE if step != (0, 0)]
FAR = [(dz, dy) for dz in (-2, -1, 0, 1, 2) for dy in STEPS]


def span(step, size, halo):
    if step == 0:
        return halo, halo, size
    if step > 0:
        return size, 0, halo
    return halo, halo + size, halo


def region(step, size, halo):
    if step == 0:
        return halo, size, 0
    if step < 0:
        return 0, halo, size - halo
    return halo + size, halo, 0


def leaky(total):
    return jnp.maximum(total, 0.1 * total)


def kernel(*refs):
    sources, refs = refs[:18], refs[18:]
    out_ref, refs = refs[0], refs[1:]
    locals_, refs = refs[:18], refs[18:]
    body(sources, locals_, out_ref, *refs)


def body(
    sources,
    locals_,
    out_ref,
    xf, vol, edge0, mine0, stack0,
    zero, edgez, minez,
    top0, pool0, pair0, edge1, mine1,
    skip1, low2, lifted1, pool1, skip2, low3, up2, pool2, wide2, edge2, mine2, folded2, folded3, low1, lifted0, part0, part1,
    wa0, wds, wdl, w1, w2, w3, wu2, wus, wul, wl0,
    pick, grow, fold2, unfold2, fold3, unfold3, fold_edge, unfold_edge,
    bias0, bias1, bias2, bias3, off2, off1, off0,
    send_sem, recv_sem, load_sem,
):
    (
        x_ref,
        k0, b0, k1, b1, k2, b2, k3, b3,
        lift2, ku2, c2, lift1, ku1, c1, lift0, kd0, c0,
    ) = locals_
    z, y, x = lax.axis_index("gz"), lax.axis_index("gy"), lax.axis_index("gx")
    nz, ny, nx = lax.axis_size("gz"), lax.axis_size("gy"), lax.axis_size("gx")

    def device(dz, dy, dx):
        return (lax.rem(z + dz + nz, nz), lax.rem(y + dy + ny, ny), lax.rem(x + dx + nx, nx))

    others = [(*step, dx) for step in PLANE for dx in STEPS if (*step, dx) != (0, 0, 0)]
    loads = [
        pltpu.make_async_copy(source, local, load_sem.at[k])
        for k, (source, local) in enumerate(zip(sources, locals_))
    ]
    loads[0].start()
    barrier = pltpu.get_barrier_semaphore()
    for step in others:
        pl.semaphore_signal(
            barrier, inc=1, device_id=device(*step), device_id_type=pl.DeviceIdType.MESH
        )
    for load in loads[1:]:
        load.start()

    count = itertools.count()

    def send(src, dst, step):
        k = next(count)
        copy = pltpu.make_async_remote_copy(
            src_ref=src,
            dst_ref=dst,
            send_sem=send_sem.at[k],
            recv_sem=recv_sem.at[k],
            device_id=device(*step),
            device_id_type=pl.DeviceIdType.MESH,
        )
        copy.start()
        return copy

    def send_rows(buffer, sizes, halos):
        copies = []
        for dz, dy in RING:
            s0, t0, n0 = span(dz, sizes[0], halos[0])
            s1, t1, n1 = span(dy, sizes[1], halos[1])
            copies.append(
                send(
                    buffer.at[pl.ds(s0, n0), pl.ds(s1, n1)],
                    buffer.at[pl.ds(t0, n0), pl.ds(t1, n1)],
                    (dz, dy, 0),
                )
            )
        return copies

    def send_edges(mine, edge, steps, reach):
        copies = []
        for dz, dy in steps:
            for dx in (-1, 1):
                side = 0 if dx > 0 else 1
                copies.append(
                    send(mine.at[1 - side], edge.at[side, reach - dz, 1 - dy], (dz, dy, dx))
                )
        return copies

    def wait_recv(copies):
        for copy in copies:
            copy.wait_recv()

    def wait_send(copies):
        for copy in copies:
            copy.wait_send()

    lane = lax.broadcasted_iota(jnp.int32, (1, 128), 1)
    inside_left = (x > 0).astype(jnp.int32)
    inside_right = (x < nx - 1).astype(jnp.int32)

    def only(keep, values):
        if keep.dtype != jnp.bool_:
            keep = (lane * 0 + keep) > 0
        return jnp.where(keep, values, jnp.zeros((), values.dtype))

    def within(dz, dy):
        pz, py = z + dz, y + dy
        ok = (pz >= 0) & (pz < nz) & (py >= 0) & (py < ny)
        return ok.astype(jnp.int32)

    loads[0].wait()
    for c in range(16):
        xf[pl.ds(c * 128, 128), :] = x_ref[c].reshape(128, 128).astype(F32)

    def to_row(r, _):
        vol[1 + lax.div(r, 16), 1 + lax.rem(r, 16)] = xf[pl.ds(r, 16, stride=128), :].astype(BF16)
        return 0

    lax.fori_loop(0, 128, to_row, 0, unroll=16)
    row_id = lax.broadcasted_iota(jnp.int32, (32, 2048), 0)
    col_id = lax.broadcasted_iota(jnp.int32, (32, 2048), 1)
    wanted = lax.rem(row_id, 16) * 128 + jnp.where(row_id < 16, 0, 127)
    chooser = (col_id == wanted).astype(F32).astype(BF16)
    flat = jnp.concatenate([x_ref[c].reshape(128, 128) for c in range(16)], axis=1)
    ends = lax.dot_general(
        chooser, flat, (((1,), (1,)), ((), ())), preferred_element_type=F32
    ).astype(BF16)
    mine0[0] = ends[:16]
    mine0[1] = ends[16:]

    pl.semaphore_wait(barrier, len(others))
    sent = []
    near_in = send_edges(mine0, edge0, [(0, 0)], 1)
    rows_in = send_rows(vol, (8, 16), (1, 1))
    edges_in = send_edges(mine0, edge0, RING, 1)
    sent += near_in + rows_in + edges_in

    for load in loads[1:]:
        load.wait()

    def column(ref, size):
        a = lax.broadcasted_iota(jnp.int32, (size, size), 0)
        b = lax.broadcasted_iota(jnp.int32, (size, size), 1)
        spread = jnp.broadcast_to(ref[...], (size, size))
        return jnp.sum(jnp.where(a == b, spread, 0.0), axis=1, keepdims=True)

    for ref, target, size, times in (
        (b0, bias0, 16, 4),
        (b1, bias1, 32, 2),
        (b2, bias2, 64, 1),
        (b3, bias3, 128, 1),
        (c2, off2, 64, 1),
        (c1, off1, 32, 2),
        (c0, off0, 16, 4),
    ):
        wide = jnp.broadcast_to(column(ref, size), (size, 128))
        for j in range(times):
            target[pl.ds(j * size, size), :] = wide

    wa0[...] = jnp.zeros(wa0.shape, BF16)
    for a, e, f in itertools.product(range(3), repeat=3):
        first = k0[(a * 3 + e) * 3 + f]
        for j in range(4):
            at = (a * 6 + e + j) * 48 + f * 16
            wa0[j * 16 : j * 16 + 16, at : at + 16] = first

    def selector(target, rule):
        a = lax.broadcasted_iota(jnp.int32, target.shape, 0)
        b = lax.broadcasted_iota(jnp.int32, target.shape, 1)
        target[...] = rule(a, b).astype(F32).astype(BF16)

    def pick_rule(a, b):
        cell = (b & 127) - 32
        return (cell >= 0) & (cell < 64) & (a == 2 * cell + (b >> 7))

    def rule2(tall, flat, spread):
        q, at = tall >> 7, (tall & 127) - 32
        w = flat & 31
        return (q == (flat >> 5)) & (at >= 2 * w) & (at < 2 * w + spread)

    def rule3(tall, flat, spread):
        r, q, at = tall >> 9, (tall >> 7) & 3, (tall & 127) - 32
        w = flat & 15
        return (q == (flat >> 5)) & (r == ((flat >> 4) & 1)) & (at >= 4 * w) & (at < 4 * w + spread)

    def rule_edge(tall, flat, spread):
        q, at, m = tall >> 7, tall & 127, flat & 31
        size = jnp.where(m < 16, 2, 4)
        start = jnp.where(m < 16, 2 * m, 4 * m - 32)
        return (q == (flat >> 5)) & (m < 20) & (at >= start) & (at < start + (size if spread else 1))

    selector(pick, pick_rule)
    def shifted(src, edge, target, steps):
        for dz, dy in steps:
            p0, n0, s0 = region(dz, 8, 1)
            p1, n1, s1 = region(dy, 16, 1)
            ok = within(dz, dy)
            left_edge = only(ok * inside_left, edge[0, dz + 1, dy + 1])
            right_edge = only(ok * inside_right, edge[1, dz + 1, dy + 1])

            def body(i, _):
                i0, i1 = lax.div(i, n1), lax.rem(i, n1)
                r = (s0 + i0) * 16 + s1 + i1
                row = only(ok, src[p0 + i0, p1 + i1])
                left = pltpu.roll(left_edge, lax.rem(128 - r, 128), 1)
                right = pltpu.roll(right_edge, 127 - r, 1)
                d, h = p0 + i0, p1 + i1
                target[d, h, 0:16, :] = jnp.where(lane == 0, left, pltpu.roll(row, 1, 1))
                target[d, h, 16:32, :] = row
                target[d, h, 32:48, :] = jnp.where(
                    lane == 127, right, pltpu.roll(row, 127, 1)
                )
                return 0

            lax.fori_loop(0, n0 * n1, body, 0, unroll=min(8, n0 * n1))

    def shift_own(src, target):
        def spread(i, _):
            d, h = 1 + lax.div(i, 16), 1 + lax.rem(i, 16)
            row = src[d, h]
            target[d, h, 0:16, :] = pltpu.roll(row, 1, 1)
            target[d, h, 16:32, :] = row
            target[d, h, 32:48, :] = pltpu.roll(row, 127, 1)
            return 0

        lax.fori_loop(0, 128, spread, 0, unroll=16)

    def close_own(edge, target):
        left_edge = only(inside_left, edge[0, 1, 1])
        right_edge = only(inside_right, edge[1, 1, 1])

        def close(r, _):
            d, h = 1 + lax.div(r, 16), 1 + lax.rem(r, 16)
            left = pltpu.roll(left_edge, lax.rem(128 - r, 128), 1)
            right = pltpu.roll(right_edge, 127 - r, 1)
            target[d, h, 0:16, :] = jnp.where(lane == 0, left, target[d, h, 0:16, :])
            target[d, h, 32:48, :] = jnp.where(lane == 127, right, target[d, h, 32:48, :])
            return 0

        lax.fori_loop(0, 128, close, 0, unroll=16)

    shift_own(vol, stack0)
    wait_recv(near_in)
    close_own(edge0, stack0)
    wait_recv(rows_in + edges_in)
    shifted(vol, edge0, stack0, RING)

    def encode(i, _):
        d, h = lax.div(i, 4) * 2, lax.rem(i, 4) * 4
        cells = [stack0[pl.ds(d + j, 3), pl.ds(h, 6)].reshape(864, 128) for j in range(2)]
        total = jnp.dot(wa0[...], jnp.concatenate(cells, axis=1), preferred_element_type=F32)
        halves = [
            leaky(total[:, j * 128 : j * 128 + 128] + bias0[...]).astype(BF16) for j in range(2)
        ]
        for j in range(2):
            zero[1 + d + j, pl.ds(1 + h, 4)] = halves[j].reshape(4, 16, 128)
        top = jnp.maximum(halves[0], halves[1]).reshape(2, 2, 16, 128)
        top = jnp.maximum(top[:, 0], top[:, 1])
        top0[lax.div(d, 2), pl.ds(lax.div(h, 2), 2)] = top
        return 0

    lax.fori_loop(0, 16, encode, 0, unroll=8)
    for d in range(4):
        both = jnp.dot(top0[d].reshape(128, 128), pick[...], preferred_element_type=F32)
        best = jnp.maximum(both[:, :128], both[:, 128:])
        pool0[3 + d, 3:11] = best.astype(BF16).reshape(8, 16, 128)
        best = best.reshape(4, 2, 16, 128)
        odd = pltpu.roll(best[:, 1].reshape(64, 128), 64, 1)
        pair0[3 + d, 2:6] = (best[:, 0].reshape(64, 128) + odd).astype(BF16).reshape(4, 16, 128)

    def pack1(r, carry):
        first, last = carry
        row = pool0[3 + lax.div(r, 8), 3 + lax.rem(r, 8)]
        mine = lax.div(lane, 4) == r
        first = jnp.where(mine, pltpu.roll(row, lax.rem(4 * r + 96, 128), 1), first)
        last = jnp.where(mine, pltpu.roll(row, lax.rem(4 * r + 35, 128), 1), last)
        return first, last

    blank = jnp.zeros((16, 128), BF16)
    first, last = lax.fori_loop(0, 32, pack1, (blank, blank), unroll=8)
    mine1[0] = first
    mine1[1] = last
    near1 = send_edges(mine1, edge1, [(0, 0)], 1)
    rows1 = send_rows(pair0, (4, 4), (3, 2))
    edges1 = send_edges(mine1, edge1, RING, 1)
    sent += near1 + rows1 + edges1

    own = (lane >= 32) & (lane < 96)

    for ref in (wds, wdl, wus, wul, wl0):
        ref[...] = jnp.zeros(ref.shape, BF16)
    for a, e, f in itertools.product(range(3), repeat=3):
        tap = (a * 3 + e) * 3 + f
        last = kd0[tap]
        for j in range(4):
            at = (a * 6 + e + j) * 48 + f * 16
            wds[j * 16 : j * 16 + 16, at : at + 16] = last[:, :16]
            wdl[j * 16 : j * 16 + 16, at : at + 16] = last[:, 16:]
        for j in range(2):
            row = (f * 2 + j) * 32
            at = (a * 4 + e + j) * 32
            wus[row : row + 32, at : at + 32] = ku1[tap][:, :32]
            wul[row : row + 32, at : at + 32] = ku1[tap][:, 32:]
        at = a * 3 + e
        wu2[f * 64 : f * 64 + 64, at * 128 : at * 128 + 128] = ku2[tap]

    def turned(pieces, size):
        a = lax.broadcasted_iota(jnp.int32, (size, size), 0)
        b = lax.broadcasted_iota(jnp.int32, (size, size), 1)
        return lax.dot_general(
            (a == b).astype(F32).astype(BF16),
            jnp.concatenate(pieces, axis=0),
            (((1,), (1,)), ((), ())),
            preferred_element_type=F32,
        ).astype(BF16)

    gap = jnp.zeros((16, 32), BF16)
    for f in range(3):
        for j in range(2):
            pieces = [
                k1[(a * 3 + g - j) * 3 + f] if 0 <= g - j < 3 else gap
                for a, g in itertools.product(range(3), range(4))
            ]
            row = (f * 2 + j) * 32
            w1[row : row + 32, :] = turned(pieces, 32)
        w2[f * 64 : f * 64 + 64, :] = turned([k2[at * 3 + f] for at in range(9)], 64)
        w3[f * 128 : f * 128 + 128, :] = turned([k3[at * 3 + f] for at in range(9)], 128)
    for j in range(2):
        wl0[j * 16 : j * 16 + 16, j * 32 : j * 32 + 32] = lift0[...]

    selector(grow, lambda a, b: a == (((b & 127) + (b >> 7) + 1) >> 1) + 31)
    selector(fold2, lambda a, b: rule2(a, b, 1))
    selector(unfold2, lambda a, b: rule2(b, a, 2))
    selector(fold3, lambda a, b: rule3(a, b, 1))
    selector(unfold3, lambda a, b: rule3(b, a, 4))
    selector(fold_edge, lambda a, b: rule_edge(a, b, False))
    selector(unfold_edge, lambda a, b: rule_edge(b, a, True))

    def packz(r, carry):
        first, last = carry
        row = zero[1 + lax.div(r, 16), 1 + lax.rem(r, 16)]
        first = jnp.where(lane == r, pltpu.roll(row, r, 1), first)
        last = jnp.where(lane == r, pltpu.roll(row, lax.rem(r + 1, 128), 1), last)
        return first, last

    first, last = lax.fori_loop(0, 128, packz, (blank, blank), unroll=8)
    minez[0] = first
    minez[1] = last
    def join_regions(steps):
        for dz, dy in steps:
            p0, n0, s0 = region(dz, 4, 3)
            p1, n1, s1 = region(dy, 8, 3)
            ok = within(dz, dy)
            left_edge = only(ok * inside_left, edge1[0, dz + 1, dy + 1])
            right_edge = only(ok * inside_right, edge1[1, dz + 1, dy + 1])
            keep = (own.astype(jnp.int32) * ok) > 0

            def join_rows(i, _):
                i0, i1 = lax.div(i, n1), lax.rem(i, n1)
                r = (s0 + i0) * 8 + s1 + i1
                if (dz, dy) == (0, 0):
                    row = pool0[p0 + i0, p1 + i1]
                else:
                    at = p1 + i1 + 1
                    row = pair0[p0 + i0, lax.div(at, 2)]
                    row = only(keep, pltpu.roll(row, 64 * lax.rem(at, 2), 1))
                left = pltpu.roll(left_edge, lax.rem(157 - 4 * r, 128), 1)
                right = pltpu.roll(right_edge, lax.rem(224 - 4 * r, 128), 1)
                row = jnp.where((lane >= 29) & (lane < 32), left, row)
                row = jnp.where((lane >= 96) & (lane < 99), right, row)
                pool0[p0 + i0, p1 + i1] = row
                return 0

            lax.fori_loop(0, n0 * n1, join_rows, 0, unroll=9 if n0 * n1 == 9 else 6 if n0 * n1 < 32 else 8)

    shift_own(zero, stack0)
    wait_recv(near1)
    join_regions([(0, 0)])
    wait_recv(rows1 + edges1)

    rowsz = send_rows(zero, (8, 16), (1, 1))
    edgesz = send_edges(minez, edgez, PLANE, 1)
    sent += rowsz + edgesz
    join_regions(RING)

    lanes_ok = ((lane >= 32) | (x > 0)) & ((lane < 96) | (x < nx - 1))
    lanes_ok = lanes_ok.astype(jnp.int32)

    def keeps(d, h, depth, height):
        gd, gh = z * depth + d, y * height + h
        ok = (gd >= 0) & (gd < nz * depth) & (gh >= 0) & (gh < ny * height)
        return (lanes_ok * ok.astype(jnp.int32)) > 0

    def combine(total, rows, shift, part):
        cut = slice(part * 128, part * 128 + 128)
        return (
            pltpu.roll(total[:rows, cut], shift, 1)
            + total[rows : 2 * rows, cut]
            + pltpu.roll(total[2 * rows :, cut], 128 - shift, 1)
        )

    def pairs(row, width):
        even = lax.rem(lax.div(lane, width), 2) == 0
        other = jnp.where(even, pltpu.roll(row, 128 - width, 1), pltpu.roll(row, width, 1))
        return jnp.maximum(row, other)

    def second(i, _):
        d, h = lax.div(i, 6) * 2, lax.rem(i, 6) * 2
        cells = [pool0[pl.ds(d + j, 3), pl.ds(h, 4)].reshape(192, 128) for j in range(2)]
        total = jnp.dot(w1[...], jnp.concatenate(cells, axis=1), preferred_element_type=F32)
        best = None
        for j in range(2):
            value = leaky(combine(total, 64, 1, j) + bias1[...])
            for g in range(2):
                row = jnp.where(keeps(d + j - 2, h + g - 2, 4, 8), value[g * 32 : g * 32 + 32], 0.0)
                skip1[d + j, h + g] = row.astype(BF16)
                best = row if best is None else jnp.maximum(best, row)
        pool1[lax.div(d, 2), lax.div(h, 2)] = pairs(best, 1).astype(BF16)
        return 0

    lax.fori_loop(0, 24, second, 0, unroll=8)


    def third(h, _):
        cells = [pool1[pl.ds(j, 3), pl.ds(h, 3)].reshape(288, 128) for j in range(2)]
        total = jnp.dot(w2[...], jnp.concatenate(cells, axis=1), preferred_element_type=F32)
        for j in range(2):
            value = leaky(combine(total, 64, 2, j) + bias2[...])
            skip2[2 + j, 2 + h] = jnp.where(own, value, 0.0).astype(BF16)
        return 0

    lax.fori_loop(0, 4, third, 0, unroll=4)
    first = jnp.zeros((64, 128), BF16)
    last = jnp.zeros((64, 128), BF16)
    for h in range(2):
        best = None
        for j, g in itertools.product(range(2), repeat=2):
            row = skip2[2 + j, 2 + 2 * h + g]
            best = row if best is None else jnp.maximum(best, row)
            r = j * 4 + 2 * h + g
            here = lax.div(lane, 4) == r
            first = jnp.where(here, pltpu.roll(row, (4 * r + 96) % 128, 1), first)
            last = jnp.where(here, pltpu.roll(row, (4 * r + 36) % 128, 1), last)
        best = pairs(best, 2)
        pool2[2, 2 + h] = best
        here = lax.div(lane, 8) == 4 + h
        first = jnp.where(here, pltpu.roll(best, 8 * h, 1), first)
        last = jnp.where(here, pltpu.roll(best, 8 * h + 72, 1), last)
    def fold(rows, groups, matrix):
        size = rows[0].shape[0] // groups
        pieces = [row[q * size : q * size + size] for q in range(groups) for row in rows]
        return jnp.dot(
            jnp.concatenate(pieces, axis=1), matrix[...], preferred_element_type=F32
        ).astype(BF16)

    mine2[0] = fold([first], 4, fold_edge)
    mine2[1] = fold([last], 4, fold_edge)
    pieces = [pool2[2, 2 + r][q * 16 : q * 16 + 16] for r in range(2) for q in range(4)]
    folded3[2, 1] = jnp.dot(
        jnp.concatenate(pieces, axis=1), fold3[...], preferred_element_type=F32
    ).astype(BF16)
    edges2 = send_edges(mine2, edge2, FAR, 2)
    pools2 = [
        send(folded3.at[2, 1], folded3.at[2 - dz, 1 - dy], (dz, dy, 0))
        for dz, dy in FAR
        if (dz, dy) != (0, 0)
    ]
    for j, g in itertools.product(range(2), repeat=2):
        rows = [skip2[2 + j, 2 + 2 * g + p] for p in range(2)]
        folded2[2 + j, 1 + g] = fold(rows, 2, fold2)
    rows2 = send_rows(folded2, (2, 2), (2, 1))
    sent += pools2 + rows2
    sent += edges2

    def upper_one_skip(i, _):
        d, h = lax.div(i, 5) * 2, lax.rem(i, 5) * 2
        cells = [skip1[pl.ds(d + j, 3), pl.ds(h, 4)].reshape(384, 128) for j in range(2)]
        total = jnp.dot(wus[...], jnp.concatenate(cells, axis=1), preferred_element_type=F32)
        for j in range(2):
            part1[i, j] = combine(total, 64, 1, j) + off1[...]
        return 0

    lax.fori_loop(0, 15, upper_one_skip, 0, unroll=5)

    wait_recv(rowsz + edgesz)
    close_own(edgez, stack0)
    shifted(zero, edgez, stack0, RING)

    def decode_skip(i, _):
        d, h = lax.div(i, 4) * 2, lax.rem(i, 4) * 4
        cells = [stack0[pl.ds(d + j, 3), pl.ds(h, 6)].reshape(864, 128) for j in range(2)]
        total = jnp.dot(wds[...], jnp.concatenate(cells, axis=1), preferred_element_type=F32)
        for j in range(2):
            value = total[:, j * 128 : j * 128 + 128] + off0[...]
            part0[d + j, pl.ds(h, 4)] = value.reshape(4, 16, 128)
        return 0

    lax.fori_loop(0, 16, decode_skip, 0, unroll=8)

    wait_recv(edges2 + pools2)
    for side in range(2):
        for dz in range(5):
            parts = jnp.dot(
                edge2[side, dz].reshape(48, 128), unfold_edge[...], preferred_element_type=F32
            ).astype(BF16)
            for q in range(4):
                wide2[side, dz, :, q * 16 : q * 16 + 16, :] = parts[
                    :, q * 128 : q * 128 + 128
                ].reshape(3, 16, 128)
    for dz in range(-2, 3):
        if dz != 0:
            tiles, steps = folded3[2 + dz].reshape(48, 128), STEPS
        else:
            tiles, steps = jnp.concatenate([folded3[2, 0], folded3[2, 2]], axis=0), (-1, 1)
        parts = jnp.dot(tiles, unfold3[...], preferred_element_type=F32).astype(BF16)
        for k, dy in enumerate(steps):
            for r, q in itertools.product(range(2), range(4)):
                at = (r * 4 + q) * 128
                pool2[2 + dz, 2 + 2 * dy + r, q * 16 : q * 16 + 16, :] = parts[
                    k * 16 : k * 16 + 16, at : at + 128
                ]
    for dz, dy in FAR:
        ok = within(dz, dy)
        left_edge = only(ok * inside_left, wide2[0, dz + 2, dy + 1])
        right_edge = only(ok * inside_right, wide2[1, dz + 2, dy + 1])
        for r in range(2):
            row = only(ok, pool2[2 + dz, 2 + 2 * dy + r])
            left = pltpu.roll(left_edge, (24 - 32 - 8 * r) % 128, 1)
            right = pltpu.roll(right_edge, (96 - 32 - 8 * r) % 128, 1)
            row = jnp.where((lane >= 24) & (lane < 32), left, row)
            row = jnp.where((lane >= 96) & (lane < 104), right, row)
            pool2[2 + dz, 2 + 2 * dy + r] = row

    def coarsest(i, _):
        d, h = lax.div(i, 2), lax.rem(i, 2) * 2
        cells = [pool2[pl.ds(d, 3), pl.ds(h + j, 3)].reshape(576, 128) for j in range(2)]
        total = jnp.dot(w3[...], jnp.concatenate(cells, axis=1), preferred_element_type=F32)
        for j in range(2):
            value = leaky(combine(total, 128, 4, j) + bias3[...])
            row = jnp.where(keeps(d - 1, h + j - 1, 1, 2), value, 0.0)
            low3[d, h + j] = row.astype(BF16)
        return 0

    def lifts(matrix, rows):
        wide = jnp.dot(
            matrix[...], jnp.concatenate(rows, axis=1), preferred_element_type=F32
        ).astype(BF16)
        return [wide[:, k * 128 : k * 128 + 128] for k in range(len(rows))]

    lax.fori_loop(0, 6, coarsest, 0, unroll=6)
    for d in range(3):
        for h, row in enumerate(lifts(lift2, [low3[d, h] for h in range(4)])):
            up2[d, h] = row

    wait_recv(rows2)
    for d in range(6):
        near = d in (2, 3)
        tiles = [folded2[d, g] for g in ((0, 3) if near else range(4))]
        parts = jnp.dot(
            jnp.concatenate(tiles, axis=0), unfold2[...], preferred_element_type=F32
        ).astype(BF16)
        for k, g in enumerate((0, 3) if near else range(4)):
            for q, p in itertools.product(range(2), repeat=2):
                at = (q * 2 + p) * 128
                skip2[d, 2 * g + p, q * 32 : q * 32 + 32, :] = parts[
                    k * 32 : k * 32 + 32, at : at + 128
                ]
    for dz, dy in PLANE:
        p0, n0, s0 = region(dz, 2, 2)
        p1, n1, s1 = region(dy, 4, 2)
        ok = within(dz, dy)
        left_edge = only(ok * inside_left, wide2[0, dz + 2, dy + 1])
        right_edge = only(ok * inside_right, wide2[1, dz + 2, dy + 1])
        for i0, i1 in itertools.product(range(n0), range(n1)):
            r = (s0 + i0) * 4 + s1 + i1
            row = only(ok, skip2[p0 + i0, p1 + i1])
            left = pltpu.roll(left_edge, (28 - 4 * r) % 128, 1)
            right = pltpu.roll(right_edge, (96 - 4 * r) % 128, 1)
            row = jnp.where((lane >= 28) & (lane < 32), left, row)
            row = jnp.where((lane >= 96) & (lane < 100), right, row)
            skip2[p0 + i0, p1 + i1] = row

    def upper_two(i, _):
        d, h = lax.div(i, 6) * 2, lax.rem(i, 6)
        cells = []
        for j in range(2):
            pieces = []
            for a, e in itertools.product(range(3), repeat=2):
                pieces.append(skip2[d + j + a, h + e])
                pieces.append(up2[lax.div(i, 6) + (j + a) // 2, lax.div(h + e, 2)])
            cells.append(jnp.concatenate(pieces, axis=0))
        total = jnp.dot(wu2[...], jnp.concatenate(cells, axis=1), preferred_element_type=F32)
        for j in range(2):
            value = leaky(combine(total, 64, 2, j) + off2[...])
            low2[d + j, h] = jnp.where(keeps(d + j - 1, h - 1, 2, 4), value, 0.0).astype(BF16)
        return 0

    lax.fori_loop(0, 12, upper_two, 0, unroll=6)
    for d in range(4):
        for h, row in enumerate(lifts(lift1, [low2[d, h] for h in range(6)])):
            lifted1[d, h] = row

    def upper_one(i, _):
        d, h = lax.div(i, 5) * 2, lax.rem(i, 5) * 2
        cells = []
        for j in range(2):
            pieces = [
                lifted1[lax.div(i, 5) + (j + a) // 2, lax.rem(i, 5) + g // 2]
                for a, g in itertools.product(range(3), range(4))
            ]
            cells.append(jnp.concatenate(pieces, axis=0))
        total = jnp.dot(wul[...], jnp.concatenate(cells, axis=1), preferred_element_type=F32)
        for j in range(2):
            value = leaky(combine(total, 64, 1, j) + part1[i, j])
            kept = [
                jnp.where(keeps(d + j - 1, h + g - 1, 4, 8), value[g * 32 : g * 32 + 32], 0.0)
                for g in range(2)
            ]
            low1[i, j] = jnp.concatenate(kept, axis=0).astype(BF16)
        return 0

    lax.fori_loop(0, 15, upper_one, 0, unroll=5)
    for d in range(3):
        order = list(itertools.product(range(2), range(5)))
        rows = lifts(wl0, [low1[d * 5 + h, j] for j, h in order])
        wide = jnp.dot(
            jnp.concatenate(rows, axis=0), grow[...], preferred_element_type=F32
        ).astype(BF16)
        for k, (j, h) in enumerate(order):
            for g, f in itertools.product(range(2), range(3)):
                at = k * 32 + g * 16
                lifted0[2 * d + j, 2 * h + g, f * 16 : f * 16 + 16, :] = wide[
                    at : at + 16, f * 128 : f * 128 + 128
                ]

    def decode(p, _):
        d = 2 * p
        for h in range(0, 16, 4):
            cells = []
            for j in range(2):
                pieces = [
                    lifted0[p + (1 + j + a) // 2, h // 2 + (1 + g) // 2]
                    for a, g in itertools.product(range(3), range(6))
                ]
                cells.append(jnp.concatenate(pieces, axis=0))
            total = jnp.dot(wdl[...], jnp.concatenate(cells, axis=1), preferred_element_type=F32)
            for j in range(2):
                held = part0[d + j, pl.ds(h, 4)].reshape(64, 128)
                value = leaky(total[:, j * 128 : j * 128 + 128] + held)
                for g in range(4):
                    at = (d + j) * 16 + h + g
                    xf[pl.ds(at, 16, stride=128), :] = value[g * 16 : g * 16 + 16]
        for c in range(16):
            rows = xf[pl.ds(pl.multiple_of(c * 128 + p * 32, 32), 32), :].astype(BF16)
            out_ref[c, pl.ds(d, 2)] = rows.reshape(2, 16, 128)
        return 0

    lax.fori_loop(0, 4, decode, 0, unroll=2)

    wait_send(sent)


def taps(weights):
    out, inner = weights.shape[:2]
    return jnp.transpose(weights, (2, 3, 4, 0, 1)).reshape(27, out, inner)


def turned_taps(weights):
    out, inner = weights.shape[:2]
    return jnp.transpose(weights, (2, 3, 4, 1, 0)).reshape(27, inner, out)


def per_device(
    volume,
    surface_conv,
    surface_bias,
    second_conv,
    second_bias,
    middle_conv,
    middle_bias,
    bottom_conv,
    bottom_bias,
    middle_lift,
    middle_return,
    middle_offset,
    second_lift,
    second_return,
    second_offset,
    surface_lift,
    surface_return,
    surface_offset,
):
    def tile(*shape):
        return pltpu.VMEM(shape, BF16)

    def wide(rows):
        return pltpu.VMEM((rows, 128), F32)

    scratch = [
        wide(2048), tile(10, 18, 16, 128), tile(2, 3, 3, 16, 128), tile(2, 16, 128), tile(10, 18, 48, 128),
        tile(10, 18, 16, 128), tile(2, 3, 3, 16, 128), tile(2, 16, 128),
        tile(4, 8, 16, 128), tile(10, 14, 16, 128), tile(10, 8, 16, 128), tile(2, 3, 3, 16, 128), tile(2, 16, 128),
        tile(8, 12, 32, 128), tile(4, 6, 64, 128), tile(4, 6, 32, 128), tile(4, 6, 32, 128),
        tile(6, 8, 64, 128), tile(3, 4, 128, 128), tile(3, 4, 64, 128),
        tile(5, 6, 64, 128), tile(2, 5, 3, 64, 128), tile(2, 5, 3, 16, 128), tile(2, 16, 128),
        tile(6, 4, 32, 128), tile(5, 3, 16, 128), tile(15, 2, 64, 128), tile(6, 10, 48, 128),
        pltpu.VMEM((8, 16, 16, 128), F32), pltpu.VMEM((15, 2, 64, 128), F32),
        tile(64, 864), tile(64, 864), tile(64, 864), tile(192, 192), tile(192, 288), tile(384, 576),
        tile(192, 1152), tile(192, 384), tile(192, 384), tile(32, 64),
        tile(128, 256), tile(128, 384),
        tile(512, 128), tile(128, 512), tile(1024, 128), tile(128, 1024), tile(512, 128), tile(128, 512),
        wide(64), wide(64), wide(64), wide(128), wide(64), wide(64), wide(64),
        pltpu.SemaphoreType.DMA((130,)), pltpu.SemaphoreType.DMA((130,)), pltpu.SemaphoreType.DMA((18,)),
    ]

    def line(values):
        return values.reshape(1, values.shape[0])

    operands = (
        volume,
        taps(surface_conv), line(surface_bias),
        turned_taps(second_conv), line(second_bias),
        turned_taps(middle_conv), line(middle_bias),
        turned_taps(bottom_conv), line(bottom_bias),
        middle_lift, taps(middle_return), line(middle_offset),
        second_lift, taps(second_return), line(second_offset),
        surface_lift, taps(surface_return), line(surface_offset),
    )
    return pl.pallas_call(
        kernel,
        out_shape=pltpu.VMEM(volume.shape, BF16),
        in_specs=[pl.BlockSpec(memory_space=pltpu.HBM)] * len(operands),
        out_specs=pl.BlockSpec(memory_space=pltpu.VMEM),
        scratch_shapes=[pltpu.VMEM(value.shape, value.dtype) for value in operands] + scratch,
        compiler_params=pltpu.CompilerParams(
            collective_id=0, has_side_effects=True, vmem_limit_bytes=60 * 2**20
        ),
    )(*operands)


def solution(mesh):
    placed = (P(None, "gz", "gy", "gx"),) + (P(),) * 17
    return jax.shard_map(
        per_device, mesh=mesh, in_specs=placed, out_specs=P(None, "gz", "gy", "gx"), check_vma=False
    )
```

```python
import itertools

import jax
import jax.numpy as jnp
from jax import lax
from jax.experimental import pallas as pl
from jax.experimental.pallas import tpu as pltpu
from jax.sharding import PartitionSpec as P

BF16 = jnp.bfloat16
F32 = jnp.float32
STEPS = (-1, 0, 1)
PLANE = [(dz, dy) for dz in STEPS for dy in STEPS]
RING = [step for step in PLANE if step != (0, 0)]
FAR = [(dz, dy) for dz in (-2, -1, 0, 1, 2) for dy in STEPS]


def span(step, size, halo):
    if step == 0:
        return halo, halo, size
    if step > 0:
        return size, 0, halo
    return halo, halo + size, halo


def region(step, size, halo):
    if step == 0:
        return halo, size, 0
    if step < 0:
        return 0, halo, size - halo
    return halo + size, halo, 0


def leaky(total):
    return jnp.maximum(total, 0.1 * total)


def kernel(*refs):
    sources, refs = refs[:18], refs[18:]
    out_ref, refs = refs[0], refs[1:]
    locals_, refs = refs[:18], refs[18:]
    body(sources, locals_, out_ref, *refs)


def body(
    sources,
    locals_,
    out_ref,
    xf, vol, edge0, mine0, stack0,
    zero, edgez, minez,
    top0, pool0, pair0, edge1, mine1,
    skip1, low2, lifted1, pool1, skip2, low3, up2, pool2, wide2, edge2, mine2, folded2, folded3, low1, lifted0, part0, part1,
    wa0, wds, wdl, w1, w2, w3, wu2, wus, wul, wl0,
    pick, grow, fold2, unfold2, fold3, unfold3, fold_edge, unfold_edge,
    bias0, bias1, bias2, bias3, off2, off1, off0,
    send_sem, recv_sem, load_sem,
):
    (
        x_ref,
        k0, b0, k1, b1, k2, b2, k3, b3,
        lift2, ku2, c2, lift1, ku1, c1, lift0, kd0, c0,
    ) = locals_
    z, y, x = lax.axis_index("gz"), lax.axis_index("gy"), lax.axis_index("gx")
    nz, ny, nx = lax.axis_size("gz"), lax.axis_size("gy"), lax.axis_size("gx")

    def device(dz, dy, dx):
        return (lax.rem(z + dz + nz, nz), lax.rem(y + dy + ny, ny), lax.rem(x + dx + nx, nx))

    others = [(*step, dx) for step in PLANE for dx in STEPS if (*step, dx) != (0, 0, 0)]
    loads = [
        pltpu.make_async_copy(source, local, load_sem.at[k])
        for k, (source, local) in enumerate(zip(sources, locals_))
    ]
    loads[0].start()
    barrier = pltpu.get_barrier_semaphore()
    for step in others:
        pl.semaphore_signal(
            barrier, inc=1, device_id=device(*step), device_id_type=pl.DeviceIdType.MESH
        )
    for load in loads[1:]:
        load.start()

    count = itertools.count()

    def send(src, dst, step):
        k = next(count)
        copy = pltpu.make_async_remote_copy(
            src_ref=src,
            dst_ref=dst,
            send_sem=send_sem.at[k],
            recv_sem=recv_sem.at[k],
            device_id=device(*step),
            device_id_type=pl.DeviceIdType.MESH,
        )
        copy.start()
        return copy

    def send_rows(buffer, sizes, halos):
        copies = []
        for dz, dy in RING:
            s0, t0, n0 = span(dz, sizes[0], halos[0])
            s1, t1, n1 = span(dy, sizes[1], halos[1])
            copies.append(
                send(
                    buffer.at[pl.ds(s0, n0), pl.ds(s1, n1)],
                    buffer.at[pl.ds(t0, n0), pl.ds(t1, n1)],
                    (dz, dy, 0),
                )
            )
        return copies

    def send_edges(mine, edge, steps, reach):
        copies = []
        for dz, dy in steps:
            for dx in (-1, 1):
                side = 0 if dx > 0 else 1
                copies.append(
                    send(mine.at[1 - side], edge.at[side, reach - dz, 1 - dy], (dz, dy, dx))
                )
        return copies

    def wait_recv(copies):
        for copy in copies:
            copy.wait_recv()

    def wait_send(copies):
        for copy in copies:
            copy.wait_send()

    lane = lax.broadcasted_iota(jnp.int32, (1, 128), 1)
    inside_left = (x > 0).astype(jnp.int32)
    inside_right = (x < nx - 1).astype(jnp.int32)

    def only(keep, values):
        if keep.dtype != jnp.bool_:
            keep = (lane * 0 + keep) > 0
        return jnp.where(keep, values, jnp.zeros((), values.dtype))

    def within(dz, dy):
        pz, py = z + dz, y + dy
        ok = (pz >= 0) & (pz < nz) & (py >= 0) & (py < ny)
        return ok.astype(jnp.int32)

    loads[0].wait()
    for c in range(16):
        xf[pl.ds(c * 128, 128), :] = x_ref[c].reshape(128, 128).astype(F32)

    def to_row(r, _):
        vol[1 + lax.div(r, 16), 1 + lax.rem(r, 16)] = xf[pl.ds(r, 16, stride=128), :].astype(BF16)
        return 0

    lax.fori_loop(0, 128, to_row, 0, unroll=16)
    row_id = lax.broadcasted_iota(jnp.int32, (32, 2048), 0)
    col_id = lax.broadcasted_iota(jnp.int32, (32, 2048), 1)
    wanted = lax.rem(row_id, 16) * 128 + jnp.where(row_id < 16, 0, 127)
    chooser = (col_id == wanted).astype(F32).astype(BF16)
    flat = jnp.concatenate([x_ref[c].reshape(128, 128) for c in range(16)], axis=1)
    ends = lax.dot_general(
        chooser, flat, (((1,), (1,)), ((), ())), preferred_element_type=F32
    ).astype(BF16)
    mine0[0] = ends[:16]
    mine0[1] = ends[16:]

    pl.semaphore_wait(barrier, len(others))
    sent = []
    near_in = send_edges(mine0, edge0, [(0, 0)], 1)
    rows_in = send_rows(vol, (8, 16), (1, 1))
    edges_in = send_edges(mine0, edge0, RING, 1)
    sent += near_in + rows_in + edges_in

    for load in loads[1:]:
        load.wait()

    def column(ref, size):
        a = lax.broadcasted_iota(jnp.int32, (size, size), 0)
        b = lax.broadcasted_iota(jnp.int32, (size, size), 1)
        spread = jnp.broadcast_to(ref[...], (size, size))
        return jnp.sum(jnp.where(a == b, spread, 0.0), axis=1, keepdims=True)

    for ref, target, size, times in (
        (b0, bias0, 16, 4),
        (b1, bias1, 32, 2),
        (b2, bias2, 64, 1),
        (b3, bias3, 128, 1),
        (c2, off2, 64, 1),
        (c1, off1, 32, 2),
        (c0, off0, 16, 4),
    ):
        wide = jnp.broadcast_to(column(ref, size), (size, 128))
        for j in range(times):
            target[pl.ds(j * size, size), :] = wide

    wa0[...] = jnp.zeros(wa0.shape, BF16)
    for a, e, f in itertools.product(range(3), repeat=3):
        first = k0[(a * 3 + e) * 3 + f]
        for j in range(4):
            at = (a * 6 + e + j) * 48 + f * 16
            wa0[j * 16 : j * 16 + 16, at : at + 16] = first

    def selector(target, rule):
        a = lax.broadcasted_iota(jnp.int32, target.shape, 0)
        b = lax.broadcasted_iota(jnp.int32, target.shape, 1)
        target[...] = rule(a, b).astype(F32).astype(BF16)

    def pick_rule(a, b):
        cell = (b & 127) - 32
        return (cell >= 0) & (cell < 64) & (a == 2 * cell + (b >> 7))

    def rule2(tall, flat, spread):
        q, at = tall >> 7, (tall & 127) - 32
        w = flat & 31
        return (q == (flat >> 5)) & (at >= 2 * w) & (at < 2 * w + spread)

    def rule3(tall, flat, spread):
        r, q, at = tall >> 9, (tall >> 7) & 3, (tall & 127) - 32
        w = flat & 15
        return (q == (flat >> 5)) & (r == ((flat >> 4) & 1)) & (at >= 4 * w) & (at < 4 * w + spread)

    def rule_edge(tall, flat, spread):
        q, at, m = tall >> 7, tall & 127, flat & 31
        size = jnp.where(m < 16, 2, 4)
        start = jnp.where(m < 16, 2 * m, 4 * m - 32)
        return (q == (flat >> 5)) & (m < 20) & (at >= start) & (at < start + (size if spread else 1))

    selector(pick, pick_rule)
    def shifted(src, edge, target, steps):
        for dz, dy in steps:
            p0, n0, s0 = region(dz, 8, 1)
            p1, n1, s1 = region(dy, 16, 1)
            ok = within(dz, dy)
            left_edge = only(ok * inside_left, edge[0, dz + 1, dy + 1])
            right_edge = only(ok * inside_right, edge[1, dz + 1, dy + 1])

            def body(i, _):
                i0, i1 = lax.div(i, n1), lax.rem(i, n1)
                r = (s0 + i0) * 16 + s1 + i1
                row = only(ok, src[p0 + i0, p1 + i1])
                left = pltpu.roll(left_edge, lax.rem(128 - r, 128), 1)
                right = pltpu.roll(right_edge, 127 - r, 1)
                d, h = p0 + i0, p1 + i1
                target[d, h, 0:16, :] = jnp.where(lane == 0, left, pltpu.roll(row, 1, 1))
                target[d, h, 16:32, :] = row
                target[d, h, 32:48, :] = jnp.where(
                    lane == 127, right, pltpu.roll(row, 127, 1)
                )
                return 0

            lax.fori_loop(0, n0 * n1, body, 0, unroll=min(8, n0 * n1))

    def shift_own(src, target):
        def spread(i, _):
            d, h = 1 + lax.div(i, 16), 1 + lax.rem(i, 16)
            row = src[d, h]
            target[d, h, 0:16, :] = pltpu.roll(row, 1, 1)
            target[d, h, 16:32, :] = row
            target[d, h, 32:48, :] = pltpu.roll(row, 127, 1)
            return 0

        lax.fori_loop(0, 128, spread, 0, unroll=16)

    def close_own(edge, target):
        left_edge = only(inside_left, edge[0, 1, 1])
        right_edge = only(inside_right, edge[1, 1, 1])

        def close(r, _):
            d, h = 1 + lax.div(r, 16), 1 + lax.rem(r, 16)
            left = pltpu.roll(left_edge, lax.rem(128 - r, 128), 1)
            right = pltpu.roll(right_edge, 127 - r, 1)
            target[d, h, 0:16, :] = jnp.where(lane == 0, left, target[d, h, 0:16, :])
            target[d, h, 32:48, :] = jnp.where(lane == 127, right, target[d, h, 32:48, :])
            return 0

        lax.fori_loop(0, 128, close, 0, unroll=16)

    shift_own(vol, stack0)
    wait_recv(near_in)
    close_own(edge0, stack0)
    wait_recv(rows_in + edges_in)
    shifted(vol, edge0, stack0, RING)

    def encode(i, _):
        d, h = lax.div(i, 4) * 2, lax.rem(i, 4) * 4
        cells = [stack0[pl.ds(d + j, 3), pl.ds(h, 6)].reshape(864, 128) for j in range(2)]
        total = jnp.dot(wa0[...], jnp.concatenate(cells, axis=1), preferred_element_type=F32)
        halves = [
            leaky(total[:, j * 128 : j * 128 + 128] + bias0[...]).astype(BF16) for j in range(2)
        ]
        for j in range(2):
            zero[1 + d + j, pl.ds(1 + h, 4)] = halves[j].reshape(4, 16, 128)
        top = jnp.maximum(halves[0], halves[1]).reshape(2, 2, 16, 128)
        top = jnp.maximum(top[:, 0], top[:, 1])
        top0[lax.div(d, 2), pl.ds(lax.div(h, 2), 2)] = top
        return 0

    lax.fori_loop(0, 16, encode, 0, unroll=8)
    for d in range(4):
        both = jnp.dot(top0[d].reshape(128, 128), pick[...], preferred_element_type=F32)
        best = jnp.maximum(both[:, :128], both[:, 128:])
        pool0[3 + d, 3:11] = best.astype(BF16).reshape(8, 16, 128)
        best = best.reshape(4, 2, 16, 128)
        odd = pltpu.roll(best[:, 1].reshape(64, 128), 64, 1)
        pair0[3 + d, 2:6] = (best[:, 0].reshape(64, 128) + odd).astype(BF16).reshape(4, 16, 128)

    def pack1(r, carry):
        first, last = carry
        row = pool0[3 + lax.div(r, 8), 3 + lax.rem(r, 8)]
        mine = lax.div(lane, 4) == r
        first = jnp.where(mine, pltpu.roll(row, lax.rem(4 * r + 96, 128), 1), first)
        last = jnp.where(mine, pltpu.roll(row, lax.rem(4 * r + 35, 128), 1), last)
        return first, last

    blank = jnp.zeros((16, 128), BF16)
    first, last = lax.fori_loop(0, 32, pack1, (blank, blank), unroll=8)
    mine1[0] = first
    mine1[1] = last
    near1 = send_edges(mine1, edge1, [(0, 0)], 1)
    rows1 = send_rows(pair0, (4, 4), (3, 2))
    edges1 = send_edges(mine1, edge1, RING, 1)
    sent += near1 + rows1 + edges1

    own = (lane >= 32) & (lane < 96)

    for ref in (wds, wdl, wus, wul, wl0):
        ref[...] = jnp.zeros(ref.shape, BF16)
    for a, e, f in itertools.product(range(3), repeat=3):
        tap = (a * 3 + e) * 3 + f
        last = kd0[tap]
        for j in range(4):
            at = (a * 6 + e + j) * 48 + f * 16
            wds[j * 16 : j * 16 + 16, at : at + 16] = last[:, :16]
            wdl[j * 16 : j * 16 + 16, at : at + 16] = last[:, 16:]
        for j in range(2):
            row = (f * 2 + j) * 32
            at = (a * 4 + e + j) * 32
            wus[row : row + 32, at : at + 32] = ku1[tap][:, :32]
            wul[row : row + 32, at : at + 32] = ku1[tap][:, 32:]
        at = a * 3 + e
        wu2[f * 64 : f * 64 + 64, at * 128 : at * 128 + 128] = ku2[tap]

    def turned(pieces, size):
        a = lax.broadcasted_iota(jnp.int32, (size, size), 0)
        b = lax.broadcasted_iota(jnp.int32, (size, size), 1)
        return lax.dot_general(
            (a == b).astype(F32).astype(BF16),
            jnp.concatenate(pieces, axis=0),
            (((1,), (1,)), ((), ())),
            preferred_element_type=F32,
        ).astype(BF16)

    gap = jnp.zeros((16, 32), BF16)
    for f in range(3):
        for j in range(2):
            pieces = [
                k1[(a * 3 + g - j) * 3 + f] if 0 <= g - j < 3 else gap
                for a, g in itertools.product(range(3), range(4))
            ]
            row = (f * 2 + j) * 32
            w1[row : row + 32, :] = turned(pieces, 32)
        w2[f * 64 : f * 64 + 64, :] = turned([k2[at * 3 + f] for at in range(9)], 64)
        w3[f * 128 : f * 128 + 128, :] = turned([k3[at * 3 + f] for at in range(9)], 128)
    for j in range(2):
        wl0[j * 16 : j * 16 + 16, j * 32 : j * 32 + 32] = lift0[...]

    selector(grow, lambda a, b: a == (((b & 127) + (b >> 7) + 1) >> 1) + 31)
    selector(fold2, lambda a, b: rule2(a, b, 1))
    selector(unfold2, lambda a, b: rule2(b, a, 2))
    selector(fold3, lambda a, b: rule3(a, b, 1))
    selector(unfold3, lambda a, b: rule3(b, a, 4))
    selector(fold_edge, lambda a, b: rule_edge(a, b, False))
    selector(unfold_edge, lambda a, b: rule_edge(b, a, True))

    def packz(r, carry):
        first, last = carry
        row = zero[1 + lax.div(r, 16), 1 + lax.rem(r, 16)]
        first = jnp.where(lane == r, pltpu.roll(row, r, 1), first)
        last = jnp.where(lane == r, pltpu.roll(row, lax.rem(r + 1, 128), 1), last)
        return first, last

    first, last = lax.fori_loop(0, 128, packz, (blank, blank), unroll=8)
    minez[0] = first
    minez[1] = last
    def join_regions(steps):
        for dz, dy in steps:
            p0, n0, s0 = region(dz, 4, 3)
            p1, n1, s1 = region(dy, 8, 3)
            ok = within(dz, dy)
            left_edge = only(ok * inside_left, edge1[0, dz + 1, dy + 1])
            right_edge = only(ok * inside_right, edge1[1, dz + 1, dy + 1])
            keep = (own.astype(jnp.int32) * ok) > 0

            def join_rows(i, _):
                i0, i1 = lax.div(i, n1), lax.rem(i, n1)
                r = (s0 + i0) * 8 + s1 + i1
                if (dz, dy) == (0, 0):
                    row = pool0[p0 + i0, p1 + i1]
                else:
                    at = p1 + i1 + 1
                    row = pair0[p0 + i0, lax.div(at, 2)]
                    row = only(keep, pltpu.roll(row, 64 * lax.rem(at, 2), 1))
                left = pltpu.roll(left_edge, lax.rem(157 - 4 * r, 128), 1)
                right = pltpu.roll(right_edge, lax.rem(224 - 4 * r, 128), 1)
                row = jnp.where((lane >= 29) & (lane < 32), left, row)
                row = jnp.where((lane >= 96) & (lane < 99), right, row)
                pool0[p0 + i0, p1 + i1] = row
                return 0

            lax.fori_loop(0, n0 * n1, join_rows, 0, unroll=9 if n0 * n1 == 9 else 6 if n0 * n1 < 32 else 8)

    shift_own(zero, stack0)
    wait_recv(near1)
    join_regions([(0, 0)])
    wait_recv(rows1 + edges1)

    rowsz = send_rows(zero, (8, 16), (1, 1))
    edgesz = send_edges(minez, edgez, PLANE, 1)
    sent += rowsz + edgesz
    join_regions(RING)

    lanes_ok = ((lane >= 32) | (x > 0)) & ((lane < 96) | (x < nx - 1))
    lanes_ok = lanes_ok.astype(jnp.int32)

    def keeps(d, h, depth, height):
        gd, gh = z * depth + d, y * height + h
        ok = (gd >= 0) & (gd < nz * depth) & (gh >= 0) & (gh < ny * height)
        return (lanes_ok * ok.astype(jnp.int32)) > 0

    def combine(total, rows, shift, part):
        cut = slice(part * 128, part * 128 + 128)
        return (
            pltpu.roll(total[:rows, cut], shift, 1)
            + total[rows : 2 * rows, cut]
            + pltpu.roll(total[2 * rows :, cut], 128 - shift, 1)
        )

    def pairs(row, width):
        even = lax.rem(lax.div(lane, width), 2) == 0
        other = jnp.where(even, pltpu.roll(row, 128 - width, 1), pltpu.roll(row, width, 1))
        return jnp.maximum(row, other)

    def second(i, _):
        d, h = lax.div(i, 6) * 2, lax.rem(i, 6) * 2
        cells = [pool0[pl.ds(d + j, 3), pl.ds(h, 4)].reshape(192, 128) for j in range(2)]
        total = jnp.dot(w1[...], jnp.concatenate(cells, axis=1), preferred_element_type=F32)
        best = None
        for j in range(2):
            value = leaky(combine(total, 64, 1, j) + bias1[...])
            for g in range(2):
                row = jnp.where(keeps(d + j - 2, h + g - 2, 4, 8), value[g * 32 : g * 32 + 32], 0.0)
                skip1[d + j, h + g] = row.astype(BF16)
                best = row if best is None else jnp.maximum(best, row)
        pool1[lax.div(d, 2), lax.div(h, 2)] = pairs(best, 1).astype(BF16)
        return 0

    lax.fori_loop(0, 24, second, 0, unroll=8)


    def third(h, _):
        cells = [pool1[pl.ds(j, 3), pl.ds(h, 3)].reshape(288, 128) for j in range(2)]
        total = jnp.dot(w2[...], jnp.concatenate(cells, axis=1), preferred_element_type=F32)
        for j in range(2):
            value = leaky(combine(total, 64, 2, j) + bias2[...])
            skip2[2 + j, 2 + h] = jnp.where(own, value, 0.0).astype(BF16)
        return 0

    lax.fori_loop(0, 4, third, 0, unroll=4)
    first = jnp.zeros((64, 128), BF16)
    last = jnp.zeros((64, 128), BF16)
    for h in range(2):
        best = None
        for j, g in itertools.product(range(2), repeat=2):
            row = skip2[2 + j, 2 + 2 * h + g]
            best = row if best is None else jnp.maximum(best, row)
            r = j * 4 + 2 * h + g
            here = lax.div(lane, 4) == r
            first = jnp.where(here, pltpu.roll(row, (4 * r + 96) % 128, 1), first)
            last = jnp.where(here, pltpu.roll(row, (4 * r + 36) % 128, 1), last)
        best = pairs(best, 2)
        pool2[2, 2 + h] = best
        here = lax.div(lane, 8) == 4 + h
        first = jnp.where(here, pltpu.roll(best, 8 * h, 1), first)
        last = jnp.where(here, pltpu.roll(best, 8 * h + 72, 1), last)
    def fold(rows, groups, matrix):
        size = rows[0].shape[0] // groups
        pieces = [row[q * size : q * size + size] for q in range(groups) for row in rows]
        return jnp.dot(
            jnp.concatenate(pieces, axis=1), matrix[...], preferred_element_type=F32
        ).astype(BF16)

    mine2[0] = fold([first], 4, fold_edge)
    mine2[1] = fold([last], 4, fold_edge)
    pieces = [pool2[2, 2 + r][q * 16 : q * 16 + 16] for r in range(2) for q in range(4)]
    folded3[2, 1] = jnp.dot(
        jnp.concatenate(pieces, axis=1), fold3[...], preferred_element_type=F32
    ).astype(BF16)
    edges2 = send_edges(mine2, edge2, FAR, 2)
    pools2 = [
        send(folded3.at[2, 1], folded3.at[2 - dz, 1 - dy], (dz, dy, 0))
        for dz, dy in FAR
        if (dz, dy) != (0, 0)
    ]
    for j, g in itertools.product(range(2), repeat=2):
        rows = [skip2[2 + j, 2 + 2 * g + p] for p in range(2)]
        folded2[2 + j, 1 + g] = fold(rows, 2, fold2)
    rows2 = send_rows(folded2, (2, 2), (2, 1))
    sent += pools2 + rows2
    sent += edges2

    def upper_one_skip(i, _):
        d, h = lax.div(i, 5) * 2, lax.rem(i, 5) * 2
        cells = [skip1[pl.ds(d + j, 3), pl.ds(h, 4)].reshape(384, 128) for j in range(2)]
        total = jnp.dot(wus[...], jnp.concatenate(cells, axis=1), preferred_element_type=F32)
        for j in range(2):
            part1[i, j] = combine(total, 64, 1, j) + off1[...]
        return 0

    lax.fori_loop(0, 15, upper_one_skip, 0, unroll=5)

    wait_recv(rowsz + edgesz)
    close_own(edgez, stack0)
    shifted(zero, edgez, stack0, RING)

    def decode_skip(i, _):
        d, h = lax.div(i, 4) * 2, lax.rem(i, 4) * 4
        cells = [stack0[pl.ds(d + j, 3), pl.ds(h, 6)].reshape(864, 128) for j in range(2)]
        total = jnp.dot(wds[...], jnp.concatenate(cells, axis=1), preferred_element_type=F32)
        for j in range(2):
            value = total[:, j * 128 : j * 128 + 128] + off0[...]
            part0[d + j, pl.ds(h, 4)] = value.reshape(4, 16, 128)
        return 0

    lax.fori_loop(0, 16, decode_skip, 0, unroll=8)

    wait_recv(edges2 + pools2)
    for side in range(2):
        for dz in range(5):
            parts = jnp.dot(
                edge2[side, dz].reshape(48, 128), unfold_edge[...], preferred_element_type=F32
            ).astype(BF16)
            for q in range(4):
                wide2[side, dz, :, q * 16 : q * 16 + 16, :] = parts[
                    :, q * 128 : q * 128 + 128
                ].reshape(3, 16, 128)
    for dz in range(-2, 3):
        if dz != 0:
            tiles, steps = folded3[2 + dz].reshape(48, 128), STEPS
        else:
            tiles, steps = jnp.concatenate([folded3[2, 0], folded3[2, 2]], axis=0), (-1, 1)
        parts = jnp.dot(tiles, unfold3[...], preferred_element_type=F32).astype(BF16)
        for k, dy in enumerate(steps):
            for r, q in itertools.product(range(2), range(4)):
                at = (r * 4 + q) * 128
                pool2[2 + dz, 2 + 2 * dy + r, q * 16 : q * 16 + 16, :] = parts[
                    k * 16 : k * 16 + 16, at : at + 128
                ]
    for dz, dy in FAR:
        ok = within(dz, dy)
        left_edge = only(ok * inside_left, wide2[0, dz + 2, dy + 1])
        right_edge = only(ok * inside_right, wide2[1, dz + 2, dy + 1])
        for r in range(2):
            row = only(ok, pool2[2 + dz, 2 + 2 * dy + r])
            left = pltpu.roll(left_edge, (24 - 32 - 8 * r) % 128, 1)
            right = pltpu.roll(right_edge, (96 - 32 - 8 * r) % 128, 1)
            row = jnp.where((lane >= 24) & (lane < 32), left, row)
            row = jnp.where((lane >= 96) & (lane < 104), right, row)
            pool2[2 + dz, 2 + 2 * dy + r] = row

    def coarsest(i, _):
        d, h = lax.div(i, 2), lax.rem(i, 2) * 2
        cells = [pool2[pl.ds(d, 3), pl.ds(h + j, 3)].reshape(576, 128) for j in range(2)]
        total = jnp.dot(w3[...], jnp.concatenate(cells, axis=1), preferred_element_type=F32)
        for j in range(2):
            value = leaky(combine(total, 128, 4, j) + bias3[...])
            row = jnp.where(keeps(d - 1, h + j - 1, 1, 2), value, 0.0)
            low3[d, h + j] = row.astype(BF16)
        return 0

    def lifts(matrix, rows):
        wide = jnp.dot(
            matrix[...], jnp.concatenate(rows, axis=1), preferred_element_type=F32
        ).astype(BF16)
        return [wide[:, k * 128 : k * 128 + 128] for k in range(len(rows))]

    lax.fori_loop(0, 6, coarsest, 0, unroll=6)
    for d in range(3):
        for h, row in enumerate(lifts(lift2, [low3[d, h] for h in range(4)])):
            up2[d, h] = row

    wait_recv(rows2)
    for d in range(6):
        near = d in (2, 3)
        tiles = [folded2[d, g] for g in ((0, 3) if near else range(4))]
        parts = jnp.dot(
            jnp.concatenate(tiles, axis=0), unfold2[...], preferred_element_type=F32
        ).astype(BF16)
        for k, g in enumerate((0, 3) if near else range(4)):
            for q, p in itertools.product(range(2), repeat=2):
                at = (q * 2 + p) * 128
                skip2[d, 2 * g + p, q * 32 : q * 32 + 32, :] = parts[
                    k * 32 : k * 32 + 32, at : at + 128
                ]
    for dz, dy in PLANE:
        p0, n0, s0 = region(dz, 2, 2)
        p1, n1, s1 = region(dy, 4, 2)
        ok = within(dz, dy)
        left_edge = only(ok * inside_left, wide2[0, dz + 2, dy + 1])
        right_edge = only(ok * inside_right, wide2[1, dz + 2, dy + 1])
        for i0, i1 in itertools.product(range(n0), range(n1)):
            r = (s0 + i0) * 4 + s1 + i1
            row = only(ok, skip2[p0 + i0, p1 + i1])
            left = pltpu.roll(left_edge, (28 - 4 * r) % 128, 1)
            right = pltpu.roll(right_edge, (96 - 4 * r) % 128, 1)
            row = jnp.where((lane >= 28) & (lane < 32), left, row)
            row = jnp.where((lane >= 96) & (lane < 100), right, row)
            skip2[p0 + i0, p1 + i1] = row

    def upper_two(i, _):
        d, h = lax.div(i, 6) * 2, lax.rem(i, 6)
        cells = []
        for j in range(2):
            pieces = []
            for a, e in itertools.product(range(3), repeat=2):
                pieces.append(skip2[d + j + a, h + e])
                pieces.append(up2[lax.div(i, 6) + (j + a) // 2, lax.div(h + e, 2)])
            cells.append(jnp.concatenate(pieces, axis=0))
        total = jnp.dot(wu2[...], jnp.concatenate(cells, axis=1), preferred_element_type=F32)
        for j in range(2):
            value = leaky(combine(total, 64, 2, j) + off2[...])
            low2[d + j, h] = jnp.where(keeps(d + j - 1, h - 1, 2, 4), value, 0.0).astype(BF16)
        return 0

    lax.fori_loop(0, 12, upper_two, 0, unroll=6)
    for d in range(4):
        for h, row in enumerate(lifts(lift1, [low2[d, h] for h in range(6)])):
            lifted1[d, h] = row

    def upper_one(i, _):
        d, h = lax.div(i, 5) * 2, lax.rem(i, 5) * 2
        cells = []
        for j in range(2):
            pieces = [
                lifted1[lax.div(i, 5) + (j + a) // 2, lax.rem(i, 5) + g // 2]
                for a, g in itertools.product(range(3), range(4))
            ]
            cells.append(jnp.concatenate(pieces, axis=0))
        total = jnp.dot(wul[...], jnp.concatenate(cells, axis=1), preferred_element_type=F32)
        for j in range(2):
            value = leaky(combine(total, 64, 1, j) + part1[i, j])
            kept = [
                jnp.where(keeps(d + j - 1, h + g - 1, 4, 8), value[g * 32 : g * 32 + 32], 0.0)
                for g in range(2)
            ]
            low1[i, j] = jnp.concatenate(kept, axis=0).astype(BF16)
        return 0

    lax.fori_loop(0, 15, upper_one, 0, unroll=5)
    for d in range(3):
        order = list(itertools.product(range(2), range(5)))
        rows = lifts(wl0, [low1[d * 5 + h, j] for j, h in order])
        wide = jnp.dot(
            jnp.concatenate(rows, axis=0), grow[...], preferred_element_type=F32
        ).astype(BF16)
        for k, (j, h) in enumerate(order):
            for g, f in itertools.product(range(2), range(3)):
                at = k * 32 + g * 16
                lifted0[2 * d + j, 2 * h + g, f * 16 : f * 16 + 16, :] = wide[
                    at : at + 16, f * 128 : f * 128 + 128
                ]

    def decode(p, _):
        d = 2 * p
        for h in range(0, 16, 4):
            cells = []
            for j in range(2):
                pieces = [
                    lifted0[p + (1 + j + a) // 2, h // 2 + (1 + g) // 2]
                    for a, g in itertools.product(range(3), range(6))
                ]
                cells.append(jnp.concatenate(pieces, axis=0))
            total = jnp.dot(wdl[...], jnp.concatenate(cells, axis=1), preferred_element_type=F32)
            for j in range(2):
                held = part0[d + j, pl.ds(h, 4)].reshape(64, 128)
                value = leaky(total[:, j * 128 : j * 128 + 128] + held)
                for g in range(4):
                    at = (d + j) * 16 + h + g
                    xf[pl.ds(at, 16, stride=128), :] = value[g * 16 : g * 16 + 16]
        for c in range(16):
            rows = xf[pl.ds(pl.multiple_of(c * 128 + p * 32, 32), 32), :].astype(BF16)
            out_ref[c, pl.ds(d, 2)] = rows.reshape(2, 16, 128)
        return 0

    lax.fori_loop(0, 4, decode, 0, unroll=2)

    wait_send(sent)


def taps(weights):
    out, inner = weights.shape[:2]
    return jnp.transpose(weights, (2, 3, 4, 0, 1)).reshape(27, out, inner)


def turned_taps(weights):
    out, inner = weights.shape[:2]
    return jnp.transpose(weights, (2, 3, 4, 1, 0)).reshape(27, inner, out)


def per_device(
    volume,
    surface_conv,
    surface_bias,
    second_conv,
    second_bias,
    middle_conv,
    middle_bias,
    bottom_conv,
    bottom_bias,
    middle_lift,
    middle_return,
    middle_offset,
    second_lift,
    second_return,
    second_offset,
    surface_lift,
    surface_return,
    surface_offset,
):
    def tile(*shape):
        return pltpu.VMEM(shape, BF16)

    def wide(rows):
        return pltpu.VMEM((rows, 128), F32)

    scratch = [
        wide(2176), tile(10, 18, 16, 128), tile(2, 3, 3, 16, 128), tile(2, 16, 128), tile(10, 18, 48, 128),
        tile(10, 18, 16, 128), tile(2, 3, 3, 16, 128), tile(2, 16, 128),
        tile(4, 8, 16, 128), tile(10, 14, 16, 128), tile(10, 8, 16, 128), tile(2, 3, 3, 16, 128), tile(2, 16, 128),
        tile(8, 12, 32, 128), tile(4, 6, 64, 128), tile(4, 6, 32, 128), tile(4, 6, 32, 128),
        tile(6, 8, 64, 128), tile(3, 4, 128, 128), tile(3, 4, 64, 128),
        tile(5, 6, 64, 128), tile(2, 5, 3, 64, 128), tile(2, 5, 3, 16, 128), tile(2, 16, 128),
        tile(6, 4, 32, 128), tile(5, 3, 16, 128), tile(15, 2, 64, 128), tile(6, 10, 48, 128),
        pltpu.VMEM((8, 16, 16, 128), F32), pltpu.VMEM((15, 2, 64, 128), F32),
        tile(64, 864), tile(64, 864), tile(64, 864), tile(192, 192), tile(192, 288), tile(384, 576),
        tile(192, 1152), tile(192, 384), tile(192, 384), tile(32, 64),
        tile(128, 256), tile(128, 384),
        tile(512, 128), tile(128, 512), tile(1024, 128), tile(128, 1024), tile(512, 128), tile(128, 512),
        wide(64), wide(64), wide(64), wide(128), wide(64), wide(64), wide(64),
        pltpu.SemaphoreType.DMA((130,)), pltpu.SemaphoreType.DMA((130,)), pltpu.SemaphoreType.DMA((18,)),
    ]

    def line(values):
        return values.reshape(1, values.shape[0])

    operands = (
        volume,
        taps(surface_conv), line(surface_bias),
        turned_taps(second_conv), line(second_bias),
        turned_taps(middle_conv), line(middle_bias),
        turned_taps(bottom_conv), line(bottom_bias),
        middle_lift, taps(middle_return), line(middle_offset),
        second_lift, taps(second_return), line(second_offset),
        surface_lift, taps(surface_return), line(surface_offset),
    )
    return pl.pallas_call(
        kernel,
        out_shape=pltpu.VMEM(volume.shape, BF16),
        in_specs=[pl.BlockSpec(memory_space=pltpu.HBM)] * len(operands),
        out_specs=pl.BlockSpec(memory_space=pltpu.VMEM),
        scratch_shapes=[pltpu.VMEM(value.shape, value.dtype) for value in operands] + scratch,
        compiler_params=pltpu.CompilerParams(
            collective_id=0, has_side_effects=True, vmem_limit_bytes=60 * 2**20
        ),
    )(*operands)


def solution(mesh):
    placed = (P(None, "gz", "gy", "gx"),) + (P(),) * 17
    return jax.shard_map(
        per_device, mesh=mesh, in_specs=placed, out_specs=P(None, "gz", "gy", "gx"), check_vma=False
    )
```
